32 devices in a mesh: dp: 8 (over y, x, core), chan: 4 (over z).
Axes of the slice: x: 2, y: 2, z: 4, core: 2. Of those that a mesh axis runs over, the one named last changes fastest.
Arguments:
- images: bfloat16 [128, 128, 1024], P('chan', 'dp'), may hold values from -6 to 6
- student_master: float32 [1152, 256], P('dp', 'chan'), may hold values from -1 to 1
- regress_master: float32 [1152, 192], P('dp', 'chan'), may hold values from -1 to 1
- teacher_weight: bfloat16 [1152, 384], P(None, 'chan'), may hold values from -0.1875 to 0.1875
- student_win: int32 [128, 128, 1024], P('chan', 'dp'), may hold values from 0 to 1
- teacher_win: int32 [192, 128, 1024], P('chan', 'dp'), may hold values from 0 to 1
- pool_win: int32 [128, 128, 256], P('chan', 'dp'), may hold values from 0 to 3
- hint_mask: int32 [128, 1024], P('dp'), may hold values from 0 to 1, as said below
- cotangent: bfloat16 [128, 128, 256], P('chan', 'dp'), may hold values from -6 to 6
- mom_student: float32 [1152, 256], P('dp', 'chan'), may hold values from -96 to 96
- sq_student: float32 [1152, 256], P('dp', 'chan'), as said below
- ema_student: float32 [1152, 256], P('dp', 'chan'), may hold values from -0.1875 to 0.1875
- mom_regress: float32 [1152, 192], P('dp', 'chan'), may hold values from -96 to 96
- sq_regress: float32 [1152, 192], P('dp', 'chan'), as said below
- ema_regress: float32 [1152, 192], P('dp', 'chan'), may hold values from -0.1875 to 0.1875
Outputs:
- pooled: bfloat16 [128, 128, 256], P('chan', 'dp')
- image_grad: bfloat16 [128, 128, 1024], P('chan', 'dp')
- new_student: float32 [1152, 256], P('dp', 'chan')
- new_mom_student: float32 [1152, 256], P('dp', 'chan')
- new_sq_student: float32 [1152, 256], P('dp', 'chan')
- new_ema_student: float32 [1152, 256], P('dp', 'chan')
- low_student: bfloat16 [1152, 256], P('dp', 'chan')
- new_regress: float32 [1152, 192], P('dp', 'chan')
- new_mom_regress: float32 [1152, 192], P('dp', 'chan')
- new_sq_regress: float32 [1152, 192], P('dp', 'chan')
- new_ema_regress: float32 [1152, 192], P('dp', 'chan')
- low_regress: bfloat16 [1152, 192], P('dp', 'chan')
- trust_norms: float32 [2, 2], replicated
The draws below stay inside these ranges and needn't reach their ends.
Inputs may be any that keep to these rules, and one draw needn't show every extreme that they name: `hint_mask`: pixels whose index is a multiple of 4 are always 1. `sq_student`: Positive. `sq_regress`: Positive.
All inputs are finite; a program needn't handle non-finite values.
Results may differ from the reference program's by a relative error of at most 0.0067.
Values may be sent and summed in bfloat16 or wider, within the bound.
A program may use at most 128 MiB of HBM per device.

```python
import math
import jax
import jax.numpy as jnp
from jax import lax

CIN = 128
CS = 128
CR = 192
CT = 192
IMG = 32
STEP = 10
HW = 1024
PHW = 256
IMAGES = 128
KIN = 1152
KREG = 1152
SOUT = 256
TOUT = 384


def scaled_weights(key, rows_len, cols_len):
    position = jnp.arange(rows_len, dtype=jnp.float32) / max(rows_len - 1, 1)
    factor = (1.0 + 0.8 * position) / math.sqrt(rows_len)
    base = jnp.clip(jax.random.normal(key, (rows_len, cols_len), jnp.float32), -6.0, 6.0)
    return base * factor[:, None]


def second_moments(key, rows_len, cols_len):
    grad_scale = 0.4 * math.sqrt(IMAGES * HW)
    position = jnp.arange(rows_len, dtype=jnp.float32) / max(rows_len - 1, 1)
    spread = jnp.exp(jax.random.uniform(key, (rows_len, cols_len), jnp.float32, 0.0, 0.285))
    return 0.001 * grad_scale * grad_scale * spread * (1.0 + 2.0 * position)[:, None]


def draw_student_master(key, part):
    return scaled_weights(key, KIN, SOUT)


def draw_regress_master(key, part):
    return scaled_weights(key, KREG, CR)


def draw_sq_student(key, part):
    return second_moments(key, KIN, SOUT)


def draw_sq_regress(key, part):
    return second_moments(key, KREG, CR)


def draw_hint_mask(key, part):
    level = jax.random.randint(key, (IMAGES, HW), 0, 1000)
    limit = 250 + 500 * jnp.arange(IMAGES, dtype=jnp.int32) // max(IMAGES - 1, 1)
    always_on = jnp.arange(HW, dtype=jnp.int32) % 4 == 0
    chosen = (level < limit[:, None]) | always_on[None, :]
    return jnp.where(chosen, 1, 0).astype(jnp.int32)


def with_ends(array, stream_key, least, top_value):
    shape = array.shape
    spot = [jax.random.randint(jax.random.fold_in(stream_key, axis), (), 0, shape[axis]) for axis in range(len(shape))]
    array = array.at[tuple(spot)].set(least)
    longest = shape.index(max(shape))
    spot[longest] = (spot[longest] + 1) % shape[longest]
    return array.at[tuple(spot)].set(top_value)


def levels(stream_key, extent, pieces, least, high):
    def one(dim, parts):
        steps = jax.random.uniform(jax.random.fold_in(jax.random.fold_in(stream_key, 6), dim), (parts,), jnp.float32, least / len(pieces), high / len(pieces))
        return jnp.repeat(jnp.exp(steps), extent[dim] // parts).reshape((-1,) + (1,) * (len(extent) - dim - 1))

    factor_of = one(*pieces[0])
    for cut in pieces[1:]:
        factor_of = factor_of * one(*cut)
    return factor_of


def normal_values(stream_key, extent, width, most, shards=(), kind=jnp.bfloat16):
    values = width * jax.random.normal(stream_key, extent, jnp.float32)
    if shards:
        values = values * levels(stream_key, extent, shards, -0.22, 0.18)
    return jnp.clip(values, -most, most).astype(kind)


def setup_inputs(seed: int = 0) -> dict:
    streams_of = jax.random.split(jax.random.key(seed), 16)
    return {
        "images": normal_values(streams_of[0], (CIN, IMAGES, HW), 1.0, 6.0, ((0, 4), (1, 8))),
        "student_master": draw_student_master(jax.random.fold_in(streams_of[15], 71), 0),
        "regress_master": draw_regress_master(jax.random.fold_in(streams_of[15], 71), 0),
        "teacher_weight": normal_values(streams_of[3], (KIN, TOUT), KIN ** -0.5, 0.1875, ((1, 4),)),
        "student_win": with_ends(jax.random.randint(streams_of[4], (CS, IMAGES, HW), 0, 2), jax.random.fold_in(streams_of[4], 1), 0, 1).astype(jnp.int32),
        "teacher_win": with_ends(jax.random.randint(streams_of[5], (CT, IMAGES, HW), 0, 2), jax.random.fold_in(streams_of[5], 1), 0, 1).astype(jnp.int32),
        "pool_win": with_ends(jax.random.randint(streams_of[6], (CS, IMAGES, PHW), 0, 4), jax.random.fold_in(streams_of[6], 1), 0, 3).astype(jnp.int32),
        "hint_mask": draw_hint_mask(jax.random.fold_in(streams_of[15], 71), 0),
        "cotangent": normal_values(streams_of[8], (CS, IMAGES, PHW), 1.0, 6.0, ((0, 4), (1, 8))),
        "mom_student": normal_values(streams_of[9], (KIN, SOUT), (0.045 * (IMAGES * HW) ** 0.5), 96.0, ((0, 8), (1, 4)), jnp.float32),
        "sq_student": draw_sq_student(jax.random.fold_in(streams_of[15], 71), 0),
        "ema_student": normal_values(streams_of[11], (KIN, SOUT), KIN ** -0.5, 0.1875, ((0, 8), (1, 4)), jnp.float32),
        "mom_regress": normal_values(streams_of[12], (KREG, CR), (0.045 * (IMAGES * HW) ** 0.5), 96.0, ((0, 8), (1, 4)), jnp.float32),
        "sq_regress": draw_sq_regress(jax.random.fold_in(streams_of[15], 71), 0),
        "ema_regress": normal_values(streams_of[14], (KREG, CR), KREG ** -0.5, 0.1875, ((0, 8), (1, 4)), jnp.float32),
    }


HINT_WEIGHT = 0.1
LEARN_RATE = 0.5
BETA_ONE = 0.9
BETA_TWO = 0.999
EPSILON = 1e-06
DECAY = 0.01
EMA_KEEP = 0.75

@jax.custom_vjp
def low(v):
    return lax.optimization_barrier(v.astype(jnp.bfloat16)).astype(jnp.float32)

@jax.custom_vjp
def low_back(v):
    return v

def low_keep(v):
    return (low(v), None)

def low_pass(kept, grad):
    return (grad,)

def back_keep(v):
    return (v, None)

def back_low(kept, grad):
    return (low(grad),)
low.defvjp(low_keep, low_pass)
low_back.defvjp(back_keep, back_low)

def convolve(inputs, weights):
    channels, batch_len, pixels = inputs.shape
    left_view = inputs.reshape(channels, batch_len, IMG, IMG)
    kernel = weights.reshape(3, 3, channels, weights.shape[1])
    result = lax.conv_general_dilated(left_view, kernel, (1, 1), ((1, 1), (1, 1)), dimension_numbers=('CNHW', 'HWIO', 'CNHW'), precision=lax.Precision.HIGHEST)
    return result.reshape(result.shape[0], batch_len, pixels)

def maxout(pre_values, winners):
    paired = pre_values.reshape(winners.shape[0], 2, winners.shape[1], winners.shape[2])
    return jnp.where(winners == 1, paired[:, 1], paired[:, 0])

def pool_values(values, winners):
    half_side = IMG // 2
    cell_grid = values.reshape(values.shape[0], values.shape[1], half_side, 2, half_side, 2)
    pooled_sum = jnp.zeros(winners.shape, values.dtype)
    for corner in range(4):
        corner_vals = cell_grid[:, :, :, corner // 2, :, corner % 2].reshape(winners.shape)
        pooled_sum = pooled_sum + jnp.where(winners == corner, corner_vals, jnp.zeros_like(corner_vals))
    return pooled_sum

def lamb_update(weights, grads, moment, second):
    moment_new = BETA_ONE * moment + (1.0 - BETA_ONE) * grads
    second_new = BETA_TWO * second + (1.0 - BETA_TWO) * grads * grads
    moment_hat = moment_new / (1.0 - BETA_ONE ** STEP)
    second_hat = second_new / (1.0 - BETA_TWO ** STEP)
    update = moment_hat / (jnp.sqrt(second_hat) + EPSILON) + DECAY * weights
    return (moment_new, second_new, update)

def reference(images, student_master, regress_master, teacher_weight, student_win, teacher_win, pool_win, hint_mask, cotangent, mom_student, sq_student, ema_student, mom_regress, sq_regress, ema_regress):
    block_len = math.gcd(IMAGES, 32)
    blocks = IMAGES // block_len
    teacher_full = teacher_weight.astype(jnp.float32)

    def one_block(sums_carry, block_idx):
        offset = (block_idx * block_len).astype(jnp.int32)
        x_block = lax.dynamic_slice_in_dim(images, offset, block_len, 1).astype(jnp.float32)
        student_sel = lax.dynamic_slice_in_dim(student_win, offset, block_len, 1)
        teacher_sel = lax.dynamic_slice_in_dim(teacher_win, offset, block_len, 1)
        pool_sel = lax.dynamic_slice_in_dim(pool_win, offset, block_len, 1)
        mask_block = lax.dynamic_slice_in_dim(hint_mask, offset, block_len, 0).astype(jnp.float32)
        cot_block = lax.dynamic_slice_in_dim(cotangent, offset, block_len, 1).astype(jnp.float32)
        teacher_out = maxout(convolve(x_block, teacher_full), teacher_sel)
        counts = lax.optimization_barrier(jnp.sum(mask_block, axis=1))
        weight_map = HINT_WEIGHT * (HW / counts)[:, None] * mask_block

        def forward(x_in, student_w, regress_w):
            pre_act = low_back(convolve(x_in, low(student_w)))
            student_out = maxout(pre_act, student_sel)
            pooled_out = pool_values(student_out, pool_sel)
            regressed = low_back(convolve(low(student_out), low(regress_w)))
            mismatch = regressed - teacher_out
            hint_loss = 0.5 * jnp.sum(weight_map[None] * mismatch * mismatch)
            return (pooled_out, hint_loss)
        (pooled_out, hint_loss), pullback = jax.vjp(forward, x_block, student_master, regress_master)
        grad_x, grad_student, grad_regress = pullback((cot_block, jnp.ones((), hint_loss.dtype)))
        new_carry = (sums_carry[0] + grad_student, sums_carry[1] + grad_regress)
        return (new_carry, (pooled_out.astype(jnp.bfloat16), grad_x.astype(jnp.bfloat16)))
    start_sums = (jnp.zeros(student_master.shape, jnp.float32), jnp.zeros(regress_master.shape, jnp.float32))
    (student_grad, regress_grad), (pooled_parts, grad_parts) = lax.scan(one_block, start_sums, jnp.arange(blocks, dtype=jnp.int32))
    pooled = pooled_parts.transpose(1, 0, 2, 3).reshape(CS, IMAGES, PHW)
    image_grad = grad_parts.transpose(1, 0, 2, 3).reshape(CIN, IMAGES, HW)
    mom_s, sq_s, upd_s = lamb_update(student_master, student_grad, mom_student, sq_student)
    mom_r, sq_r, upd_r = lamb_update(regress_master, regress_grad, mom_regress, sq_regress)
    norm_ws = jnp.sqrt(jnp.sum(student_master * student_master))
    norm_us = jnp.sqrt(jnp.sum(upd_s * upd_s))
    norm_wr = jnp.sqrt(jnp.sum(regress_master * regress_master))
    norm_ur = jnp.sqrt(jnp.sum(upd_r * upd_r))
    new_student = student_master - LEARN_RATE * (norm_ws / norm_us) * upd_s
    new_regress = regress_master - LEARN_RATE * (norm_wr / norm_ur) * upd_r
    ema_s = EMA_KEEP * ema_student + (1.0 - EMA_KEEP) * new_student
    ema_r = EMA_KEEP * ema_regress + (1.0 - EMA_KEEP) * new_regress
    trust_norms = jnp.stack([jnp.stack([norm_ws, norm_us]), jnp.stack([norm_wr, norm_ur])])
    return (pooled, image_grad, new_student, mom_s, sq_s, ema_s, new_student.astype(jnp.bfloat16), new_regress, mom_r, sq_r, ema_r, new_regress.astype(jnp.bfloat16), trust_norms)
```

```python
import functools

import jax
import jax.numpy as jnp
from jax import lax
from jax.experimental import pallas as pl
from jax.experimental.pallas import tpu as pltpu
from jax.sharding import PartitionSpec as P

IMG = 32
STEP = 10
HINT_WEIGHT = 0.1
LEARN_RATE = 0.5
BETA_ONE = 0.9
BETA_TWO = 0.999
EPSILON = 1e-06
DECAY = 0.01
EMA_KEEP = 0.75

MESH = pl.DeviceIdType.MESH
F32 = jnp.float32
BF16 = jnp.bfloat16
CHUNK = 256
LANES = 128


def dot(left, right):
    return jnp.dot(left, right, preferred_element_type=F32)


def dot_nt(left, right):
    return lax.dot_general(left, right, (((1,), (1,)), ((), ())), preferred_element_type=F32)


def layer_kernel(
    size,
    images,
    swin,
    twin,
    pwin,
    cot,
    mask,
    w_in,
    w_reg,
    w_reg_back,
    w_in_back,
    pool_out,
    grad_out,
    sgrad,
    rgrad,
    raw,
    raw_cot,
    wide,
    swin_wide,
    twin_wide,
    pwin_wide,
    cot_wide,
    load_sem,
    send,
    send_pool,
    held,
    held_pool,
    low_part,
    pool_part,
    edge,
    up,
    x_cols,
    o_cols,
    h_cols,
    p_cols,
    out_low,
    pool_back,
    hint,
    pre_grad,
    in_send,
    in_recv,
    pool_in_send,
    pool_in_recv,
    own_sem,
    out_send,
    out_recv,
    pool_out_send,
    pool_out_recv,
    own_out_sem,
):
    n, batch, cl, tl = size["n"], size["batch"], size["cl"], size["tl"]
    slots = batch // n
    chans, touts = n * cl, n * tl
    pixels = IMG * IMG
    cells = pixels // 4
    me = lax.axis_index("chan")

    barrier = pltpu.get_barrier_semaphore()
    for step in range(1, n):
        pl.semaphore_signal(
            barrier, inc=1, device_id={"chan": lax.rem(me + step, n)}, device_id_type=MESH
        )
    pl.semaphore_wait(barrier, n - 1)

    loads = [
        pltpu.make_async_copy(images, raw, load_sem.at[0]),
        pltpu.make_async_copy(cot, raw_cot, load_sem.at[1]),
    ]
    for src, dst in ((swin, swin_wide), (twin, twin_wide), (pwin, pwin_wide)):
        for j in range(dst.shape[0]):
            loads.append(
                pltpu.make_async_copy(
                    src.at[:, pl.ds(j * LANES, LANES)], dst.at[j], load_sem.at[len(loads)]
                )
            )
    for copy in loads:
        copy.start()
    for copy in loads:
        copy.wait()
    for j in range(wide.shape[0]):
        wide[j] = raw[:, j * LANES : (j + 1) * LANES].astype(F32)
    for j in range(cot_wide.shape[0]):
        cot_wide[j] = raw_cot[:, j * LANES : (j + 1) * LANES].astype(F32)

    def in_copies(slot, step):
        to = lax.rem(me + step, n)
        return (
            pltpu.make_async_remote_copy(
                send.at[slot, to],
                held.at[slot, me],
                in_send.at[slot, step],
                in_recv.at[slot, step],
                device_id={"chan": to},
                device_id_type=MESH,
            ),
            pltpu.make_async_remote_copy(
                send_pool.at[slot, to],
                held_pool.at[slot, me],
                pool_in_send.at[slot, step],
                pool_in_recv.at[slot, step],
                device_id={"chan": to},
                device_id_type=MESH,
            ),
        )

    def own_copies(slot):
        return (
            pltpu.make_async_copy(send.at[slot, me], held.at[slot, me], own_sem.at[slot, 0]),
            pltpu.make_async_copy(
                send_pool.at[slot, me], held_pool.at[slot, me], own_sem.at[slot, 1]
            ),
        )

    def out_copies(slot, step):
        to = lax.rem(me + step, n)
        return (
            pltpu.make_async_remote_copy(
                low_part.at[slot, pl.ds(pl.multiple_of(to * cl, cl), cl)],
                grad_out.at[me * slots + slot],
                out_send.at[slot, step],
                out_recv.at[slot, step],
                device_id={"chan": to},
                device_id_type=MESH,
            ),
            pltpu.make_async_remote_copy(
                pool_part.at[slot, pl.ds(pl.multiple_of(to * cl, cl), cl)],
                pool_out.at[me * slots + slot],
                pool_out_send.at[slot, step],
                pool_out_recv.at[slot, step],
                device_id={"chan": to},
                device_id_type=MESH,
            ),
        )

    def own_out(slot):
        mine = pl.ds(pl.multiple_of(me * cl, cl), cl)
        return (
            pltpu.make_async_copy(
                low_part.at[slot, mine], grad_out.at[me * slots + slot], own_out_sem.at[slot, 0]
            ),
            pltpu.make_async_copy(
                pool_part.at[slot, mine], pool_out.at[me * slots + slot], own_out_sem.at[slot, 1]
            ),
        )

    def prepare(slot, carry):
        for to in range(n):
            row = to * slots + slot
            for src, dst, first, rows in (
                (wide, send, 0, cl),
                (swin_wide, send, cl, cl),
                (twin_wide, send, 2 * cl, tl),
                (pwin_wide, send_pool, 0, cl),
                (cot_wide, send_pool, cl, cl),
            ):
                for j in range(src.shape[0]):
                    dst[slot, to, first : first + rows, j * LANES : (j + 1) * LANES] = (
                        src[j, pl.ds(row, rows, stride=batch), :].astype(F32).astype(BF16)
                    )
        for step in range(1, n):
            for copy in in_copies(slot, step):
                copy.start()
        for copy in own_copies(slot):
            copy.start()
        return carry

    lax.fori_loop(0, slots, prepare, 0)

    lane = lax.broadcasted_iota(jnp.int32, (16, pixels), 1)
    row_of, col_of = lane // IMG, lane % IMG
    for which, bad in enumerate((row_of == 0, row_of == IMG - 1, col_of == 0, col_of == IMG - 1)):
        edge[which] = jnp.where(bad, 0.0, 1.0).astype(BF16)
    cell = lax.broadcasted_iota(jnp.int32, (cells, pixels), 0)
    spot = lax.broadcasted_iota(jnp.int32, (cells, pixels), 1)
    home = (spot // (2 * IMG)) * (IMG // 2) + (spot % IMG) // 2
    up[...] = jnp.where(cell == home, 1.0, 0.0).astype(BF16)
    sgrad[...] = jnp.zeros_like(sgrad)
    rgrad[...] = jnp.zeros_like(rgrad)

    def columns(load, rows, dst):
        def group(g, carry):
            first = pl.multiple_of(g * 16, 16)
            base = load(first)
            for ky in range(3):
                if ky == 1:
                    moved = base
                else:
                    moved = pltpu.roll(base, (pixels - IMG * (ky - 1)) % pixels, 1)
                    moved = moved * edge[0 if ky == 0 else 1]
                for kx in range(3):
                    if kx == 1:
                        tap = moved
                    else:
                        tap = pltpu.roll(moved, (pixels - (kx - 1)) % pixels, 1)
                        tap = tap * edge[2 if kx == 0 else 3]
                    dst[pl.ds((3 * ky + kx) * rows + first, 16), :] = tap
            return carry

        lax.fori_loop(0, rows // 16, group, 0)

    def chunks(body):
        def one(c, carry):
            body(pl.ds(pl.multiple_of(c * CHUNK, CHUNK), CHUNK))
            return carry

        lax.fori_loop(0, pixels // CHUNK, one, 0)

    def corner_of(here):
        at = lax.broadcasted_iota(jnp.int32, (1, CHUNK), 1)
        return (2 * ((at // IMG) % 2) + at % 2).astype(F32)

    def image(slot, carry):
        for step in range(1, n):
            for copy in in_copies(slot, step):
                copy.wait_recv()
        for copy in own_copies(slot):
            copy.wait()

        def image_rows(first):
            return held[slot, first // cl, pl.ds(pl.multiple_of(first % cl, 16), 16), :]

        columns(image_rows, chans, x_cols)
        pool_part[slot] = jnp.zeros((chans, cells), BF16)

        def head(here):
            pre = dot(w_in[0 : 2 * chans, :], x_cols[:, here])
            pick = held[slot, :, cl : 2 * cl, here].reshape(chans, CHUNK).astype(F32)
            value = jnp.where(pick > 0.5, pre[chans:], pre[:chans]).astype(BF16)
            out_low[:, here] = value
            cell_win = held_pool[slot, :, 0:cl, :].reshape(chans, cells)
            cell_cot = held_pool[slot, :, cl : 2 * cl, :].reshape(chans, cells)
            chosen = dot(cell_win, up[:, here]) == corner_of(here)
            spread = dot(cell_cot, up[:, here])
            pool_back[:, here] = jnp.where(chosen, spread, 0.0).astype(BF16)
            kept = jnp.where(chosen, value.astype(F32), 0.0).astype(BF16)
            part = dot_nt(kept, up[:, here])
            pool_part[slot] = (pool_part[slot].astype(F32) + part).astype(BF16)

        chunks(head)
        columns(lambda first: out_low[pl.ds(first, 16), :], chans, o_cols)

        spot_mask = mask[pl.ds(me * slots + slot, 1), :].astype(F32)
        count = jnp.sum(spot_mask, axis=1, keepdims=True)
        scale = HINT_WEIGHT * (pixels / count)

        def hints(here):
            teach = dot(w_in[2 * chans :, :], x_cols[:, here])
            pick = held[slot, :, 2 * cl :, here].reshape(touts, CHUNK).astype(F32)
            target = jnp.where(pick > 0.5, teach[touts:], teach[:touts])
            guess = dot(w_reg[...], o_cols[:, here])
            weight = scale * mask[pl.ds(me * slots + slot, 1), here].astype(F32)
            hint[:, here] = (weight * (guess - target)).astype(BF16)

        chunks(hints)
        columns(lambda first: hint[pl.ds(first, 16), :], hint.shape[0], h_cols)
        rgrad[...] += dot_nt(o_cols[...], hint[...])

        def back(here):
            total = dot(w_reg_back[...], h_cols[:, here]) + pool_back[:, here].astype(F32)
            pick = held[slot, :, cl : 2 * cl, here].reshape(chans, CHUNK).astype(F32) > 0.5
            pre_grad[0:chans, here] = jnp.where(pick, 0.0, total).astype(BF16)
            pre_grad[chans:, here] = jnp.where(pick, total, 0.0).astype(BF16)

        chunks(back)
        columns(lambda first: pre_grad[pl.ds(first, 16), :], 2 * chans, p_cols)
        sgrad[...] += dot_nt(x_cols[...], pre_grad[...])

        def image_back(here):
            low_part[slot, :, here] = dot(w_in_back[...], p_cols[:, here]).astype(BF16)

        chunks(image_back)
        for step in range(1, n):
            for copy in out_copies(slot, step):
                copy.start()
        for copy in own_out(slot):
            copy.start()
        return carry

    lax.fori_loop(0, slots, image, 0)

    def finish(slot, carry):
        for step in range(1, n):
            for copy in in_copies(slot, step):
                copy.wait_send()
            for copy in out_copies(slot, step):
                copy.wait()
        for copy in own_out(slot):
            copy.wait()
        return carry

    lax.fori_loop(0, slots, finish, 0)


def layer_pass(n, images, swin, twin, pwin, cot, mask, w_in, w_reg, w_reg_back, w_in_back):
    cl, batch, pixels = images.shape
    tl = twin.shape[0]
    cells = pwin.shape[2]
    slots = batch // n
    chans, touts = n * cl, n * tl
    regs = w_reg.shape[0]
    size = {"n": n, "batch": batch, "cl": cl, "tl": tl}
    vmem = pl.BlockSpec(memory_space=pltpu.VMEM)
    flat = lambda a: a.reshape(a.shape[0] * a.shape[1], a.shape[2])
    flops = 2 * slots * pixels * 9 * chans * (3 * 2 * chans + 2 * touts + 3 * regs)
    return pl.pallas_call(
        functools.partial(layer_kernel, size),
        out_shape=[
            jax.ShapeDtypeStruct((batch, cl, cells), BF16),
            jax.ShapeDtypeStruct((batch, cl, pixels), BF16),
            jax.ShapeDtypeStruct((9 * chans, 2 * chans), F32),
            jax.ShapeDtypeStruct((9 * chans, regs), F32),
        ],
        in_specs=[pl.BlockSpec(memory_space=pl.ANY)] * 5 + [vmem] * 5,
        out_specs=[vmem] * 4,
        scratch_shapes=[
            pltpu.VMEM((cl * batch, pixels), BF16),
            pltpu.VMEM((cl * batch, cells), BF16),
            pltpu.VMEM((pixels // LANES, cl * batch, LANES), F32),
            pltpu.VMEM((pixels // LANES, cl * batch, LANES), jnp.int32),
            pltpu.VMEM((pixels // LANES, tl * batch, LANES), jnp.int32),
            pltpu.VMEM((cells // LANES, cl * batch, LANES), jnp.int32),
            pltpu.VMEM((cells // LANES, cl * batch, LANES), F32),
            pltpu.SemaphoreType.DMA((2 + 2 * (pixels // LANES) + cells // LANES,)),
            pltpu.VMEM((slots, n, 2 * cl + tl, pixels), BF16),
            pltpu.VMEM((slots, n, 2 * cl, cells), BF16),
            pltpu.VMEM((slots, n, 2 * cl + tl, pixels), BF16),
            pltpu.VMEM((slots, n, 2 * cl, cells), BF16),
            pltpu.VMEM((slots, chans, pixels), BF16),
            pltpu.VMEM((slots, chans, cells), BF16),
            pltpu.VMEM((4, 16, pixels), BF16),
            pltpu.VMEM((cells, pixels), BF16),
            pltpu.VMEM((9 * chans, pixels), BF16),
            pltpu.VMEM((9 * chans, pixels), BF16),
            pltpu.VMEM((9 * regs, pixels), BF16),
            pltpu.VMEM((9 * 2 * chans, pixels), BF16),
            pltpu.VMEM((chans, pixels), BF16),
            pltpu.VMEM((chans, pixels), BF16),
            pltpu.VMEM((regs, pixels), BF16),
            pltpu.VMEM((2 * chans, pixels), BF16),
            pltpu.SemaphoreType.DMA((slots, n)),
            pltpu.SemaphoreType.DMA((slots, n)),
            pltpu.SemaphoreType.DMA((slots, n)),
            pltpu.SemaphoreType.DMA((slots, n)),
            pltpu.SemaphoreType.DMA((slots, 2)),
            pltpu.SemaphoreType.DMA((slots, n)),
            pltpu.SemaphoreType.DMA((slots, n)),
            pltpu.SemaphoreType.DMA((slots, n)),
            pltpu.SemaphoreType.DMA((slots, n)),
            pltpu.SemaphoreType.DMA((slots, 2)),
        ],
        compiler_params=pltpu.CompilerParams(
            collective_id=0, has_side_effects=True, vmem_limit_bytes=56 << 20
        ),
        cost_estimate=pl.CostEstimate(flops=flops, bytes_accessed=16 << 20, transcendentals=0),
        name="layer",
    )(
        flat(images),
        flat(swin),
        flat(twin),
        flat(pwin),
        flat(cot),
        mask,
        w_in,
        w_reg,
        w_reg_back,
        w_in_back,
    )


def split_pieces(weights):
    rows, cols = weights.shape
    return weights.reshape(rows, cols // 2, 2).transpose(2, 1, 0).reshape(cols, rows)


def back_weights(weights, outs):
    channels = weights.shape[0] // 9
    taps = weights.reshape(9, channels, outs)[::-1]
    return taps.transpose(1, 0, 2).reshape(channels, 9 * outs)


def lamb_update(weights, grads, moment, second):
    moment_new = BETA_ONE * moment + (1.0 - BETA_ONE) * grads
    second_new = BETA_TWO * second + (1.0 - BETA_TWO) * grads * grads
    moment_hat = moment_new / (1.0 - BETA_ONE**STEP)
    second_hat = second_new / (1.0 - BETA_TWO**STEP)
    update = moment_hat / (jnp.sqrt(second_hat) + EPSILON) + DECAY * weights
    return (moment_new, second_new, update)


def on_device(
    n,
    images,
    student_master,
    regress_master,
    teacher_weight,
    student_win,
    teacher_win,
    pool_win,
    hint_mask,
    cotangent,
    mom_student,
    sq_student,
    ema_student,
    mom_regress,
    sq_regress,
    ema_regress,
):
    student_full = lax.all_gather(student_master.astype(BF16), "dp", axis=0, tiled=True)
    student_full = lax.all_gather(student_full, "chan", axis=1, tiled=True)
    regress_full = lax.all_gather(regress_master.astype(BF16), "dp", axis=0, tiled=True)
    regress_full = lax.all_gather(regress_full, "chan", axis=1, tiled=True)
    teacher_full = lax.all_gather(teacher_weight, "chan", axis=1, tiled=True)
    souts = student_full.shape[1]
    regs = regress_full.shape[1]
    student_rows = split_pieces(student_full)
    w_in = jnp.concatenate([student_rows, split_pieces(teacher_full)], axis=0)
    pooled, image_grad, student_part, regress_part = layer_pass(
        n,
        images,
        student_win,
        teacher_win,
        pool_win,
        cotangent,
        hint_mask,
        w_in,
        regress_full.T,
        back_weights(regress_full, regs),
        back_weights(student_rows.T, souts),
    )
    half = souts // 2
    student_part = student_part.reshape(-1, 2, half).transpose(0, 2, 1).reshape(-1, souts)
    student_grad = lax.psum_scatter(student_part, "dp", scatter_dimension=0, tiled=True)
    student_grad = lax.psum_scatter(student_grad, "chan", scatter_dimension=1, tiled=True)
    regress_grad = lax.psum_scatter(regress_part, "dp", scatter_dimension=0, tiled=True)
    regress_grad = lax.psum_scatter(regress_grad, "chan", scatter_dimension=1, tiled=True)
    mom_s, sq_s, upd_s = lamb_update(student_master, student_grad, mom_student, sq_student)
    mom_r, sq_r, upd_r = lamb_update(regress_master, regress_grad, mom_regress, sq_regress)
    all_sums = lax.psum(
        jnp.stack(
            [
                jnp.sum(student_master * student_master),
                jnp.sum(upd_s * upd_s),
                jnp.sum(regress_master * regress_master),
                jnp.sum(upd_r * upd_r),
            ]
        ),
        ("dp", "chan"),
    )
    norms = jnp.sqrt(all_sums)
    new_student = student_master - LEARN_RATE * (norms[0] / norms[1]) * upd_s
    new_regress = regress_master - LEARN_RATE * (norms[2] / norms[3]) * upd_r
    ema_s = EMA_KEEP * ema_student + (1.0 - EMA_KEEP) * new_student
    ema_r = EMA_KEEP * ema_regress + (1.0 - EMA_KEEP) * new_regress
    return (
        pooled.transpose(1, 0, 2),
        image_grad.transpose(1, 0, 2),
        new_student,
        mom_s,
        sq_s,
        ema_s,
        new_student.astype(BF16),
        new_regress,
        mom_r,
        sq_r,
        ema_r,
        new_regress.astype(BF16),
        norms.reshape(2, 2),
    )


def solution(mesh):
    acts = P("chan", "dp", None)
    rows = P("dp", "chan")
    in_specs = (
        (acts, rows, rows, P(None, "chan"))
        + (acts, acts, acts, P("dp", None), acts)
        + (rows,) * 6
    )
    out_specs = (acts, acts) + (rows,) * 10 + (P(),)
    return jax.shard_map(
        functools.partial(on_device, mesh.shape["chan"]),
        mesh=mesh,
        in_specs=in_specs,
        out_specs=out_specs,
        check_vma=False,
    )
```

```python
import functools
import types

import jax
import jax.numpy as jnp
from jax import lax
from jax.experimental import pallas as pl
from jax.experimental.pallas import tpu as pltpu
from jax.sharding import PartitionSpec as P

IMG = 32
STEP = 10
HINT_WEIGHT = 0.1
LEARN_RATE = 0.5
BETA_ONE = 0.9
BETA_TWO = 0.999
EPSILON = 1e-06
DECAY = 0.01
EMA_KEEP = 0.75

MESH = pl.DeviceIdType.MESH
F32 = jnp.float32
BF16 = jnp.bfloat16
CHUNK = 256
LANES = 128


def dot(left, right):
    return jnp.dot(left, right, preferred_element_type=F32)


def dot_nt(left, right, precision=None):
    return lax.dot_general(
        left, right, (((1,), (1,)), ((), ())), precision=precision, preferred_element_type=F32
    )


def one_hot(shape, target, axis):
    at = lax.broadcasted_iota(jnp.int32, shape, axis)
    return jnp.where(at == target, 1.0, 0.0).astype(BF16)


def layer_kernel(size, names, *refs):
    r = types.SimpleNamespace(**dict(zip(names, refs)))
    n, batch, cl, tl, rl = size["n"], size["batch"], size["cl"], size["tl"], size["rl"]
    fused, group = size["fused"], size["group"]
    slots = batch // n
    chans, touts, regs = n * cl, n * tl, n * rl
    pixels = IMG * IMG
    cells = pixels // 4
    me = lax.axis_index("chan")
    row = lax.axis_index("dp")
    core, chip, pairs = row % 2, row // 2, group // 2
    held, send = r.held, r.send

    def beside(step):
        return lax.rem(me + step, n)

    def at_chan(index):
        return {"chan": index}

    def at_row(index):
        return {"dp": index}

    def remote(src, dst, out_sem, in_sem, device):
        return pltpu.make_async_remote_copy(
            src, dst, out_sem, in_sem, device_id=device, device_id_type=MESH
        )

    greeted = [at_chan(beside(step)) for step in range(1, n)]
    if fused:
        greeted += [at_row(lax.rem(row + step, group)) for step in range(1, group)]

    loads = [
        pltpu.make_async_copy(r.images, r.raw, r.load_sem.at[0]),
        pltpu.make_async_copy(r.cot, r.raw_cot, r.load_sem.at[1]),
    ]
    for src, dst in ((r.swin, r.swin_wide), (r.twin, r.twin_wide), (r.pwin, r.pwin_wide)):
        for j in range(dst.shape[0]):
            loads.append(
                pltpu.make_async_copy(
                    src.at[:, pl.ds(j * LANES, LANES)], dst.at[j], r.load_sem.at[len(loads)]
                )
            )
    for copy in loads:
        copy.start()

    barrier = pltpu.get_barrier_semaphore()
    for device in greeted:
        pl.semaphore_signal(barrier, inc=1, device_id=device, device_id_type=MESH)

    if fused:
        depth = r.student_master.shape[0]

        def block(index):
            return pl.ds(pl.multiple_of(index * depth, 16), depth)

        mine = block(row)
        r.filters[me, mine, :] = jnp.zeros((depth, r.filters.shape[2]), BF16)
        r.filters[me, mine, 0 : 2 * cl] = r.student_master[...].astype(BF16)
        r.filters[me, mine, 2 * cl : 2 * cl + rl] = r.regress_master[...].astype(BF16)
        r.filters[me, mine, LANES : LANES + 2 * tl] = r.teacher[mine, :]

    pl.semaphore_wait(barrier, len(greeted))

    if fused:
        filter_z = [
            remote(
                r.filters.at[me, mine],
                r.filters.at[me, mine],
                r.fz_send.at[step],
                r.fz_recv.at[step],
                at_chan(beside(step)),
            )
            for step in range(1, n)
        ]
        for copy in filter_z:
            copy.start()

    for copy in loads:
        copy.wait()
    for j in range(r.wide.shape[0]):
        r.wide[j] = r.raw[:, j * LANES : (j + 1) * LANES].astype(F32)
    for j in range(r.cot_wide.shape[0]):
        r.cot_wide[j] = r.raw_cot[:, j * LANES : (j + 1) * LANES].astype(F32)

    def in_copies(slot, step):
        to = beside(step)
        return (
            remote(
                send.at[slot, to],
                held.at[slot, me],
                r.in_send.at[slot, step],
                r.in_recv.at[slot, step],
                at_chan(to),
            ),
            remote(
                r.send_pool.at[slot, to],
                r.held_pool.at[slot, me],
                r.pool_in_send.at[slot, step],
                r.pool_in_recv.at[slot, step],
                at_chan(to),
            ),
        )

    def own_copies(slot):
        return (
            pltpu.make_async_copy(send.at[slot, me], held.at[slot, me], r.own_sem.at[slot, 0]),
            pltpu.make_async_copy(
                r.send_pool.at[slot, me], r.held_pool.at[slot, me], r.own_sem.at[slot, 1]
            ),
        )

    def lanes_of(index):
        return pl.ds(pl.multiple_of(index * cl, cl), cl)

    def out_copies(slot, step):
        to = beside(step)
        return (
            remote(
                r.low_part.at[slot, lanes_of(to)],
                r.grad_out.at[me * slots + slot],
                r.out_send.at[slot, step],
                r.out_recv.at[slot, step],
                at_chan(to),
            ),
            remote(
                r.pool_part.at[slot, lanes_of(to)],
                r.pool_out.at[me * slots + slot],
                r.pool_out_send.at[slot, step],
                r.pool_out_recv.at[slot, step],
                at_chan(to),
            ),
        )

    def own_out(slot):
        here = me * slots + slot
        return (
            pltpu.make_async_copy(
                r.low_part.at[slot, lanes_of(me)], r.grad_out.at[here], r.own_out_sem.at[slot, 0]
            ),
            pltpu.make_async_copy(
                r.pool_part.at[slot, lanes_of(me)], r.pool_out.at[here], r.own_out_sem.at[slot, 1]
            ),
        )

    def prepare(slot, carry):
        for to in range(n):
            first_row = to * slots + slot
            for src, dst, first, rows in (
                (r.wide, send, 0, cl),
                (r.swin_wide, send, cl, cl),
                (r.twin_wide, send, 2 * cl, tl),
                (r.pwin_wide, r.send_pool, 0, cl),
                (r.cot_wide, r.send_pool, cl, cl),
            ):
                for j in range(src.shape[0]):
                    dst[slot, to, first : first + rows, j * LANES : (j + 1) * LANES] = (
                        src[j, pl.ds(first_row, rows, stride=batch), :].astype(F32).astype(BF16)
                    )
        for step in range(1, n):
            for copy in in_copies(slot, step):
                copy.start()
        for copy in own_copies(slot):
            copy.start()
        return carry

    lax.fori_loop(0, slots, prepare, 0)

    lane = lax.broadcasted_iota(jnp.int32, (16, pixels), 1)
    row_of, col_of = lane // IMG, lane % IMG
    for which, bad in enumerate((row_of == 0, row_of == IMG - 1, col_of == 0, col_of == IMG - 1)):
        r.edge[which] = jnp.where(bad, 0.0, 1.0).astype(BF16)
    spot = lax.broadcasted_iota(jnp.int32, (1, pixels), 1)
    home = (spot // (2 * IMG)) * (IMG // 2) + (spot % IMG) // 2
    r.up[...] = one_hot((cells, pixels), home, 0)
    r.sgrad[...] = jnp.zeros_like(r.sgrad)
    r.rgrad[...] = jnp.zeros_like(r.rgrad)

    if fused:
        picked = 2 * cl + rl + 2 * tl
        at = lax.broadcasted_iota(jnp.int32, (picked, 1), 0)
        teach = at - 2 * cl - rl
        lane_at = jnp.where(
            at < 2 * cl,
            2 * (at % cl) + at // cl,
            jnp.where(at < 2 * cl + rl, at, LANES + 2 * (teach % tl) + teach // tl),
        )
        r.gather_rows[...] = one_hot((picked, r.filters.shape[2]), lane_at, 1)
        for z in range(n):
            at = lax.broadcasted_iota(jnp.int32, (LANES, 1), 0)
            col_at = jnp.where(
                at < 2 * cl,
                (at % 2) * chans + z * cl + at // 2,
                jnp.where(at < 2 * cl + rl, 2 * chans + z * rl + at - 2 * cl, -1),
            )
            r.spread[z] = one_hot((LANES, r.spread.shape[2]), col_at, 1)

        for copy in filter_z:
            copy.wait_recv()

        def filter_chip(step):
            to = lax.rem(chip + step, pairs)
            return remote(
                r.filters.at[:, mine],
                r.filters.at[:, mine],
                r.fx_send.at[step],
                r.fx_recv.at[step],
                at_row(2 * to + core),
            )

        def filter_core(step):
            rows = block(2 * lax.rem(chip + pairs - step, pairs) + core)
            return remote(
                r.filters.at[:, rows],
                r.filters.at[:, rows],
                r.fc_send.at[step],
                r.fc_recv.at[step],
                at_row(row + 1 - 2 * core),
            )

        for step in range(1, pairs):
            filter_chip(step).start()
        filter_core(0).start()
        for step in range(1, pairs):
            filter_chip(step).wait_recv()
            filter_core(step).start()
        for step in range(pairs):
            filter_core(step).wait_recv()

        for z in range(n):
            rows_of = dot_nt(r.gather_rows[...], r.filters[z]).astype(BF16)
            first = 0
            for dst, start, many in (
                (r.w_in, z * cl, cl),
                (r.w_in, chans + z * cl, cl),
                (r.w_reg, z * rl, rl),
                (r.w_in, 2 * chans + z * tl, tl),
                (r.w_in, 2 * chans + touts + z * tl, tl),
            ):
                dst[start : start + many, :] = rows_of[first : first + many, :]
                first += many
        for tap in range(9):
            rows = slice((8 - tap) * chans, (9 - tap) * chans)
            total = dot(r.filters[0, rows, 0:LANES], r.spread[0])
            for z in range(1, n):
                total += dot(r.filters[z, rows, 0:LANES], r.spread[z])
            total = total.astype(BF16)
            r.w_in_back[:, tap * 2 * chans : (tap + 1) * 2 * chans] = total[:, 0 : 2 * chans]
            r.w_reg_back[:, tap * regs : (tap + 1) * regs] = total[:, 2 * chans : 2 * chans + regs]

    def columns(load, rows, dst):
        def group(g, carry):
            first = pl.multiple_of(g * 16, 16)
            base = load(first)
            for ky in range(3):
                if ky == 1:
                    moved = base
                else:
                    moved = pltpu.roll(base, (pixels - IMG * (ky - 1)) % pixels, 1)
                    moved = moved * r.edge[0 if ky == 0 else 1]
                for kx in range(3):
                    if kx == 1:
                        tap = moved
                    else:
                        tap = pltpu.roll(moved, (pixels - (kx - 1)) % pixels, 1)
                        tap = tap * r.edge[2 if kx == 0 else 3]
                    dst[pl.ds((3 * ky + kx) * rows + first, 16), :] = tap
            return carry

        lax.fori_loop(0, rows // 16, group, 0)

    def chunks(body):
        def one(c, carry):
            body(pl.ds(pl.multiple_of(c * CHUNK, CHUNK), CHUNK))
            return carry

        lax.fori_loop(0, pixels // CHUNK, one, 0)

    def corner_of(here):
        at = lax.broadcasted_iota(jnp.int32, (1, CHUNK), 1)
        return (2 * ((at // IMG) % 2) + at % 2).astype(F32)

    if fused:
        parts = ((r.rgrad, r.rc_send, r.rc_recv, r.rx_send, r.rx_recv),
                 (r.sgrad, r.sc_send, r.sc_recv, r.sx_send, r.sx_recv))

        def core_copy(which):
            return remote(
                parts[which][1],
                parts[which][2],
                r.core_send.at[which],
                r.core_recv.at[which],
                at_row(row + 1 - 2 * core),
            )

        def start_core(which):
            grads, out = parts[which][:2]
            for pair in range(pairs):
                out[pair] = grads[block(2 * pair + 1 - core), :].astype(BF16)
            core_copy(which).start()

        def chip_copy(which, step):
            return remote(
                parts[which][3].at[step],
                parts[which][4].at[step],
                r.chip_send.at[which, step],
                r.chip_recv.at[which, step],
                at_row(2 * lax.rem(chip + step, pairs) + core),
            )

        def chan_copy(step):
            return remote(
                r.zs_send.at[step],
                r.zs_recv.at[step],
                r.chan_send.at[step],
                r.chan_recv.at[step],
                at_chan(beside(step)),
            )

        def row_norm(step):
            return remote(
                r.part_rows.at[row],
                r.part_rows.at[row],
                r.rn_send.at[step],
                r.rn_recv.at[step],
                at_row(lax.rem(row + step, group)),
            )

        def chan_norm(step):
            return remote(
                r.part_chans.at[me],
                r.part_chans.at[me],
                r.cn_send.at[step],
                r.cn_recv.at[step],
                at_chan(beside(step)),
            )

    def image(slot, carry):
        for step in range(1, n):
            for copy in in_copies(slot, step):
                copy.wait_recv()
        for copy in own_copies(slot):
            copy.wait()

        def image_rows(first):
            return held[slot, first // cl, pl.ds(pl.multiple_of(first % cl, 16), 16), :]

        columns(image_rows, chans, r.x_cols)
        r.pool_part[slot] = jnp.zeros((chans, cells), BF16)

        def head(here):
            pre = dot(r.w_in[0 : 2 * chans, :], r.x_cols[:, here])
            pick = held[slot, :, cl : 2 * cl, here].reshape(chans, CHUNK).astype(F32)
            value = jnp.where(pick > 0.5, pre[chans:], pre[:chans]).astype(BF16)
            r.out_low[:, here] = value
            cell_win = r.held_pool[slot, :, 0:cl, :].reshape(chans, cells)
            cell_cot = r.held_pool[slot, :, cl : 2 * cl, :].reshape(chans, cells)
            chosen = dot(cell_win, r.up[:, here]) == corner_of(here)
            spread = dot(cell_cot, r.up[:, here])
            r.pool_back[:, here] = jnp.where(chosen, spread, 0.0).astype(BF16)
            kept = jnp.where(chosen, value.astype(F32), 0.0).astype(BF16)
            part = dot_nt(kept, r.up[:, here])
            r.pool_part[slot] = (r.pool_part[slot].astype(F32) + part).astype(BF16)

        chunks(head)
        columns(lambda first: r.out_low[pl.ds(first, 16), :], chans, r.o_cols)

        spot_mask = r.mask[pl.ds(me * slots + slot, 1), :].astype(F32)
        count = jnp.sum(spot_mask, axis=1, keepdims=True)
        scale = HINT_WEIGHT * (pixels / count)

        def hints(here):
            teach = dot(r.w_in[2 * chans :, :], r.x_cols[:, here])
            pick = held[slot, :, 2 * cl :, here].reshape(touts, CHUNK).astype(F32)
            target = jnp.where(pick > 0.5, teach[touts:], teach[:touts])
            guess = dot(r.w_reg[...], r.o_cols[:, here])
            weight = scale * r.mask[pl.ds(me * slots + slot, 1), here].astype(F32)
            r.hint[:, here] = (weight * (guess - target)).astype(BF16)

        chunks(hints)
        columns(lambda first: r.hint[pl.ds(first, 16), :], regs, r.h_cols)
        r.rgrad[...] += dot_nt(r.o_cols[...], r.hint[...])
        if fused:
            pl.when(slot == slots - 1)(lambda: start_core(0))

        def back(here):
            total = dot(r.w_reg_back[...], r.h_cols[:, here]) + r.pool_back[:, here].astype(F32)
            pick = held[slot, :, cl : 2 * cl, here].reshape(chans, CHUNK).astype(F32) > 0.5
            r.pre_grad[0:chans, here] = jnp.where(pick, 0.0, total).astype(BF16)
            r.pre_grad[chans:, here] = jnp.where(pick, total, 0.0).astype(BF16)

        chunks(back)
        columns(lambda first: r.pre_grad[pl.ds(first, 16), :], 2 * chans, r.p_cols)
        r.sgrad[...] += dot_nt(r.x_cols[...], r.pre_grad[...])
        if fused:
            pl.when(slot == slots - 1)(lambda: start_core(1))

        def image_back(here):
            r.low_part[slot, :, here] = dot(r.w_in_back[...], r.p_cols[:, here]).astype(BF16)

        chunks(image_back)
        for step in range(1, n):
            for copy in out_copies(slot, step):
                copy.start()
        for copy in own_out(slot):
            copy.start()
        return carry

    lax.fori_loop(0, slots, image, 0)

    if fused:
        r.whole_grad[...] = jnp.zeros_like(r.whole_grad)
        for which, cols in ((0, slice(2 * chans, 2 * chans + regs)), (1, slice(0, 2 * chans))):
            grads, _, came, out, _ = parts[which]
            core_copy(which).wait_recv()
            for step in range(1, pairs):
                to = lax.rem(chip + step, pairs)
                out[step] = (grads[block(2 * to + core), :] + came[to].astype(F32)).astype(BF16)
                chip_copy(which, step).start()
            r.whole_grad[:, cols] = grads[block(row), :] + came[chip].astype(F32)
        for which, cols in ((0, slice(2 * chans, 2 * chans + regs)), (1, slice(0, 2 * chans))):
            came = parts[which][4]
            for step in range(1, pairs):
                chip_copy(which, step).wait_recv()
            total = r.whole_grad[:, cols]
            for step in range(1, pairs):
                total += came[step].astype(F32)
            r.whole_grad[:, cols] = total
        low_grad = r.whole_grad[...].astype(BF16)
        for step in range(1, n):
            r.zs_send[step] = dot_nt(low_grad, r.spread[beside(step)]).astype(BF16)
            chan_copy(step).start()
        total = dot_nt(
            r.whole_grad[...], r.spread[me].astype(F32), precision=lax.Precision.HIGHEST
        )
        for step in range(1, n):
            chan_copy(step).wait_recv()
        for step in range(1, n):
            total += r.zs_recv[step].astype(F32)
        r.grad_sum[...] = total
        shifted = pltpu.roll(total, LANES - 2 * cl, 1)
        student, regress = r.student_master[...], r.regress_master[...]
        upd_s = lamb_update(student, total[:, 0 : 2 * cl], r.mom_student[...], r.sq_student[...])[2]
        upd_r = lamb_update(regress, shifted[:, 0:rl], r.mom_regress[...], r.sq_regress[...])[2]
        place = lax.broadcasted_iota(jnp.int32, (8, LANES), 1)
        tile = jnp.zeros((8, LANES), F32)
        for index, value in enumerate((student, upd_s, regress, upd_r)):
            square = jnp.sum(jnp.sum(value * value, axis=1, keepdims=True), axis=0, keepdims=True)
            tile = jnp.where(place == index, square, tile)
        r.part_rows[row] = tile
        for step in range(1, group):
            row_norm(step).start()
        for step in range(1, group):
            row_norm(step).wait_recv()
        tile = r.part_rows[0]
        for index in range(1, group):
            tile += r.part_rows[index]
        r.part_chans[me] = tile
        for step in range(1, n):
            chan_norm(step).start()
        for step in range(1, n):
            chan_norm(step).wait_recv()
        tile = r.part_chans[0]
        for index in range(1, n):
            tile += r.part_chans[index]
        r.sums[...] = tile

    def finish(slot, carry):
        for step in range(1, n):
            for copy in in_copies(slot, step):
                copy.wait_send()
            for copy in out_copies(slot, step):
                copy.wait()
        for copy in own_out(slot):
            copy.wait()
        return carry

    lax.fori_loop(0, slots, finish, 0)
    if fused:
        for step in range(1, n):
            filter_z[step - 1].wait_send()
            chan_copy(step).wait_send()
            chan_norm(step).wait_send()
        for step in range(1, group):
            row_norm(step).wait_send()
        for step in range(pairs):
            filter_core(step).wait_send()
        for step in range(1, pairs):
            filter_chip(step).wait_send()
        for which in range(2):
            core_copy(which).wait_send()
            for step in range(1, pairs):
                chip_copy(which, step).wait_send()


def lamb_update(weights, grads, moment, second):
    moment_new = BETA_ONE * moment + (1.0 - BETA_ONE) * grads
    second_new = BETA_TWO * second + (1.0 - BETA_TWO) * grads * grads
    moment_hat = moment_new / (1.0 - BETA_ONE**STEP)
    second_hat = second_new / (1.0 - BETA_TWO**STEP)
    update = moment_hat / (jnp.sqrt(second_hat) + EPSILON) + DECAY * weights
    return (moment_new, second_new, update)


def layer_pass(n, group, fused, arrays):
    cl, batch, pixels = arrays["images"].shape
    tl = arrays["twin"].shape[0]
    cells = arrays["pwin"].shape[2]
    slots = batch // n
    chans = n * cl
    if fused:
        rl = arrays["regress_master"].shape[1]
        depth = arrays["student_master"].shape[0]
    else:
        rl = arrays["w_reg"].shape[0] // n
    regs, touts, pairs = n * rl, n * tl, group // 2
    size = dict(n=n, batch=batch, cl=cl, tl=tl, rl=rl, fused=fused, group=group)
    vmem = pl.BlockSpec(memory_space=pltpu.VMEM)
    in_hbm = ("images", "swin", "twin", "pwin", "cot")
    ins = {
        name: a.reshape(a.shape[0] * a.shape[1], a.shape[2]) if name in in_hbm else a
        for name, a in arrays.items()
    }
    outs = {
        "pool_out": jax.ShapeDtypeStruct((batch, cl, cells), BF16),
        "grad_out": jax.ShapeDtypeStruct((batch, cl, pixels), BF16),
    }
    grads = {"sgrad": (9 * chans, 2 * chans), "rgrad": (9 * chans, regs)}
    dma = lambda *shape: pltpu.SemaphoreType.DMA(shape)
    scratch = {
        "raw": pltpu.VMEM((cl * batch, pixels), BF16),
        "raw_cot": pltpu.VMEM((cl * batch, cells), BF16),
        "wide": pltpu.VMEM((pixels // LANES, cl * batch, LANES), F32),
        "swin_wide": pltpu.VMEM((pixels // LANES, cl * batch, LANES), jnp.int32),
        "twin_wide": pltpu.VMEM((pixels // LANES, tl * batch, LANES), jnp.int32),
        "pwin_wide": pltpu.VMEM((cells // LANES, cl * batch, LANES), jnp.int32),
        "cot_wide": pltpu.VMEM((cells // LANES, cl * batch, LANES), F32),
        "load_sem": dma(2 + 2 * (pixels // LANES) + cells // LANES),
        "send": pltpu.VMEM((slots, n, 2 * cl + tl, pixels), BF16),
        "send_pool": pltpu.VMEM((slots, n, 2 * cl, cells), BF16),
        "held": pltpu.VMEM((slots, n, 2 * cl + tl, pixels), BF16),
        "held_pool": pltpu.VMEM((slots, n, 2 * cl, cells), BF16),
        "low_part": pltpu.VMEM((slots, chans, pixels), BF16),
        "pool_part": pltpu.VMEM((slots, chans, cells), BF16),
        "edge": pltpu.VMEM((4, 16, pixels), BF16),
        "up": pltpu.VMEM((cells, pixels), BF16),
        "x_cols": pltpu.VMEM((9 * chans, pixels), BF16),
        "o_cols": pltpu.VMEM((9 * chans, pixels), BF16),
        "h_cols": pltpu.VMEM((9 * regs, pixels), BF16),
        "p_cols": pltpu.VMEM((9 * 2 * chans, pixels), BF16),
        "out_low": pltpu.VMEM((chans, pixels), BF16),
        "pool_back": pltpu.VMEM((chans, pixels), BF16),
        "hint": pltpu.VMEM((regs, pixels), BF16),
        "pre_grad": pltpu.VMEM((2 * chans, pixels), BF16),
        "own_sem": dma(slots, 2),
        "own_out_sem": dma(slots, 2),
    }
    for name in ("in", "pool_in", "out", "pool_out"):
        scratch[name + "_send"] = dma(slots, n)
        scratch[name + "_recv"] = dma(slots, n)
    if fused:
        cols = 2 * chans + 2 * LANES
        outs["grad_sum"] = jax.ShapeDtypeStruct((depth, LANES), F32)
        outs["sums"] = jax.ShapeDtypeStruct((8, LANES), F32)
        scratch.update({name: pltpu.VMEM(shape, F32) for name, shape in grads.items()})
        scratch.update(
            {
                "filters": pltpu.VMEM((n, 9 * chans, 2 * LANES), BF16),
                "gather_rows": pltpu.VMEM((2 * cl + rl + 2 * tl, 2 * LANES), BF16),
                "spread": pltpu.VMEM((n, LANES, cols), BF16),
                "w_in": pltpu.VMEM((2 * chans + 2 * touts, 9 * chans), BF16),
                "w_reg": pltpu.VMEM((regs, 9 * chans), BF16),
                "w_reg_back": pltpu.VMEM((chans, 9 * regs), BF16),
                "w_in_back": pltpu.VMEM((chans, 9 * 2 * chans), BF16),
                "rc_send": pltpu.VMEM((pairs, depth, regs), BF16),
                "rc_recv": pltpu.VMEM((pairs, depth, regs), BF16),
                "rx_send": pltpu.VMEM((pairs, depth, regs), BF16),
                "rx_recv": pltpu.VMEM((pairs, depth, regs), BF16),
                "sc_send": pltpu.VMEM((pairs, depth, 2 * chans), BF16),
                "sc_recv": pltpu.VMEM((pairs, depth, 2 * chans), BF16),
                "sx_send": pltpu.VMEM((pairs, depth, 2 * chans), BF16),
                "sx_recv": pltpu.VMEM((pairs, depth, 2 * chans), BF16),
                "whole_grad": pltpu.VMEM((depth, cols), F32),
                "zs_send": pltpu.VMEM((n, depth, LANES), BF16),
                "zs_recv": pltpu.VMEM((n, depth, LANES), BF16),
                "part_rows": pltpu.VMEM((group, 8, LANES), F32),
                "part_chans": pltpu.VMEM((n, 8, LANES), F32),
                "core_send": dma(2),
                "core_recv": dma(2),
                "chip_send": dma(2, pairs),
                "chip_recv": dma(2, pairs),
            }
        )
        for name, many in (
            ("fz", n), ("fx", pairs), ("fc", pairs), ("chan", n), ("rn", group), ("cn", n)
        ):
            scratch[name + "_send"] = dma(many)
            scratch[name + "_recv"] = dma(many)
    else:
        outs.update({name: jax.ShapeDtypeStruct(shape, F32) for name, shape in grads.items()})
    flops = 2 * slots * pixels * 9 * chans * (3 * 2 * chans + 2 * touts + 3 * regs)
    names = tuple(ins) + tuple(outs) + tuple(scratch)
    return pl.pallas_call(
        functools.partial(layer_kernel, size, names),
        out_shape=list(outs.values()),
        in_specs=[
            pl.BlockSpec(memory_space=pl.ANY) if name in in_hbm else vmem for name in ins
        ],
        out_specs=[vmem] * len(outs),
        scratch_shapes=list(scratch.values()),
        compiler_params=pltpu.CompilerParams(
            collective_id=0, has_side_effects=True, vmem_limit_bytes=58 << 20
        ),
        cost_estimate=pl.CostEstimate(flops=flops, bytes_accessed=16 << 20, transcendentals=0),
        name="layer",
    )(*ins.values())


def split_pieces(weights):
    rows, cols = weights.shape
    return weights.reshape(rows, cols // 2, 2).transpose(2, 1, 0).reshape(cols, rows)


def back_weights(weights, outs):
    channels = weights.shape[0] // 9
    taps = weights.reshape(9, channels, outs)[::-1]
    return taps.transpose(1, 0, 2).reshape(channels, 9 * outs)


def gathered_filters(student_master, regress_master, teacher_weight):
    student_full = lax.all_gather(student_master.astype(BF16), "dp", axis=0, tiled=True)
    student_full = lax.all_gather(student_full, "chan", axis=1, tiled=True)
    regress_full = lax.all_gather(regress_master.astype(BF16), "dp", axis=0, tiled=True)
    regress_full = lax.all_gather(regress_full, "chan", axis=1, tiled=True)
    teacher_full = lax.all_gather(teacher_weight, "chan", axis=1, tiled=True)
    student_rows = split_pieces(student_full)
    return {
        "w_in": jnp.concatenate([student_rows, split_pieces(teacher_full)], axis=0),
        "w_reg": regress_full.T,
        "w_reg_back": back_weights(regress_full, regress_full.shape[1]),
        "w_in_back": back_weights(student_rows.T, student_full.shape[1]),
    }


def scattered_grads(student_part, regress_part):
    souts = student_part.shape[1]
    student_part = student_part.reshape(-1, 2, souts // 2).transpose(0, 2, 1).reshape(-1, souts)
    student_grad = lax.psum_scatter(student_part, "dp", scatter_dimension=0, tiled=True)
    student_grad = lax.psum_scatter(student_grad, "chan", scatter_dimension=1, tiled=True)
    regress_grad = lax.psum_scatter(regress_part, "dp", scatter_dimension=0, tiled=True)
    regress_grad = lax.psum_scatter(regress_grad, "chan", scatter_dimension=1, tiled=True)
    return student_grad, regress_grad


def on_device(
    n,
    group,
    images,
    student_master,
    regress_master,
    teacher_weight,
    student_win,
    teacher_win,
    pool_win,
    hint_mask,
    cotangent,
    mom_student,
    sq_student,
    ema_student,
    mom_regress,
    sq_regress,
    ema_regress,
):
    depth = student_master.shape[0]
    fused = group % 2 == 0 and depth % 16 == 0
    arrays = dict(
        images=images,
        swin=student_win,
        twin=teacher_win,
        pwin=pool_win,
        cot=cotangent,
        mask=hint_mask,
    )
    if fused:
        arrays.update(
            student_master=student_master,
            regress_master=regress_master,
            teacher=teacher_weight,
            mom_student=mom_student,
            sq_student=sq_student,
            mom_regress=mom_regress,
            sq_regress=sq_regress,
        )
        pooled, image_grad, grad_sum, sums = layer_pass(n, group, fused, arrays)
        souts, regs = student_master.shape[1], regress_master.shape[1]
        student_grad = grad_sum[:, 0:souts]
        regress_grad = grad_sum[:, souts : souts + regs]
    else:
        arrays.update(gathered_filters(student_master, regress_master, teacher_weight))
        pooled, image_grad, student_part, regress_part = layer_pass(n, group, fused, arrays)
        student_grad, regress_grad = scattered_grads(student_part, regress_part)
    mom_s, sq_s, upd_s = lamb_update(student_master, student_grad, mom_student, sq_student)
    mom_r, sq_r, upd_r = lamb_update(regress_master, regress_grad, mom_regress, sq_regress)
    if fused:
        all_sums = sums[0, 0:4]
    else:
        all_sums = lax.psum(
            jnp.stack(
                [jnp.sum(v * v) for v in (student_master, upd_s, regress_master, upd_r)]
            ),
            ("dp", "chan"),
        )
    norms = jnp.sqrt(all_sums)
    new_student = student_master - LEARN_RATE * (norms[0] / norms[1]) * upd_s
    new_regress = regress_master - LEARN_RATE * (norms[2] / norms[3]) * upd_r
    ema_s = EMA_KEEP * ema_student + (1.0 - EMA_KEEP) * new_student
    ema_r = EMA_KEEP * ema_regress + (1.0 - EMA_KEEP) * new_regress
    return (
        pooled.transpose(1, 0, 2),
        image_grad.transpose(1, 0, 2),
        new_student,
        mom_s,
        sq_s,
        ema_s,
        new_student.astype(BF16),
        new_regress,
        mom_r,
        sq_r,
        ema_r,
        new_regress.astype(BF16),
        norms.reshape(2, 2),
    )


def solution(mesh):
    acts = P("chan", "dp", None)
    rows = P("dp", "chan")
    in_specs = (
        (acts, rows, rows, P(None, "chan"))
        + (acts, acts, acts, P("dp", None), acts)
        + (rows,) * 6
    )
    out_specs = (acts, acts) + (rows,) * 10 + (P(),)
    return jax.shard_map(
        functools.partial(on_device, mesh.shape["chan"], mesh.shape["dp"]),
        mesh=mesh,
        in_specs=in_specs,
        out_specs=out_specs,
        check_vma=False,
    )
```

```python
import functools
import types

import jax
import jax.numpy as jnp
from jax import lax
from jax.experimental import pallas as pl
from jax.experimental.pallas import tpu as pltpu
from jax.sharding import PartitionSpec as P

IMG = 32
STEP = 10
HINT_WEIGHT = 0.1
LEARN_RATE = 0.5
BETA_ONE = 0.9
BETA_TWO = 0.999
EPSILON = 1e-06
DECAY = 0.01
EMA_KEEP = 0.75

MESH = pl.DeviceIdType.MESH
F32 = jnp.float32
BF16 = jnp.bfloat16
CHUNK = 256
LANES = 128


def dot(left, right):
    return jnp.dot(left, right, preferred_element_type=F32)


def dot_nt(left, right, precision=None):
    return lax.dot_general(
        left, right, (((1,), (1,)), ((), ())), precision=precision, preferred_element_type=F32
    )


def one_hot(shape, target, axis):
    at = lax.broadcasted_iota(jnp.int32, shape, axis)
    return jnp.where(at == target, 1.0, 0.0).astype(BF16)


def layer_kernel(size, names, *refs):
    r = types.SimpleNamespace(**dict(zip(names, refs)))
    n, batch, cl, tl, rl = size["n"], size["batch"], size["cl"], size["tl"], size["rl"]
    fused, group = size["fused"], size["group"]
    slots = batch // n
    chans, touts, regs = n * cl, n * tl, n * rl
    pixels = IMG * IMG
    cells = pixels // 4
    me = lax.axis_index("chan")
    row = lax.axis_index("dp")
    core, chip, pairs = row % 2, row // 2, group // 2
    held, send = r.held, r.send

    def beside(step):
        return lax.rem(me + step, n)

    def at_chan(index):
        return {"chan": index}

    def at_row(index):
        return {"dp": index}

    def remote(src, dst, out_sem, in_sem, device):
        return pltpu.make_async_remote_copy(
            src, dst, out_sem, in_sem, device_id=device, device_id_type=MESH
        )

    greeted = [at_chan(beside(step)) for step in range(1, n)]
    if fused:
        greeted += [at_row(lax.rem(row + step, group)) for step in range(1, group)]

    loads = [
        pltpu.make_async_copy(r.images, r.raw, r.load_sem.at[0]),
        pltpu.make_async_copy(r.cot, r.raw_cot, r.load_sem.at[1]),
    ]
    for src, dst in ((r.swin, r.swin_wide), (r.twin, r.twin_wide), (r.pwin, r.pwin_wide)):
        for j in range(dst.shape[0]):
            loads.append(
                pltpu.make_async_copy(
                    src.at[:, pl.ds(j * LANES, LANES)], dst.at[j], r.load_sem.at[len(loads)]
                )
            )
    for copy in loads:
        copy.start()

    barrier = pltpu.get_barrier_semaphore()
    for device in greeted:
        pl.semaphore_signal(barrier, inc=1, device_id=device, device_id_type=MESH)

    if fused:
        depth = r.student_t.shape[1]

        def block(index):
            return pl.ds(pl.multiple_of(index * depth, 16), depth)

        mine = block(row)
        r.flat[...] = jnp.zeros_like(r.flat)
        r.flat[0 : 2 * cl, 0:depth] = r.student_t[...]
        r.flat[2 * cl : 2 * cl + rl, 0:depth] = r.regress_t[...]
        r.filters[me, mine, 0:LANES] = r.flat[...].T[0:depth, :].astype(BF16)
        r.teach_flat[...] = jnp.zeros_like(r.teach_flat)
        r.teach_flat[0 : 2 * tl, :] = r.teacher_t[...].astype(F32)
        r.teach_cols[...] = r.teach_flat[...].T
        r.filters[me, mine, LANES:] = r.teach_cols[mine, :].astype(BF16)

    pl.semaphore_wait(barrier, len(greeted))

    if fused:
        filter_z = [
            remote(
                r.filters.at[me, mine],
                r.filters.at[me, mine],
                r.fz_send.at[step],
                r.fz_recv.at[step],
                at_chan(beside(step)),
            )
            for step in range(1, n)
        ]
        for copy in filter_z:
            copy.start()

    for copy in loads:
        copy.wait()
    for j in range(r.wide.shape[0]):
        r.wide[j] = r.raw[:, j * LANES : (j + 1) * LANES].astype(F32)
    for j in range(r.cot_wide.shape[0]):
        r.cot_wide[j] = r.raw_cot[:, j * LANES : (j + 1) * LANES].astype(F32)

    def in_copies(slot, step):
        to = beside(step)
        return (
            remote(
                send.at[slot, to],
                held.at[slot, me],
                r.in_send.at[slot, step],
                r.in_recv.at[slot, step],
                at_chan(to),
            ),
            remote(
                r.send_pool.at[slot, to],
                r.held_pool.at[slot, me],
                r.pool_in_send.at[slot, step],
                r.pool_in_recv.at[slot, step],
                at_chan(to),
            ),
        )

    def own_copies(slot):
        return (
            pltpu.make_async_copy(send.at[slot, me], held.at[slot, me], r.own_sem.at[slot, 0]),
            pltpu.make_async_copy(
                r.send_pool.at[slot, me], r.held_pool.at[slot, me], r.own_sem.at[slot, 1]
            ),
        )

    def lanes_of(index):
        return pl.ds(pl.multiple_of(index * cl, cl), cl)

    def out_copies(slot, step):
        to = beside(step)
        return (
            remote(
                r.low_part.at[slot, lanes_of(to)],
                r.grad_out.at[me * slots + slot],
                r.out_send.at[slot, step],
                r.out_recv.at[slot, step],
                at_chan(to),
            ),
            remote(
                r.pool_part.at[slot, lanes_of(to)],
                r.pool_out.at[me * slots + slot],
                r.pool_out_send.at[slot, step],
                r.pool_out_recv.at[slot, step],
                at_chan(to),
            ),
        )

    def own_out(slot):
        here = me * slots + slot
        return (
            pltpu.make_async_copy(
                r.low_part.at[slot, lanes_of(me)], r.grad_out.at[here], r.own_out_sem.at[slot, 0]
            ),
            pltpu.make_async_copy(
                r.pool_part.at[slot, lanes_of(me)], r.pool_out.at[here], r.own_out_sem.at[slot, 1]
            ),
        )

    def start_out(slot):
        for step in range(1, n):
            for copy in out_copies(slot, step):
                copy.start()

    def start_early():
        for slot in range(slots - 1):
            start_out(slot)

    def prepare(slot, carry):
        for to in range(n):
            first_row = to * slots + slot
            for src, dst, first, rows in (
                (r.wide, send, 0, cl),
                (r.swin_wide, send, cl, cl),
                (r.twin_wide, send, 2 * cl, tl),
                (r.pwin_wide, r.send_pool, 0, cl),
                (r.cot_wide, r.send_pool, cl, cl),
            ):
                for j in range(src.shape[0]):
                    dst[slot, to, first : first + rows, j * LANES : (j + 1) * LANES] = (
                        src[j, pl.ds(first_row, rows, stride=batch), :].astype(F32).astype(BF16)
                    )
        for step in range(1, n):
            for copy in in_copies(slot, step):
                copy.start()
        for copy in own_copies(slot):
            copy.start()
        return carry

    lax.fori_loop(0, slots, prepare, 0)

    lane = lax.broadcasted_iota(jnp.int32, (16, pixels), 1)
    row_of, col_of = lane // IMG, lane % IMG
    for which, bad in enumerate((row_of == 0, row_of == IMG - 1, col_of == 0, col_of == IMG - 1)):
        r.edge[which] = jnp.where(bad, 0.0, 1.0).astype(BF16)
    spot = lax.broadcasted_iota(jnp.int32, (1, pixels), 1)
    home = (spot // (2 * IMG)) * (IMG // 2) + (spot % IMG) // 2
    r.up[...] = one_hot((cells, pixels), home, 0)
    r.sgrad[...] = jnp.zeros_like(r.sgrad)
    r.rgrad[...] = jnp.zeros_like(r.rgrad)

    if fused:
        picked = 2 * cl + rl + 2 * tl
        at = lax.broadcasted_iota(jnp.int32, (picked, 1), 0)
        teach = at - 2 * cl - rl
        lane_at = jnp.where(
            at < 2 * cl,
            2 * (at % cl) + at // cl,
            jnp.where(at < 2 * cl + rl, at, LANES + 2 * (teach % tl) + teach // tl),
        )
        r.gather_rows[...] = one_hot((picked, r.filters.shape[2]), lane_at, 1)
        for z in range(n):
            at = lax.broadcasted_iota(jnp.int32, (LANES, 1), 0)
            col_at = jnp.where(
                at < 2 * cl,
                (at % 2) * chans + z * cl + at // 2,
                jnp.where(at < 2 * cl + rl, 2 * chans + z * rl + at - 2 * cl, -1),
            )
            r.spread[z] = one_hot((LANES, r.spread.shape[2]), col_at, 1)

        for copy in filter_z:
            copy.wait_recv()

        def filter_chip(step):
            to = lax.rem(chip + step, pairs)
            return remote(
                r.filters.at[:, mine],
                r.filters.at[:, mine],
                r.fx_send.at[step],
                r.fx_recv.at[step],
                at_row(2 * to + core),
            )

        def filter_core(step):
            rows = block(2 * lax.rem(chip + pairs - step, pairs) + core)
            return remote(
                r.filters.at[:, rows],
                r.filters.at[:, rows],
                r.fc_send.at[step],
                r.fc_recv.at[step],
                at_row(row + 1 - 2 * core),
            )

        for step in range(1, pairs):
            filter_chip(step).start()
        filter_core(0).start()
        for step in range(1, pairs):
            filter_chip(step).wait_recv()
            filter_core(step).start()
        for step in range(pairs):
            filter_core(step).wait_recv()

        for z in range(n):
            rows_of = dot_nt(r.gather_rows[...], r.filters[z]).astype(BF16)
            first = 0
            for dst, start, many in (
                (r.w_in, z * cl, cl),
                (r.w_in, chans + z * cl, cl),
                (r.w_reg, z * rl, rl),
                (r.w_in, 2 * chans + z * tl, tl),
                (r.w_in, 2 * chans + touts + z * tl, tl),
            ):
                dst[start : start + many, :] = rows_of[first : first + many, :]
                first += many
        for tap in range(9):
            rows = slice((8 - tap) * chans, (9 - tap) * chans)
            total = dot(r.filters[0, rows, 0:LANES], r.spread[0])
            for z in range(1, n):
                total += dot(r.filters[z, rows, 0:LANES], r.spread[z])
            total = total.astype(BF16)
            r.w_in_back[:, tap * 2 * chans : (tap + 1) * 2 * chans] = total[:, 0 : 2 * chans]
            r.w_reg_back[:, tap * regs : (tap + 1) * regs] = total[:, 2 * chans : 2 * chans + regs]

    def columns(load, rows, dst):
        def group(g, carry):
            first = pl.multiple_of(g * 16, 16)
            base = load(first)
            for ky in range(3):
                if ky == 1:
                    moved = base
                else:
                    moved = pltpu.roll(base, (pixels - IMG * (ky - 1)) % pixels, 1)
                    moved = moved * r.edge[0 if ky == 0 else 1]
                for kx in range(3):
                    if kx == 1:
                        tap = moved
                    else:
                        tap = pltpu.roll(moved, (pixels - (kx - 1)) % pixels, 1)
                        tap = tap * r.edge[2 if kx == 0 else 3]
                    dst[pl.ds((3 * ky + kx) * rows + first, 16), :] = tap
            return carry

        lax.fori_loop(0, rows // 16, group, 0, unroll=2)

    def chunks(body):
        def one(c, carry):
            body(pl.ds(pl.multiple_of(c * CHUNK, CHUNK), CHUNK))
            return carry

        lax.fori_loop(0, pixels // CHUNK, one, 0)

    def corner_of(here):
        at = lax.broadcasted_iota(jnp.int32, (1, CHUNK), 1)
        return (2 * ((at // IMG) % 2) + at % 2).astype(F32)

    if fused:
        parts = ((r.rgrad, r.rc_send, r.rc_recv, r.rx_send, r.rx_recv),
                 (r.sgrad, r.sc_send, r.sc_recv, r.sx_send, r.sx_recv))

        def core_copy(which):
            return remote(
                parts[which][1],
                parts[which][2],
                r.core_send.at[which],
                r.core_recv.at[which],
                at_row(row + 1 - 2 * core),
            )

        def start_core(which):
            grads, out = parts[which][:2]
            for pair in range(pairs):
                out[pair] = grads[block(2 * pair + 1 - core), :].astype(BF16)
            core_copy(which).start()

        def chip_copy(which, step):
            return remote(
                parts[which][3].at[step],
                parts[which][4].at[step],
                r.chip_send.at[which, step],
                r.chip_recv.at[which, step],
                at_row(2 * lax.rem(chip + step, pairs) + core),
            )

        def chan_copy(step):
            return remote(
                r.zs_send.at[step],
                r.zs_recv.at[step],
                r.chan_send.at[step],
                r.chan_recv.at[step],
                at_chan(beside(step)),
            )

        def row_norm(step):
            return remote(
                r.part_rows.at[row],
                r.part_rows.at[row],
                r.rn_send.at[step],
                r.rn_recv.at[step],
                at_row(lax.rem(row + step, group)),
            )

        def chan_norm(step):
            return remote(
                r.part_chans.at[me],
                r.part_chans.at[me],
                r.cn_send.at[step],
                r.cn_recv.at[step],
                at_chan(beside(step)),
            )

    def image(slot, carry):
        for step in range(1, n):
            for copy in in_copies(slot, step):
                copy.wait_recv()
        for copy in own_copies(slot):
            copy.wait()
        pl.when(slot == slots - 1)(start_early)

        def image_rows(first):
            return held[slot, first // cl, pl.ds(pl.multiple_of(first % cl, 16), 16), :]

        columns(image_rows, chans, r.x_cols)
        r.pool_part[slot] = jnp.zeros((chans, cells), BF16)

        def head(here):
            pre = dot(r.w_in[0 : 2 * chans, :], r.x_cols[:, here])
            pick = held[slot, :, cl : 2 * cl, here].reshape(chans, CHUNK).astype(F32)
            value = jnp.where(pick > 0.5, pre[chans:], pre[:chans]).astype(BF16)
            r.out_low[:, here] = value
            cell_win = r.held_pool[slot, :, 0:cl, :].reshape(chans, cells)
            cell_cot = r.held_pool[slot, :, cl : 2 * cl, :].reshape(chans, cells)
            chosen = dot(cell_win, r.up[:, here]) == corner_of(here)
            spread = dot(cell_cot, r.up[:, here])
            r.pool_back[:, here] = jnp.where(chosen, spread, 0.0).astype(BF16)
            kept = jnp.where(chosen, value.astype(F32), 0.0).astype(BF16)
            part = dot_nt(kept, r.up[:, here])
            r.pool_part[slot] = (r.pool_part[slot].astype(F32) + part).astype(BF16)

        chunks(head)
        columns(lambda first: r.out_low[pl.ds(first, 16), :], chans, r.o_cols)

        spot_mask = r.mask[pl.ds(me * slots + slot, 1), :].astype(F32)
        count = jnp.sum(spot_mask, axis=1, keepdims=True)
        scale = HINT_WEIGHT * (pixels / count)

        def hints(here):
            teach = dot(r.w_in[2 * chans :, :], r.x_cols[:, here])
            pick = held[slot, :, 2 * cl :, here].reshape(touts, CHUNK).astype(F32)
            target = jnp.where(pick > 0.5, teach[touts:], teach[:touts])
            guess = dot(r.w_reg[...], r.o_cols[:, here])
            weight = scale * r.mask[pl.ds(me * slots + slot, 1), here].astype(F32)
            r.hint[:, here] = (weight * (guess - target)).astype(BF16)

        chunks(hints)
        columns(lambda first: r.hint[pl.ds(first, 16), :], regs, r.h_cols)
        r.rgrad[...] += dot_nt(r.o_cols[...], r.hint[...])
        if fused:
            pl.when(slot == slots - 1)(lambda: start_core(0))

        def back(here):
            total = dot(r.w_reg_back[...], r.h_cols[:, here]) + r.pool_back[:, here].astype(F32)
            pick = held[slot, :, cl : 2 * cl, here].reshape(chans, CHUNK).astype(F32) > 0.5
            r.pre_grad[0:chans, here] = jnp.where(pick, 0.0, total).astype(BF16)
            r.pre_grad[chans:, here] = jnp.where(pick, total, 0.0).astype(BF16)

        chunks(back)
        columns(lambda first: r.pre_grad[pl.ds(first, 16), :], 2 * chans, r.p_cols)
        r.sgrad[...] += dot_nt(r.x_cols[...], r.pre_grad[...])
        if fused:
            pl.when(slot == slots - 1)(lambda: start_core(1))

        def image_back(here):
            r.low_part[slot, :, here] = dot(r.w_in_back[...], r.p_cols[:, here]).astype(BF16)

        chunks(image_back)
        pl.when(slot == slots - 1)(lambda: start_out(slots - 1))
        for copy in own_out(slot):
            copy.start()
        return carry

    lax.fori_loop(0, slots, image, 0)

    if fused:
        r.whole_grad[...] = jnp.zeros_like(r.whole_grad)
        for which, cols in ((0, slice(2 * chans, 2 * chans + regs)), (1, slice(0, 2 * chans))):
            grads, _, came, out, _ = parts[which]
            core_copy(which).wait_recv()
            for step in range(1, pairs):
                to = lax.rem(chip + step, pairs)
                out[step] = (grads[block(2 * to + core), :] + came[to].astype(F32)).astype(BF16)
                chip_copy(which, step).start()
            r.whole_grad[:, cols] = grads[block(row), :] + came[chip].astype(F32)
        for which, cols in ((0, slice(2 * chans, 2 * chans + regs)), (1, slice(0, 2 * chans))):
            came = parts[which][4]
            for step in range(1, pairs):
                chip_copy(which, step).wait_recv()
            total = r.whole_grad[:, cols]
            for step in range(1, pairs):
                total += came[step].astype(F32)
            r.whole_grad[:, cols] = total
        low_grad = r.whole_grad[...].astype(BF16)
        for step in range(1, n):
            r.zs_send[step] = dot_nt(low_grad, r.spread[beside(step)]).astype(BF16)
            chan_copy(step).start()
        total = dot_nt(
            r.whole_grad[...], r.spread[me].astype(F32), precision=lax.Precision.HIGHEST
        )
        for step in range(1, n):
            chan_copy(step).wait_recv()
        for step in range(1, n):
            total += r.zs_recv[step].astype(F32)
        r.tall[0:depth, :] = total
        total = r.tall[...].T[:, 0:depth]
        r.grad_sum[...] = total
        student, regress = r.student_t[...], r.regress_t[...]
        upd_s = lamb_update(student, total[0 : 2 * cl], r.mom_student[...], r.sq_student[...])[2]
        upd_r = lamb_update(
            regress, total[2 * cl : 2 * cl + rl], r.mom_regress[...], r.sq_regress[...]
        )[2]
        place = lax.broadcasted_iota(jnp.int32, (8, LANES), 1)
        tile = jnp.zeros((8, LANES), F32)
        for index, value in enumerate((student, upd_s, regress, upd_r)):
            square = jnp.sum(jnp.sum(value * value, axis=1, keepdims=True), axis=0, keepdims=True)
            tile = jnp.where(place == index, square, tile)
        r.part_rows[row] = tile
        for step in range(1, group):
            row_norm(step).start()
        for step in range(1, group):
            row_norm(step).wait_recv()
        tile = r.part_rows[0]
        for index in range(1, group):
            tile += r.part_rows[index]
        r.part_chans[me] = tile
        for step in range(1, n):
            chan_norm(step).start()
        for step in range(1, n):
            chan_norm(step).wait_recv()
        tile = r.part_chans[0]
        for index in range(1, n):
            tile += r.part_chans[index]
        r.sums[...] = tile

    def finish(slot, carry):
        for step in range(1, n):
            for copy in in_copies(slot, step):
                copy.wait_send()
            for copy in out_copies(slot, step):
                copy.wait()
        for copy in own_out(slot):
            copy.wait()
        return carry

    lax.fori_loop(0, slots, finish, 0)
    if fused:
        for step in range(1, n):
            filter_z[step - 1].wait_send()
            chan_copy(step).wait_send()
            chan_norm(step).wait_send()
        for step in range(1, group):
            row_norm(step).wait_send()
        for step in range(pairs):
            filter_core(step).wait_send()
        for step in range(1, pairs):
            filter_chip(step).wait_send()
        for which in range(2):
            core_copy(which).wait_send()
            for step in range(1, pairs):
                chip_copy(which, step).wait_send()


def lamb_update(weights, grads, moment, second):
    moment_new = BETA_ONE * moment + (1.0 - BETA_ONE) * grads
    second_new = BETA_TWO * second + (1.0 - BETA_TWO) * grads * grads
    moment_hat = moment_new / (1.0 - BETA_ONE**STEP)
    second_hat = second_new / (1.0 - BETA_TWO**STEP)
    update = moment_hat / (jnp.sqrt(second_hat) + EPSILON) + DECAY * weights
    return (moment_new, second_new, update)


def layer_pass(n, group, fused, arrays):
    cl, batch, pixels = arrays["images"].shape
    tl = arrays["twin"].shape[0]
    cells = arrays["pwin"].shape[2]
    slots = batch // n
    chans = n * cl
    if fused:
        rl, depth = arrays["regress_t"].shape
    else:
        rl = arrays["w_reg"].shape[0] // n
    regs, touts, pairs = n * rl, n * tl, group // 2
    size = dict(n=n, batch=batch, cl=cl, tl=tl, rl=rl, fused=fused, group=group)
    vmem = pl.BlockSpec(memory_space=pltpu.VMEM)
    in_hbm = ("images", "swin", "twin", "pwin", "cot")
    ins = {
        name: a.reshape(a.shape[0] * a.shape[1], a.shape[2]) if name in in_hbm else a
        for name, a in arrays.items()
    }
    outs = {
        "pool_out": jax.ShapeDtypeStruct((batch, cl, cells), BF16),
        "grad_out": jax.ShapeDtypeStruct((batch, cl, pixels), BF16),
    }
    grads = {"sgrad": (9 * chans, 2 * chans), "rgrad": (9 * chans, regs)}
    dma = lambda *shape: pltpu.SemaphoreType.DMA(shape)
    scratch = {
        "raw": pltpu.VMEM((cl * batch, pixels), BF16),
        "raw_cot": pltpu.VMEM((cl * batch, cells), BF16),
        "wide": pltpu.VMEM((pixels // LANES, cl * batch, LANES), F32),
        "swin_wide": pltpu.VMEM((pixels // LANES, cl * batch, LANES), jnp.int32),
        "twin_wide": pltpu.VMEM((pixels // LANES, tl * batch, LANES), jnp.int32),
        "pwin_wide": pltpu.VMEM((cells // LANES, cl * batch, LANES), jnp.int32),
        "cot_wide": pltpu.VMEM((cells // LANES, cl * batch, LANES), F32),
        "load_sem": dma(2 + 2 * (pixels // LANES) + cells // LANES),
        "send": pltpu.VMEM((slots, n, 2 * cl + tl, pixels), BF16),
        "send_pool": pltpu.VMEM((slots, n, 2 * cl, cells), BF16),
        "held": pltpu.VMEM((slots, n, 2 * cl + tl, pixels), BF16),
        "held_pool": pltpu.VMEM((slots, n, 2 * cl, cells), BF16),
        "low_part": pltpu.VMEM((slots, chans, pixels), BF16),
        "pool_part": pltpu.VMEM((slots, chans, cells), BF16),
        "edge": pltpu.VMEM((4, 16, pixels), BF16),
        "up": pltpu.VMEM((cells, pixels), BF16),
        "x_cols": pltpu.VMEM((9 * chans, pixels), BF16),
        "o_cols": pltpu.VMEM((9 * chans, pixels), BF16),
        "h_cols": pltpu.VMEM((9 * regs, pixels), BF16),
        "p_cols": pltpu.VMEM((9 * 2 * chans, pixels), BF16),
        "out_low": pltpu.VMEM((chans, pixels), BF16),
        "pool_back": pltpu.VMEM((chans, pixels), BF16),
        "hint": pltpu.VMEM((regs, pixels), BF16),
        "pre_grad": pltpu.VMEM((2 * chans, pixels), BF16),
        "own_sem": dma(slots, 2),
        "own_out_sem": dma(slots, 2),
    }
    for name in ("in", "pool_in", "out", "pool_out"):
        scratch[name + "_send"] = dma(slots, n)
        scratch[name + "_recv"] = dma(slots, n)
    if fused:
        cols = 2 * chans + 2 * LANES
        tall = -(-depth // LANES) * LANES
        outs["grad_sum"] = jax.ShapeDtypeStruct((LANES, depth), F32)
        outs["sums"] = jax.ShapeDtypeStruct((8, LANES), F32)
        scratch.update({name: pltpu.VMEM(shape, F32) for name, shape in grads.items()})
        scratch.update(
            {
                "flat": pltpu.VMEM((LANES, tall), F32),
                "tall": pltpu.VMEM((tall, LANES), F32),
                "teach_flat": pltpu.VMEM((LANES, 9 * chans), F32),
                "teach_cols": pltpu.VMEM((9 * chans, LANES), F32),
                "filters": pltpu.VMEM((n, 9 * chans, 2 * LANES), BF16),
                "gather_rows": pltpu.VMEM((2 * cl + rl + 2 * tl, 2 * LANES), BF16),
                "spread": pltpu.VMEM((n, LANES, cols), BF16),
                "w_in": pltpu.VMEM((2 * chans + 2 * touts, 9 * chans), BF16),
                "w_reg": pltpu.VMEM((regs, 9 * chans), BF16),
                "w_reg_back": pltpu.VMEM((chans, 9 * regs), BF16),
                "w_in_back": pltpu.VMEM((chans, 9 * 2 * chans), BF16),
                "rc_send": pltpu.VMEM((pairs, depth, regs), BF16),
                "rc_recv": pltpu.VMEM((pairs, depth, regs), BF16),
                "rx_send": pltpu.VMEM((pairs, depth, regs), BF16),
                "rx_recv": pltpu.VMEM((pairs, depth, regs), BF16),
                "sc_send": pltpu.VMEM((pairs, depth, 2 * chans), BF16),
                "sc_recv": pltpu.VMEM((pairs, depth, 2 * chans), BF16),
                "sx_send": pltpu.VMEM((pairs, depth, 2 * chans), BF16),
                "sx_recv": pltpu.VMEM((pairs, depth, 2 * chans), BF16),
                "whole_grad": pltpu.VMEM((depth, cols), F32),
                "zs_send": pltpu.VMEM((n, depth, LANES), BF16),
                "zs_recv": pltpu.VMEM((n, depth, LANES), BF16),
                "part_rows": pltpu.VMEM((group, 8, LANES), F32),
                "part_chans": pltpu.VMEM((n, 8, LANES), F32),
                "core_send": dma(2),
                "core_recv": dma(2),
                "chip_send": dma(2, pairs),
                "chip_recv": dma(2, pairs),
            }
        )
        for name, many in (
            ("fz", n), ("fx", pairs), ("fc", pairs), ("chan", n), ("rn", group), ("cn", n)
        ):
            scratch[name + "_send"] = dma(many)
            scratch[name + "_recv"] = dma(many)
    else:
        outs.update({name: jax.ShapeDtypeStruct(shape, F32) for name, shape in grads.items()})
    flops = 2 * slots * pixels * 9 * chans * (3 * 2 * chans + 2 * touts + 3 * regs)
    names = tuple(ins) + tuple(outs) + tuple(scratch)
    return pl.pallas_call(
        functools.partial(layer_kernel, size, names),
        out_shape=list(outs.values()),
        in_specs=[
            pl.BlockSpec(memory_space=pl.ANY) if name in in_hbm else vmem for name in ins
        ],
        out_specs=[vmem] * len(outs),
        scratch_shapes=list(scratch.values()),
        compiler_params=pltpu.CompilerParams(
            collective_id=0, has_side_effects=True, vmem_limit_bytes=58 << 20
        ),
        cost_estimate=pl.CostEstimate(flops=flops, bytes_accessed=16 << 20, transcendentals=0),
        name="layer",
    )(*ins.values())


def final_kernel(batch, *refs):
    wide, came_sem = refs[-2:]
    came = []
    for index, (src, dst) in enumerate(zip(refs[0:4], refs[-6:-2])):
        came.append(pltpu.make_async_copy(src, dst, came_sem.at[index]))
        came[-1].start()
    pool_in, grad_in, grad_sum, sums = refs[-6:-2]
    student, regress, mom_s, sq_s, mom_r, sq_r, ema_s, ema_r = refs[4:12]
    pooled, image_grad, new_s, new_r, trust = refs[12], refs[13], refs[14:19], refs[19:24], refs[24]
    came[2].wait()
    came[3].wait()
    norm = [jnp.sqrt(sums[0:1, k : k + 1]) for k in range(4)]
    souts, regs = student.shape[0], regress.shape[0]
    for weights, grads, moment, second, average, outs, top, bottom in (
        (student, grad_sum[0:souts, :], mom_s, sq_s, ema_s, new_s, norm[0], norm[1]),
        (regress, grad_sum[souts : souts + regs, :], mom_r, sq_r, ema_r, new_r, norm[2], norm[3]),
    ):
        moment_new, second_new, update = lamb_update(
            weights[...], grads, moment[...], second[...]
        )
        new = weights[...] - LEARN_RATE * (top / bottom) * update
        outs[0][...] = new
        outs[1][...] = moment_new
        outs[2][...] = second_new
        outs[3][...] = EMA_KEEP * average[...] + (1.0 - EMA_KEEP) * new
        outs[4][...] = new.astype(BF16)
    across = lax.broadcasted_iota(jnp.int32, (2, 2), 1)
    down = lax.broadcasted_iota(jnp.int32, (2, 2), 0)
    first = jnp.where(across == 0, norm[0], norm[1])
    trust[...] = jnp.where(down == 0, first, jnp.where(across == 0, norm[2], norm[3]))
    for copy, src, dst in ((came[0], pool_in, pooled), (came[1], grad_in, image_grad)):
        copy.wait()
        cl = src.shape[0] // batch
        for j in range(src.shape[1] // LANES):
            lanes = slice(j * LANES, (j + 1) * LANES)
            wide[j] = src[:, lanes].astype(F32)
            for c in range(cl):
                dst[c * batch : (c + 1) * batch, lanes] = wide[
                    j, pl.ds(c, batch, stride=cl), :
                ].astype(BF16)


def final_pass(pooled, image_grad, grad_sum, sums, *small):
    batch, cl, pixels = image_grad.shape
    flat = lambda a: a.reshape(a.shape[0] * a.shape[1], a.shape[2])
    parts = (flat(pooled), flat(image_grad), grad_sum, sums)
    student, regress = small[0:2]
    outs = [jax.ShapeDtypeStruct((cl * batch, a.shape[2]), BF16) for a in (pooled, image_grad)]
    for a in (student, regress):
        outs += [jax.ShapeDtypeStruct(a.shape, F32)] * 4 + [jax.ShapeDtypeStruct(a.shape, BF16)]
    outs.append(jax.ShapeDtypeStruct((2, 2), F32))
    vmem = pl.BlockSpec(memory_space=pltpu.VMEM)
    results = pl.pallas_call(
        functools.partial(final_kernel, batch),
        out_shape=outs,
        in_specs=[pl.BlockSpec(memory_space=pl.ANY)] * 4 + [vmem] * len(small),
        out_specs=[vmem] * len(outs),
        scratch_shapes=[pltpu.VMEM(a.shape, a.dtype) for a in parts]
        + [
            pltpu.VMEM((pixels // LANES, batch * cl, LANES), F32),
            pltpu.SemaphoreType.DMA((len(parts),)),
        ],
        compiler_params=pltpu.CompilerParams(vmem_limit_bytes=58 << 20),
        name="final",
    )(*parts, *small)
    acts = [a.reshape(cl, batch, a.shape[1]) for a in results[0:2]]
    return (*acts, *(a.T for a in results[2:12]), results[12])


def split_pieces(weights):
    rows, cols = weights.shape
    return weights.reshape(rows, cols // 2, 2).transpose(2, 1, 0).reshape(cols, rows)


def back_weights(weights, outs):
    channels = weights.shape[0] // 9
    taps = weights.reshape(9, channels, outs)[::-1]
    return taps.transpose(1, 0, 2).reshape(channels, 9 * outs)


def gathered_filters(student_master, regress_master, teacher_weight):
    student_full = lax.all_gather(student_master.astype(BF16), "dp", axis=0, tiled=True)
    student_full = lax.all_gather(student_full, "chan", axis=1, tiled=True)
    regress_full = lax.all_gather(regress_master.astype(BF16), "dp", axis=0, tiled=True)
    regress_full = lax.all_gather(regress_full, "chan", axis=1, tiled=True)
    teacher_full = lax.all_gather(teacher_weight, "chan", axis=1, tiled=True)
    student_rows = split_pieces(student_full)
    return {
        "w_in": jnp.concatenate([student_rows, split_pieces(teacher_full)], axis=0),
        "w_reg": regress_full.T,
        "w_reg_back": back_weights(regress_full, regress_full.shape[1]),
        "w_in_back": back_weights(student_rows.T, student_full.shape[1]),
    }


def scattered_grads(student_part, regress_part):
    souts = student_part.shape[1]
    student_part = student_part.reshape(-1, 2, souts // 2).transpose(0, 2, 1).reshape(-1, souts)
    student_grad = lax.psum_scatter(student_part, "dp", scatter_dimension=0, tiled=True)
    student_grad = lax.psum_scatter(student_grad, "chan", scatter_dimension=1, tiled=True)
    regress_grad = lax.psum_scatter(regress_part, "dp", scatter_dimension=0, tiled=True)
    regress_grad = lax.psum_scatter(regress_grad, "chan", scatter_dimension=1, tiled=True)
    return student_grad, regress_grad


def on_device(
    n,
    group,
    images,
    student_master,
    regress_master,
    teacher_weight,
    student_win,
    teacher_win,
    pool_win,
    hint_mask,
    cotangent,
    mom_student,
    sq_student,
    ema_student,
    mom_regress,
    sq_regress,
    ema_regress,
):
    depth = student_master.shape[0]
    fused = group % 2 == 0 and depth % 16 == 0
    arrays = dict(
        images=images,
        swin=student_win,
        twin=teacher_win,
        pwin=pool_win,
        cot=cotangent,
        mask=hint_mask,
    )
    if fused:
        small = (student_master, regress_master, mom_student, sq_student, mom_regress, sq_regress)
        small = [a.T for a in small]
        names = ("student_t", "regress_t", "mom_student", "sq_student", "mom_regress", "sq_regress")
        arrays.update(zip(names, small))
        parts = layer_pass(n, group, fused, dict(arrays, teacher_t=teacher_weight.T))
        return final_pass(*parts, *small, ema_student.T, ema_regress.T)
    arrays.update(gathered_filters(student_master, regress_master, teacher_weight))
    pooled, image_grad, student_part, regress_part = layer_pass(n, group, fused, arrays)
    student_grad, regress_grad = scattered_grads(student_part, regress_part)
    mom_s, sq_s, upd_s = lamb_update(student_master, student_grad, mom_student, sq_student)
    mom_r, sq_r, upd_r = lamb_update(regress_master, regress_grad, mom_regress, sq_regress)
    all_sums = lax.psum(
        jnp.stack([jnp.sum(v * v) for v in (student_master, upd_s, regress_master, upd_r)]),
        ("dp", "chan"),
    )
    norms = jnp.sqrt(all_sums)
    new_student = student_master - LEARN_RATE * (norms[0] / norms[1]) * upd_s
    new_regress = regress_master - LEARN_RATE * (norms[2] / norms[3]) * upd_r
    ema_s = EMA_KEEP * ema_student + (1.0 - EMA_KEEP) * new_student
    ema_r = EMA_KEEP * ema_regress + (1.0 - EMA_KEEP) * new_regress
    return (
        pooled.transpose(1, 0, 2),
        image_grad.transpose(1, 0, 2),
        new_student,
        mom_s,
        sq_s,
        ema_s,
        new_student.astype(BF16),
        new_regress,
        mom_r,
        sq_r,
        ema_r,
        new_regress.astype(BF16),
        norms.reshape(2, 2),
    )


def solution(mesh):
    acts = P("chan", "dp", None)
    rows = P("dp", "chan")
    in_specs = (
        (acts, rows, rows, P(None, "chan"))
        + (acts, acts, acts, P("dp", None), acts)
        + (rows,) * 6
    )
    out_specs = (acts, acts) + (rows,) * 10 + (P(),)
    return jax.shard_map(
        functools.partial(on_device, mesh.shape["chan"], mesh.shape["dp"]),
        mesh=mesh,
        in_specs=in_specs,
        out_specs=out_specs,
        check_vma=False,
    )
```

```python
import functools
import types

import jax
import jax.numpy as jnp
from jax import lax
from jax.experimental import pallas as pl
from jax.experimental.pallas import tpu as pltpu
from jax.sharding import PartitionSpec as P

IMG = 32
STEP = 10
HINT_WEIGHT = 0.1
LEARN_RATE = 0.5
BETA_ONE = 0.9
BETA_TWO = 0.999
EPSILON = 1e-06
DECAY = 0.01
EMA_KEEP = 0.75

MESH = pl.DeviceIdType.MESH
F32 = jnp.float32
BF16 = jnp.bfloat16
STAGES = 1
CHUNK = IMG * IMG // STAGES
LANES = 128
AHEAD = 3
EARLY = 2


def dot(left, right):
    return jnp.dot(left, right, preferred_element_type=F32)


def dot_nt(left, right, precision=None):
    return lax.dot_general(
        left, right, (((1,), (1,)), ((), ())), precision=precision, preferred_element_type=F32
    )


def one_hot(shape, target, axis):
    at = lax.broadcasted_iota(jnp.int32, shape, axis)
    return jnp.where(at == target, 1.0, 0.0).astype(BF16)


def layer_kernel(size, names, *refs):
    r = types.SimpleNamespace(**dict(zip(names, refs)))
    n, batch, cl, tl, rl = size["n"], size["batch"], size["cl"], size["tl"], size["rl"]
    fused, group = size["fused"], size["group"]
    slots = batch // n
    chans, touts, regs = n * cl, n * tl, n * rl
    pixels = IMG * IMG
    cells = pixels // 4
    me = lax.axis_index("chan")
    row = lax.axis_index("dp")
    core, chip, pairs = row % 2, row // 2, group // 2
    held, send = r.held, r.send

    def beside(step):
        return lax.rem(me + step, n)

    def at_chan(index):
        return {"chan": index}

    def at_row(index):
        return {"dp": index}

    def remote(src, dst, out_sem, in_sem, device):
        return pltpu.make_async_remote_copy(
            src, dst, out_sem, in_sem, device_id=device, device_id_type=MESH
        )

    greeted = [at_chan(beside(step)) for step in range(1, n)]
    if fused:
        greeted += [at_row(lax.rem(row + step, group)) for step in range(1, group)]

    loads = [
        pltpu.make_async_copy(r.images, r.raw, r.load_sem.at[0]),
        pltpu.make_async_copy(r.cot, r.raw_cot, r.load_sem.at[1]),
    ]
    for src, dst in ((r.swin, r.swin_wide), (r.twin, r.twin_wide), (r.pwin, r.pwin_wide)):
        for j in range(dst.shape[0]):
            loads.append(
                pltpu.make_async_copy(
                    src.at[:, pl.ds(j * LANES, LANES)], dst.at[j], r.load_sem.at[len(loads)]
                )
            )
    for copy in loads:
        copy.start()

    barrier = pltpu.get_barrier_semaphore()
    for device in greeted:
        pl.semaphore_signal(barrier, inc=1, device_id=device, device_id_type=MESH)

    if fused:
        depth = r.student_t.shape[1]

        def block(index):
            return pl.ds(pl.multiple_of(index * depth, 16), depth)

        mine = block(row)
        r.flat[...] = jnp.zeros_like(r.flat)
        r.flat[0 : 2 * cl, 0:depth] = r.student_t[...]
        r.flat[2 * cl : 2 * cl + rl, 0:depth] = r.regress_t[...]
        r.filters[me, mine, 0:LANES] = r.flat[...].T[0:depth, :].astype(BF16)
        r.teach_flat[...] = jnp.zeros_like(r.teach_flat)
        r.teach_flat[0 : 2 * tl, :] = r.teacher_t[...].astype(F32)
        r.teach_cols[...] = r.teach_flat[...].T
        r.filters[me, mine, LANES:] = r.teach_cols[mine, :].astype(BF16)

    pl.semaphore_wait(barrier, len(greeted))

    if fused:
        filter_z = [
            remote(
                r.filters.at[me, mine],
                r.filters.at[me, mine],
                r.fz_send.at[step],
                r.fz_recv.at[step],
                at_chan(beside(step)),
            )
            for step in range(1, n)
        ]
        for copy in filter_z:
            copy.start()

    for copy in loads:
        copy.wait()
    for j in range(r.wide.shape[0]):
        r.wide[j] = r.raw[:, j * LANES : (j + 1) * LANES].astype(F32)
    for j in range(r.cot_wide.shape[0]):
        r.cot_wide[j] = r.raw_cot[:, j * LANES : (j + 1) * LANES].astype(F32)

    def in_copies(slot, step, part):
        to = beside(step)
        rows = pl.ds(0, 2 * cl) if part == 0 else pl.ds(2 * cl, tl)
        copies = [
            remote(
                send.at[slot, to, rows],
                held.at[slot, me, rows],
                r.in_send.at[slot, part, step],
                r.in_recv.at[slot, part, step],
                at_chan(to),
            )
        ]
        if part == 1:
            copies.append(
                remote(
                    r.send_pool.at[slot, to],
                    r.held_pool.at[slot, me],
                    r.pool_in_send.at[slot, step],
                    r.pool_in_recv.at[slot, step],
                    at_chan(to),
                )
            )
        return copies

    def start_in(slot, part):
        for step in range(1, n):
            for copy in in_copies(slot, step, part):
                copy.start()

    def wait_in(slot, part):
        for step in range(1, n):
            for copy in in_copies(slot, step, part):
                copy.wait_recv()

    def start_later(slot, part):
        later = slot + (part + AHEAD) // 2
        pl.when(later < slots)(lambda: start_in(later, (part + AHEAD) % 2))

    def own_copies(slot):
        return (
            pltpu.make_async_copy(send.at[slot, me], held.at[slot, me], r.own_sem.at[slot, 0]),
            pltpu.make_async_copy(
                r.send_pool.at[slot, me], r.held_pool.at[slot, me], r.own_sem.at[slot, 1]
            ),
        )

    def lanes_of(index):
        return pl.ds(pl.multiple_of(index * cl, cl), cl)

    def out_copies(slot, step):
        to = beside(step)
        return (
            remote(
                r.low_part.at[slot, lanes_of(to)],
                r.grad_out.at[me * slots + slot],
                r.out_send.at[slot, step],
                r.out_recv.at[slot, step],
                at_chan(to),
            ),
            remote(
                r.pool_part.at[slot, lanes_of(to)],
                r.pool_out.at[me * slots + slot],
                r.pool_out_send.at[slot, step],
                r.pool_out_recv.at[slot, step],
                at_chan(to),
            ),
        )

    def own_out(slot):
        here = me * slots + slot
        return (
            pltpu.make_async_copy(
                r.low_part.at[slot, lanes_of(me)], r.grad_out.at[here], r.own_out_sem.at[slot, 0]
            ),
            pltpu.make_async_copy(
                r.pool_part.at[slot, lanes_of(me)], r.pool_out.at[here], r.own_out_sem.at[slot, 1]
            ),
        )

    def start_out(slot):
        for step in range(1, n):
            for copy in out_copies(slot, step):
                copy.start()

    out_order = {"early": range(0, EARLY), "mid": range(EARLY, slots - 1), "late": range(slots - 1, slots)}

    def start_outs(when):
        for slot in out_order[when]:
            start_out(slot)

    def prepare(slot, carry):
        for to in range(n):
            first_row = to * slots + slot
            for src, dst, first, rows in (
                (r.wide, send, 0, cl),
                (r.swin_wide, send, cl, cl),
                (r.twin_wide, send, 2 * cl, tl),
                (r.pwin_wide, r.send_pool, 0, cl),
                (r.cot_wide, r.send_pool, cl, cl),
            ):
                for j in range(src.shape[0]):
                    dst[slot, to, first : first + rows, j * LANES : (j + 1) * LANES] = (
                        src[j, pl.ds(first_row, rows, stride=batch), :].astype(F32).astype(BF16)
                    )
        for part in range(2):
            pl.when(2 * slot + part < AHEAD)(functools.partial(start_in, slot, part))
        for copy in own_copies(slot):
            copy.start()
        return carry

    lax.fori_loop(0, slots, prepare, 0)

    lane = lax.broadcasted_iota(jnp.int32, (16, pixels), 1)
    row_of, col_of = lane // IMG, lane % IMG
    for which, bad in enumerate((row_of == 0, row_of == IMG - 1, col_of == 0, col_of == IMG - 1)):
        r.edge[which] = jnp.where(bad, 0.0, 1.0).astype(BF16)
    spot = lax.broadcasted_iota(jnp.int32, (1, pixels), 1)
    home = (spot // (2 * IMG)) * (IMG // 2) + (spot % IMG) // 2
    r.up[...] = one_hot((cells, pixels), home, 0)
    r.sgrad[...] = jnp.zeros_like(r.sgrad)
    r.rgrad[...] = jnp.zeros_like(r.rgrad)

    if fused:
        picked = 2 * cl + rl + 2 * tl
        at = lax.broadcasted_iota(jnp.int32, (picked, 1), 0)
        teach = at - 2 * cl - rl
        lane_at = jnp.where(
            at < 2 * cl,
            2 * (at % cl) + at // cl,
            jnp.where(at < 2 * cl + rl, at, LANES + 2 * (teach % tl) + teach // tl),
        )
        r.gather_rows[...] = one_hot((picked, r.filters.shape[2]), lane_at, 1)
        for z in range(n):
            at = lax.broadcasted_iota(jnp.int32, (LANES, 1), 0)
            col_at = jnp.where(
                at < 2 * cl,
                (at % 2) * chans + z * cl + at // 2,
                jnp.where(at < 2 * cl + rl, 2 * chans + z * rl + at - 2 * cl, -1),
            )
            r.spread[z] = one_hot((LANES, r.spread.shape[2]), col_at, 1)

        for copy in filter_z:
            copy.wait_recv()

        def filter_chip(step):
            to = lax.rem(chip + step, pairs)
            return remote(
                r.filters.at[:, mine],
                r.filters.at[:, mine],
                r.fx_send.at[step],
                r.fx_recv.at[step],
                at_row(2 * to + core),
            )

        def filter_core(step):
            rows = block(2 * lax.rem(chip + pairs - step, pairs) + core)
            return remote(
                r.filters.at[:, rows],
                r.filters.at[:, rows],
                r.fc_send.at[step],
                r.fc_recv.at[step],
                at_row(row + 1 - 2 * core),
            )

        for step in range(1, pairs):
            filter_chip(step).start()
        filter_core(0).start()
        for step in range(1, pairs):
            filter_chip(step).wait_recv()
            filter_core(step).start()
        for step in range(pairs):
            filter_core(step).wait_recv()

        for z in range(n):
            rows_of = dot_nt(r.gather_rows[...], r.filters[z]).astype(BF16)
            first = 0
            for dst, start, many in (
                (r.w_in, z * cl, cl),
                (r.w_in, chans + z * cl, cl),
                (r.w_reg, z * rl, rl),
                (r.w_in, 2 * chans + z * tl, tl),
                (r.w_in, 2 * chans + touts + z * tl, tl),
            ):
                dst[start : start + many, :] = rows_of[first : first + many, :]
                first += many
        for tap in range(9):
            rows = slice((8 - tap) * chans, (9 - tap) * chans)
            total = dot(r.filters[0, rows, 0:LANES], r.spread[0])
            for z in range(1, n):
                total += dot(r.filters[z, rows, 0:LANES], r.spread[z])
            total = total.astype(BF16)
            r.w_in_back[:, tap * 2 * chans : (tap + 1) * 2 * chans] = total[:, 0 : 2 * chans]
            r.w_reg_back[:, tap * regs : (tap + 1) * regs] = total[:, 2 * chans : 2 * chans + regs]

    def columns(load, rows, dst, stage):
        many = rows // (16 * STAGES)
        for g in range(many):
            first = pl.multiple_of((stage * many + g) * 16, 16)
            base = load(first)
            for ky in range(3):
                if ky == 1:
                    moved = base
                else:
                    moved = pltpu.roll(base, (pixels - IMG * (ky - 1)) % pixels, 1)
                    moved = moved * r.edge[0 if ky == 0 else 1]
                for kx in range(3):
                    if kx == 1:
                        tap = moved
                    else:
                        tap = pltpu.roll(moved, (pixels - (kx - 1)) % pixels, 1)
                        tap = tap * r.edge[2 if kx == 0 else 3]
                    dst[pl.ds((3 * ky + kx) * rows + first, 16), :] = tap

    def stages(*bodies):
        def one(stage, carry):
            for body in bodies:
                body(stage)
            return carry

        lax.fori_loop(0, STAGES, one, 0)

    def chunks(body):
        def one(stage):
            body(pl.ds(pl.multiple_of(stage * CHUNK, CHUNK), CHUNK))

        return one

    def add_grads(grads, left, right):
        many = grads.shape[0] // STAGES

        def one(stage):
            rows = pl.ds(pl.multiple_of(stage * many, 16), many)
            grads[rows, :] += dot_nt(left[rows, :], right[...])

        return one

    def corner_of(here):
        at = lax.broadcasted_iota(jnp.int32, (1, CHUNK), 1)
        return (2 * ((at // IMG) % 2) + at % 2).astype(F32)

    if fused:
        parts = ((r.rgrad, r.rc_send, r.rc_recv, r.rx_send, r.rx_recv),
                 (r.sgrad, r.sc_send, r.sc_recv, r.sx_send, r.sx_recv))

        def core_copy(which):
            return remote(
                parts[which][1],
                parts[which][2],
                r.core_send.at[which],
                r.core_recv.at[which],
                at_row(row + 1 - 2 * core),
            )

        def start_core(which):
            grads, out = parts[which][:2]
            for pair in range(pairs):
                out[pair] = grads[block(2 * pair + 1 - core), :].astype(BF16)
            core_copy(which).start()

        def chip_copy(which, step):
            return remote(
                parts[which][3].at[step],
                parts[which][4].at[step],
                r.chip_send.at[which, step],
                r.chip_recv.at[which, step],
                at_row(2 * lax.rem(chip + step, pairs) + core),
            )

        def chan_copy(step):
            return remote(
                r.zs_send.at[step],
                r.zs_recv.at[step],
                r.chan_send.at[step],
                r.chan_recv.at[step],
                at_chan(beside(step)),
            )

        def row_norm(step):
            return remote(
                r.part_rows.at[row],
                r.part_rows.at[row],
                r.rn_send.at[step],
                r.rn_recv.at[step],
                at_row(lax.rem(row + step, group)),
            )

        def chan_norm(step):
            return remote(
                r.part_chans.at[me],
                r.part_chans.at[me],
                r.cn_send.at[step],
                r.cn_recv.at[step],
                at_chan(beside(step)),
            )

    def step_chip(which):
        grads, _, came, out, _ = parts[which]
        cols = slice(2 * chans, 2 * chans + regs) if which == 0 else slice(0, 2 * chans)
        core_copy(which).wait_recv()
        for step in range(1, pairs):
            to = lax.rem(chip + step, pairs)
            out[step] = (grads[block(2 * to + core), :] + came[to].astype(F32)).astype(BF16)
            chip_copy(which, step).start()
        r.whole_grad[:, cols] = grads[block(row), :] + came[chip].astype(F32)

    def image(slot, carry):
        last = slot == slots - 1
        wait_in(slot, 0)
        start_later(slot, 0)
        for copy in own_copies(slot):
            copy.wait()

        def image_rows(first):
            return held[slot, first // cl, pl.ds(pl.multiple_of(first % cl, 16), 16), :]

        def picked(here):
            return held[slot, :, cl : 2 * cl, here].reshape(chans, CHUNK).astype(F32) > 0.5

        def head(here):
            pre = dot(r.w_in[0 : 2 * chans, :], r.x_cols[:, here])
            r.out_low[:, here] = jnp.where(picked(here), pre[chans:], pre[:chans]).astype(BF16)

        def teach(here):
            r.teach[:, here] = dot(r.w_in[2 * chans :, :], r.x_cols[:, here])

        def guess(here):
            r.guess[:, here] = dot(r.w_reg[...], r.o_cols[:, here])

        def pooling(here):
            cell_win = r.held_pool[slot, :, 0:cl, :].reshape(chans, cells)
            cell_cot = r.held_pool[slot, :, cl : 2 * cl, :].reshape(chans, cells)
            chosen = dot(cell_win, r.up[:, here]) == corner_of(here)
            spread = dot(cell_cot, r.up[:, here])
            r.pool_back[:, here] = jnp.where(chosen, spread, 0.0).astype(BF16)
            kept = jnp.where(chosen, r.out_low[:, here].astype(F32), 0.0).astype(BF16)
            part = dot_nt(kept, r.up[:, here])
            r.pool_part[slot] = (r.pool_part[slot].astype(F32) + part).astype(BF16)

        def hints(here):
            pick = held[slot, :, 2 * cl :, here].reshape(touts, CHUNK).astype(F32)
            target = jnp.where(pick > 0.5, r.teach[touts:, here], r.teach[:touts, here])
            weight = scale * r.mask[pl.ds(me * slots + slot, 1), here].astype(F32)
            r.hint[:, here] = (weight * (r.guess[:, here] - target)).astype(BF16)

        def back(here):
            total = dot(r.w_reg_back[...], r.h_cols[:, here]) + r.pool_back[:, here].astype(F32)
            pick = picked(here)
            r.pre_grad[0:chans, here] = jnp.where(pick, 0.0, total).astype(BF16)
            r.pre_grad[chans:, here] = jnp.where(pick, total, 0.0).astype(BF16)

        def image_back(here):
            r.low_part[slot, :, here] = dot(r.w_in_back[...], r.p_cols[:, here]).astype(BF16)

        def columns_of(src, dst):
            rows = src.shape[0]
            return lambda stage: columns(lambda first: src[pl.ds(first, 16), :], rows, dst, stage)

        spot_mask = r.mask[pl.ds(me * slots + slot, 1), :].astype(F32)
        count = jnp.sum(spot_mask, axis=1, keepdims=True)
        scale = HINT_WEIGHT * (pixels / count)
        r.pool_part[slot] = jnp.zeros((chans, cells), BF16)

        stages(lambda stage: columns(image_rows, chans, r.x_cols, stage))
        stages(chunks(head))
        stages(chunks(teach), columns_of(r.out_low, r.o_cols))
        stages(chunks(guess))
        wait_in(slot, 1)
        start_later(slot, 1)
        pl.when(last)(lambda: start_outs("early"))
        stages(chunks(hints))
        stages(add_grads(r.rgrad, r.o_cols, r.hint), columns_of(r.hint, r.h_cols))
        if fused:
            pl.when(last)(lambda: start_core(0))
        stages(chunks(pooling))
        stages(chunks(back))
        stages(add_grads(r.sgrad, r.x_cols, r.pre_grad), columns_of(r.pre_grad, r.p_cols))
        if fused:

            def reduce_more():
                start_core(1)
                step_chip(0)

            pl.when(last)(reduce_more)
        stages(chunks(image_back))
        if not fused:

            def start_rest():
                start_outs("mid")
                start_outs("late")

            pl.when(last)(start_rest)
        for copy in own_out(slot):
            copy.start()
        return carry

    if fused:
        r.whole_grad[...] = jnp.zeros_like(r.whole_grad)
    lax.fori_loop(0, slots, image, 0)

    if fused:
        step_chip(1)
        for which, cols in ((0, slice(2 * chans, 2 * chans + regs)), (1, slice(0, 2 * chans))):
            came = parts[which][4]
            for step in range(1, pairs):
                chip_copy(which, step).wait_recv()
            total = r.whole_grad[:, cols]
            for step in range(1, pairs):
                total += came[step].astype(F32)
            r.whole_grad[:, cols] = total
        low_grad = r.whole_grad[...].astype(BF16)
        for step in range(1, n):
            r.zs_send[step] = dot_nt(low_grad, r.spread[beside(step)]).astype(BF16)
            chan_copy(step).start()
        start_outs("mid")
        total = dot_nt(
            r.whole_grad[...], r.spread[me].astype(F32), precision=lax.Precision.HIGHEST
        )
        for step in range(1, n):
            chan_copy(step).wait_recv()
        for step in range(1, n):
            total += r.zs_recv[step].astype(F32)
        r.tall[0:depth, :] = total
        total = r.tall[...].T[:, 0:depth]
        r.grad_sum[...] = total
        student, regress = r.student_t[...], r.regress_t[...]
        upd_s = lamb_update(student, total[0 : 2 * cl], r.mom_student[...], r.sq_student[...])[2]
        upd_r = lamb_update(
            regress, total[2 * cl : 2 * cl + rl], r.mom_regress[...], r.sq_regress[...]
        )[2]
        place = lax.broadcasted_iota(jnp.int32, (8, LANES), 1)
        tile = jnp.zeros((8, LANES), F32)
        for index, value in enumerate((student, upd_s, regress, upd_r)):
            square = jnp.sum(jnp.sum(value * value, axis=1, keepdims=True), axis=0, keepdims=True)
            tile = jnp.where(place == index, square, tile)
        r.part_chans[me] = tile
        for step in range(1, n):
            chan_norm(step).start()
        start_outs("late")
        for step in range(1, n):
            chan_norm(step).wait_recv()
        tile = r.part_chans[0]
        for index in range(1, n):
            tile += r.part_chans[index]
        r.part_rows[row] = tile
        for step in range(1, group):
            row_norm(step).start()
        for step in range(1, group):
            row_norm(step).wait_recv()
        tile = r.part_rows[0]
        for index in range(1, group):
            tile += r.part_rows[index]
        r.sums[...] = tile

    def finish(slot, carry):
        for step in range(1, n):
            for copy in in_copies(slot, step, 0) + in_copies(slot, step, 1):
                copy.wait_send()
            for copy in out_copies(slot, step):
                copy.wait()
        for copy in own_out(slot):
            copy.wait()
        return carry

    lax.fori_loop(0, slots, finish, 0)
    if fused:
        for step in range(1, n):
            filter_z[step - 1].wait_send()
            chan_copy(step).wait_send()
            chan_norm(step).wait_send()
        for step in range(1, group):
            row_norm(step).wait_send()
        for step in range(pairs):
            filter_core(step).wait_send()
        for step in range(1, pairs):
            filter_chip(step).wait_send()
        for which in range(2):
            core_copy(which).wait_send()
            for step in range(1, pairs):
                chip_copy(which, step).wait_send()


def lamb_update(weights, grads, moment, second):
    moment_new = BETA_ONE * moment + (1.0 - BETA_ONE) * grads
    second_new = BETA_TWO * second + (1.0 - BETA_TWO) * grads * grads
    moment_hat = moment_new / (1.0 - BETA_ONE**STEP)
    second_hat = second_new / (1.0 - BETA_TWO**STEP)
    update = moment_hat / (jnp.sqrt(second_hat) + EPSILON) + DECAY * weights
    return (moment_new, second_new, update)


def layer_pass(n, group, fused, arrays):
    cl, batch, pixels = arrays["images"].shape
    tl = arrays["twin"].shape[0]
    cells = arrays["pwin"].shape[2]
    slots = batch // n
    chans = n * cl
    if fused:
        rl, depth = arrays["regress_t"].shape
    else:
        rl = arrays["w_reg"].shape[0] // n
    regs, touts, pairs = n * rl, n * tl, group // 2
    size = dict(n=n, batch=batch, cl=cl, tl=tl, rl=rl, fused=fused, group=group)
    vmem = pl.BlockSpec(memory_space=pltpu.VMEM)
    in_hbm = ("images", "swin", "twin", "pwin", "cot")
    ins = {
        name: a.reshape(a.shape[0] * a.shape[1], a.shape[2]) if name in in_hbm else a
        for name, a in arrays.items()
    }
    outs = {
        "pool_out": jax.ShapeDtypeStruct((batch, cl, cells), BF16),
        "grad_out": jax.ShapeDtypeStruct((batch, cl, pixels), BF16),
    }
    grads = {"sgrad": (9 * chans, 2 * chans), "rgrad": (9 * chans, regs)}
    dma = lambda *shape: pltpu.SemaphoreType.DMA(shape)
    scratch = {
        "raw": pltpu.VMEM((cl * batch, pixels), BF16),
        "raw_cot": pltpu.VMEM((cl * batch, cells), BF16),
        "wide": pltpu.VMEM((pixels // LANES, cl * batch, LANES), F32),
        "swin_wide": pltpu.VMEM((pixels // LANES, cl * batch, LANES), jnp.int32),
        "twin_wide": pltpu.VMEM((pixels // LANES, tl * batch, LANES), jnp.int32),
        "pwin_wide": pltpu.VMEM((cells // LANES, cl * batch, LANES), jnp.int32),
        "cot_wide": pltpu.VMEM((cells // LANES, cl * batch, LANES), F32),
        "load_sem": dma(2 + 2 * (pixels // LANES) + cells // LANES),
        "send": pltpu.VMEM((slots, n, 2 * cl + tl, pixels), BF16),
        "send_pool": pltpu.VMEM((slots, n, 2 * cl, cells), BF16),
        "held": pltpu.VMEM((slots, n, 2 * cl + tl, pixels), BF16),
        "held_pool": pltpu.VMEM((slots, n, 2 * cl, cells), BF16),
        "low_part": pltpu.VMEM((slots, chans, pixels), BF16),
        "pool_part": pltpu.VMEM((slots, chans, cells), BF16),
        "edge": pltpu.VMEM((4, 16, pixels), BF16),
        "up": pltpu.VMEM((cells, pixels), BF16),
        "x_cols": pltpu.VMEM((9 * chans, pixels), BF16),
        "o_cols": pltpu.VMEM((9 * chans, pixels), BF16),
        "h_cols": pltpu.VMEM((9 * regs, pixels), BF16),
        "p_cols": pltpu.VMEM((9 * 2 * chans, pixels), BF16),
        "out_low": pltpu.VMEM((chans, pixels), BF16),
        "pool_back": pltpu.VMEM((chans, pixels), BF16),
        "hint": pltpu.VMEM((regs, pixels), BF16),
        "teach": pltpu.VMEM((2 * touts, pixels), F32),
        "guess": pltpu.VMEM((regs, pixels), F32),
        "pre_grad": pltpu.VMEM((2 * chans, pixels), BF16),
        "own_sem": dma(slots, 2),
        "own_out_sem": dma(slots, 2),
    }
    scratch["in_send"] = dma(slots, 2, n)
    scratch["in_recv"] = dma(slots, 2, n)
    for name in ("pool_in", "out", "pool_out"):
        scratch[name + "_send"] = dma(slots, n)
        scratch[name + "_recv"] = dma(slots, n)
    if fused:
        cols = 2 * chans + 2 * LANES
        tall = -(-depth // LANES) * LANES
        outs["grad_sum"] = jax.ShapeDtypeStruct((LANES, depth), F32)
        outs["sums"] = jax.ShapeDtypeStruct((8, LANES), F32)
        scratch.update({name: pltpu.VMEM(shape, F32) for name, shape in grads.items()})
        scratch.update(
            {
                "flat": pltpu.VMEM((LANES, tall), F32),
                "tall": pltpu.VMEM((tall, LANES), F32),
                "teach_flat": pltpu.VMEM((LANES, 9 * chans), F32),
                "teach_cols": pltpu.VMEM((9 * chans, LANES), F32),
                "filters": pltpu.VMEM((n, 9 * chans, 2 * LANES), BF16),
                "gather_rows": pltpu.VMEM((2 * cl + rl + 2 * tl, 2 * LANES), BF16),
                "spread": pltpu.VMEM((n, LANES, cols), BF16),
                "w_in": pltpu.VMEM((2 * chans + 2 * touts, 9 * chans), BF16),
                "w_reg": pltpu.VMEM((regs, 9 * chans), BF16),
                "w_reg_back": pltpu.VMEM((chans, 9 * regs), BF16),
                "w_in_back": pltpu.VMEM((chans, 9 * 2 * chans), BF16),
                "rc_send": pltpu.VMEM((pairs, depth, regs), BF16),
                "rc_recv": pltpu.VMEM((pairs, depth, regs), BF16),
                "rx_send": pltpu.VMEM((pairs, depth, regs), BF16),
                "rx_recv": pltpu.VMEM((pairs, depth, regs), BF16),
                "sc_send": pltpu.VMEM((pairs, depth, 2 * chans), BF16),
                "sc_recv": pltpu.VMEM((pairs, depth, 2 * chans), BF16),
                "sx_send": pltpu.VMEM((pairs, depth, 2 * chans), BF16),
                "sx_recv": pltpu.VMEM((pairs, depth, 2 * chans), BF16),
                "whole_grad": pltpu.VMEM((depth, cols), F32),
                "zs_send": pltpu.VMEM((n, depth, LANES), BF16),
                "zs_recv": pltpu.VMEM((n, depth, LANES), BF16),
                "part_rows": pltpu.VMEM((group, 8, LANES), F32),
                "part_chans": pltpu.VMEM((n, 8, LANES), F32),
                "core_send": dma(2),
                "core_recv": dma(2),
                "chip_send": dma(2, pairs),
                "chip_recv": dma(2, pairs),
            }
        )
        for name, many in (
            ("fz", n), ("fx", pairs), ("fc", pairs), ("chan", n), ("rn", group), ("cn", n)
        ):
            scratch[name + "_send"] = dma(many)
            scratch[name + "_recv"] = dma(many)
    else:
        outs.update({name: jax.ShapeDtypeStruct(shape, F32) for name, shape in grads.items()})
    flops = 2 * slots * pixels * 9 * chans * (3 * 2 * chans + 2 * touts + 3 * regs)
    names = tuple(ins) + tuple(outs) + tuple(scratch)
    return pl.pallas_call(
        functools.partial(layer_kernel, size, names),
        out_shape=list(outs.values()),
        in_specs=[
            pl.BlockSpec(memory_space=pl.ANY) if name in in_hbm else vmem for name in ins
        ],
        out_specs=[vmem] * len(outs),
        scratch_shapes=list(scratch.values()),
        compiler_params=pltpu.CompilerParams(
            collective_id=0, has_side_effects=True, vmem_limit_bytes=58 << 20
        ),
        cost_estimate=pl.CostEstimate(flops=flops, bytes_accessed=16 << 20, transcendentals=0),
        name="layer",
    )(*ins.values())


def final_kernel(batch, *refs):
    wide, came_sem = refs[-2:]
    came = []
    for index, (src, dst) in enumerate(zip(refs[0:4], refs[-6:-2])):
        came.append(pltpu.make_async_copy(src, dst, came_sem.at[index]))
        came[-1].start()
    pool_in, grad_in, grad_sum, sums = refs[-6:-2]
    student, regress, mom_s, sq_s, mom_r, sq_r, ema_s, ema_r = refs[4:12]
    pooled, image_grad, new_s, new_r, trust = refs[12], refs[13], refs[14:19], refs[19:24], refs[24]
    came[2].wait()
    came[3].wait()
    norm = [jnp.sqrt(sums[0:1, k : k + 1]) for k in range(4)]
    souts, regs = student.shape[0], regress.shape[0]
    for weights, grads, moment, second, average, outs, top, bottom in (
        (student, grad_sum[0:souts, :], mom_s, sq_s, ema_s, new_s, norm[0], norm[1]),
        (regress, grad_sum[souts : souts + regs, :], mom_r, sq_r, ema_r, new_r, norm[2], norm[3]),
    ):
        moment_new, second_new, update = lamb_update(
            weights[...], grads, moment[...], second[...]
        )
        new = weights[...] - LEARN_RATE * (top / bottom) * update
        outs[0][...] = new
        outs[1][...] = moment_new
        outs[2][...] = second_new
        outs[3][...] = EMA_KEEP * average[...] + (1.0 - EMA_KEEP) * new
        outs[4][...] = new.astype(BF16)
    across = lax.broadcasted_iota(jnp.int32, (2, 2), 1)
    down = lax.broadcasted_iota(jnp.int32, (2, 2), 0)
    first = jnp.where(across == 0, norm[0], norm[1])
    trust[...] = jnp.where(down == 0, first, jnp.where(across == 0, norm[2], norm[3]))
    for copy, src, dst in ((came[0], pool_in, pooled), (came[1], grad_in, image_grad)):
        copy.wait()
        cl = src.shape[0] // batch
        for j in range(src.shape[1] // LANES):
            lanes = slice(j * LANES, (j + 1) * LANES)
            wide[j] = src[:, lanes].astype(F32)
            for c in range(cl):
                dst[c * batch : (c + 1) * batch, lanes] = wide[
                    j, pl.ds(c, batch, stride=cl), :
                ].astype(BF16)


def final_pass(pooled, image_grad, grad_sum, sums, *small):
    batch, cl, pixels = image_grad.shape
    flat = lambda a: a.reshape(a.shape[0] * a.shape[1], a.shape[2])
    parts = (flat(pooled), flat(image_grad), grad_sum, sums)
    student, regress = small[0:2]
    outs = [jax.ShapeDtypeStruct((cl * batch, a.shape[2]), BF16) for a in (pooled, image_grad)]
    for a in (student, regress):
        outs += [jax.ShapeDtypeStruct(a.shape, F32)] * 4 + [jax.ShapeDtypeStruct(a.shape, BF16)]
    outs.append(jax.ShapeDtypeStruct((2, 2), F32))
    vmem = pl.BlockSpec(memory_space=pltpu.VMEM)
    results = pl.pallas_call(
        functools.partial(final_kernel, batch),
        out_shape=outs,
        in_specs=[pl.BlockSpec(memory_space=pl.ANY)] * 4 + [vmem] * len(small),
        out_specs=[vmem] * len(outs),
        scratch_shapes=[pltpu.VMEM(a.shape, a.dtype) for a in parts]
        + [
            pltpu.VMEM((pixels // LANES, batch * cl, LANES), F32),
            pltpu.SemaphoreType.DMA((len(parts),)),
        ],
        compiler_params=pltpu.CompilerParams(vmem_limit_bytes=58 << 20),
        name="final",
    )(*parts, *small)
    acts = [a.reshape(cl, batch, a.shape[1]) for a in results[0:2]]
    return (*acts, *(a.T for a in results[2:12]), results[12])


def split_pieces(weights):
    rows, cols = weights.shape
    return weights.reshape(rows, cols // 2, 2).transpose(2, 1, 0).reshape(cols, rows)


def back_weights(weights, outs):
    channels = weights.shape[0] // 9
    taps = weights.reshape(9, channels, outs)[::-1]
    return taps.transpose(1, 0, 2).reshape(channels, 9 * outs)


def gathered_filters(student_master, regress_master, teacher_weight):
    student_full = lax.all_gather(student_master.astype(BF16), "dp", axis=0, tiled=True)
    student_full = lax.all_gather(student_full, "chan", axis=1, tiled=True)
    regress_full = lax.all_gather(regress_master.astype(BF16), "dp", axis=0, tiled=True)
    regress_full = lax.all_gather(regress_full, "chan", axis=1, tiled=True)
    teacher_full = lax.all_gather(teacher_weight, "chan", axis=1, tiled=True)
    student_rows = split_pieces(student_full)
    return {
        "w_in": jnp.concatenate([student_rows, split_pieces(teacher_full)], axis=0),
        "w_reg": regress_full.T,
        "w_reg_back": back_weights(regress_full, regress_full.shape[1]),
        "w_in_back": back_weights(student_rows.T, student_full.shape[1]),
    }


def scattered_grads(student_part, regress_part):
    souts = student_part.shape[1]
    student_part = student_part.reshape(-1, 2, souts // 2).transpose(0, 2, 1).reshape(-1, souts)
    student_grad = lax.psum_scatter(student_part, "dp", scatter_dimension=0, tiled=True)
    student_grad = lax.psum_scatter(student_grad, "chan", scatter_dimension=1, tiled=True)
    regress_grad = lax.psum_scatter(regress_part, "dp", scatter_dimension=0, tiled=True)
    regress_grad = lax.psum_scatter(regress_grad, "chan", scatter_dimension=1, tiled=True)
    return student_grad, regress_grad


def on_device(
    n,
    group,
    images,
    student_master,
    regress_master,
    teacher_weight,
    student_win,
    teacher_win,
    pool_win,
    hint_mask,
    cotangent,
    mom_student,
    sq_student,
    ema_student,
    mom_regress,
    sq_regress,
    ema_regress,
):
    depth = student_master.shape[0]
    fused = group % 2 == 0 and depth % 16 == 0
    arrays = dict(
        images=images,
        swin=student_win,
        twin=teacher_win,
        pwin=pool_win,
        cot=cotangent,
        mask=hint_mask,
    )
    if fused:
        small = (student_master, regress_master, mom_student, sq_student, mom_regress, sq_regress)
        small = [a.T for a in small]
        names = ("student_t", "regress_t", "mom_student", "sq_student", "mom_regress", "sq_regress")
        arrays.update(zip(names, small))
        parts = layer_pass(n, group, fused, dict(arrays, teacher_t=teacher_weight.T))
        return final_pass(*parts, *small, ema_student.T, ema_regress.T)
    arrays.update(gathered_filters(student_master, regress_master, teacher_weight))
    pooled, image_grad, student_part, regress_part = layer_pass(n, group, fused, arrays)
    student_grad, regress_grad = scattered_grads(student_part, regress_part)
    mom_s, sq_s, upd_s = lamb_update(student_master, student_grad, mom_student, sq_student)
    mom_r, sq_r, upd_r = lamb_update(regress_master, regress_grad, mom_regress, sq_regress)
    all_sums = lax.psum(
        jnp.stack([jnp.sum(v * v) for v in (student_master, upd_s, regress_master, upd_r)]),
        ("dp", "chan"),
    )
    norms = jnp.sqrt(all_sums)
    new_student = student_master - LEARN_RATE * (norms[0] / norms[1]) * upd_s
    new_regress = regress_master - LEARN_RATE * (norms[2] / norms[3]) * upd_r
    ema_s = EMA_KEEP * ema_student + (1.0 - EMA_KEEP) * new_student
    ema_r = EMA_KEEP * ema_regress + (1.0 - EMA_KEEP) * new_regress
    return (
        pooled.transpose(1, 0, 2),
        image_grad.transpose(1, 0, 2),
        new_student,
        mom_s,
        sq_s,
        ema_s,
        new_student.astype(BF16),
        new_regress,
        mom_r,
        sq_r,
        ema_r,
        new_regress.astype(BF16),
        norms.reshape(2, 2),
    )


def solution(mesh):
    acts = P("chan", "dp", None)
    rows = P("dp", "chan")
    in_specs = (
        (acts, rows, rows, P(None, "chan"))
        + (acts, acts, acts, P("dp", None), acts)
        + (rows,) * 6
    )
    out_specs = (acts, acts) + (rows,) * 10 + (P(),)
    return jax.shard_map(
        functools.partial(on_device, mesh.shape["chan"], mesh.shape["dp"]),
        mesh=mesh,
        in_specs=in_specs,
        out_specs=out_specs,
        check_vma=False,
    )
```

```python
import functools
import types

import jax
import jax.numpy as jnp
from jax import lax
from jax.experimental import pallas as pl
from jax.experimental.pallas import tpu as pltpu
from jax.sharding import PartitionSpec as P

IMG = 32
STEP = 10
HINT_WEIGHT = 0.1
LEARN_RATE = 0.5
BETA_ONE = 0.9
BETA_TWO = 0.999
EPSILON = 1e-06
DECAY = 0.01
EMA_KEEP = 0.75

MESH = pl.DeviceIdType.MESH
F32 = jnp.float32
BF16 = jnp.bfloat16
STAGES = 1
CHUNK = IMG * IMG // STAGES
LANES = 128
AHEAD = 5
ORDER = (2, 1, 3)
EARLY = 3
LOADS = 1
CHIP_AT = 1
PIECES = 4


def dot(left, right):
    return jnp.dot(left, right, preferred_element_type=F32)


def dot_nt(left, right, precision=None):
    return lax.dot_general(
        left, right, (((1,), (1,)), ((), ())), precision=precision, preferred_element_type=F32
    )


def one_hot(shape, target, axis):
    at = lax.broadcasted_iota(jnp.int32, shape, axis)
    return jnp.where(at == target, 1.0, 0.0).astype(BF16)


def layer_kernel(size, names, *refs):
    r = types.SimpleNamespace(**dict(zip(names, refs)))
    small_loads = []
    for index, name in enumerate(size["small"]):
        small_loads.append(
            pltpu.make_async_copy(getattr(r, name + "_hbm"), getattr(r, name), r.small_sem.at[index])
        )
    n, batch, cl, tl, rl = size["n"], size["batch"], size["cl"], size["tl"], size["rl"]
    fused, group = size["fused"], size["group"]
    slots = batch // n
    chans, touts, regs = n * cl, n * tl, n * rl
    pixels = IMG * IMG
    cells = pixels // 4
    me = lax.axis_index("chan")
    row = lax.axis_index("dp")
    core, chip, pairs = row % 2, row // 2, group // 2
    held, send = r.held, r.send

    def beside(step):
        if n & (n - 1):
            return lax.rem(me + step, n)
        other, bit = me, 1
        while bit < n:
            if step & bit:
                other = other + bit - 2 * bit * ((me // bit) % 2)
            bit *= 2
        return other

    partners = ORDER if n == 4 else range(1, n)

    def at_chan(index):
        return {"chan": index}

    def at_row(index):
        return {"dp": index}

    def remote(src, dst, out_sem, in_sem, device):
        return pltpu.make_async_remote_copy(
            src, dst, out_sem, in_sem, device_id=device, device_id_type=MESH
        )

    greeted = [at_chan(beside(step)) for step in range(1, n)]
    if fused:
        greeted += [at_row(lax.rem(row + step, group)) for step in range(1, group)]

    sources = {
        "images": (r.images, r.raw, None),
        "swin": (r.swin, r.swin_wide, LANES),
        "twin": (r.twin, r.twin_wide, LANES),
        "pwin": (r.pwin, r.pwin_wide, LANES),
        "cot": (r.cot, r.raw_cot, None),
    }
    loads, count = {}, 0
    for name, (src, dst, lanes) in sources.items():
        loads[name] = []
        for j in range(dst.shape[0] if lanes else 1):
            pair = (src.at[:, pl.ds(j * LANES, LANES)], dst.at[j]) if lanes else (src, dst)
            loads[name].append(pltpu.make_async_copy(*pair, r.load_sem.at[count]))
            count += 1

    def start_load(*names):
        for name in names:
            for copy in loads[name]:
                copy.start()

    if LOADS == 0:
        start_load(*sources)
    else:
        start_load("images", "swin")

    for copy in small_loads:
        copy.start()

    def wait_load(name):
        for copy in loads[name]:
            copy.wait()

    barrier = pltpu.get_barrier_semaphore()
    for device in greeted:
        pl.semaphore_signal(barrier, inc=1, device_id=device, device_id_type=MESH)

    if fused:
        depth = r.student_t.shape[1]

        def block(index):
            return pl.ds(pl.multiple_of(index * depth, 16), depth)

        mine = block(row)
        filter_z = [
            remote(
                r.filters.at[me, mine],
                r.filters.at[me, mine],
                r.fz_send.at[step],
                r.fz_recv.at[step],
                at_chan(beside(step)),
            )
            for step in range(1, n)
        ]
        if n == 4:
            passed = beside(2)
            filter_z[2] = remote(
                r.filters.at[passed, mine],
                r.filters.at[passed, mine],
                r.fz_send.at[3],
                r.fz_recv.at[3],
                at_chan(beside(1)),
            )

    def in_copies(slot, step, part):
        to = beside(step)
        rows = pl.ds(0, 2 * cl) if part == 0 else pl.ds(2 * cl, tl)
        copies = [
            remote(
                send.at[slot, to, rows],
                held.at[slot, me, rows],
                r.in_send.at[slot, part, step],
                r.in_recv.at[slot, part, step],
                at_chan(to),
            )
        ]
        if part == 1:
            copies.append(
                remote(
                    r.send_pool.at[slot, to],
                    r.held_pool.at[slot, me],
                    r.pool_in_send.at[slot, step],
                    r.pool_in_recv.at[slot, step],
                    at_chan(to),
                )
            )
        return copies

    def start_in(slot, part):
        for step in partners:
            for copy in in_copies(slot, step, part):
                copy.start()

    def wait_in(slot, part):
        for step in partners:
            for copy in in_copies(slot, step, part):
                copy.wait_recv()

    def start_later(slot, part):
        later = slot + (part + AHEAD) // 2
        pl.when(later < slots)(lambda: start_in(later, (part + AHEAD) % 2))

    def own_copies(slot):
        return (
            pltpu.make_async_copy(send.at[slot, me], held.at[slot, me], r.own_sem.at[slot, 0]),
            pltpu.make_async_copy(
                r.send_pool.at[slot, me], r.held_pool.at[slot, me], r.own_sem.at[slot, 1]
            ),
        )

    def lanes_of(index):
        return pl.ds(pl.multiple_of(index * cl, cl), cl)

    def out_copies(slot, step):
        to = beside(step)
        return (
            remote(
                r.low_part.at[slot, lanes_of(to)],
                r.grad_land.at[me * slots + slot],
                r.out_send.at[slot, step],
                r.out_recv.at[slot, step],
                at_chan(to),
            ),
            remote(
                r.pool_part.at[slot, lanes_of(to)],
                r.pool_land.at[me * slots + slot],
                r.pool_out_send.at[slot, step],
                r.pool_out_recv.at[slot, step],
                at_chan(to),
            ),
        )

    def own_out(slot):
        here = me * slots + slot
        return (
            pltpu.make_async_copy(
                r.low_part.at[slot, lanes_of(me)], r.grad_land.at[here], r.own_out_sem.at[slot, 0]
            ),
            pltpu.make_async_copy(
                r.pool_part.at[slot, lanes_of(me)], r.pool_land.at[here], r.own_out_sem.at[slot, 1]
            ),
        )

    def start_out(slot):
        for step in partners:
            for copy in out_copies(slot, step):
                copy.start()

    def land(slot):
        for step in partners:
            for copy in out_copies(slot, step):
                copy.wait_recv()
        for copy in own_out(slot):
            copy.wait()
        for src, dst in ((r.grad_land, r.wide), (r.pool_land, r.cot_wide)):
            for z in range(n):
                for j in range(dst.shape[0]):
                    part = src[z * slots + slot, :, j * LANES : (j + 1) * LANES].astype(F32)
                    dst[j, pl.ds(z * slots + slot, cl, stride=batch), :] = part

    out_order = {"early": range(0, EARLY), "mid": range(EARLY, slots - 1), "late": range(slots - 1, slots)}

    def start_outs(when):
        for slot in out_order[when]:
            start_out(slot)

    def prepare(slot, part):
        if part == 0:
            pieces = ((r.wide, send, 0, cl), (r.swin_wide, send, cl, cl))
        else:
            pieces = (
                (r.twin_wide, send, 2 * cl, tl),
                (r.pwin_wide, r.send_pool, 0, cl),
                (r.cot_wide, r.send_pool, cl, cl),
            )
        for to in range(n):
            first_row = to * slots + slot
            for src, dst, first, rows in pieces:
                for j in range(src.shape[0]):
                    dst[slot, to, first : first + rows, j * LANES : (j + 1) * LANES] = (
                        src[j, pl.ds(first_row, rows, stride=batch), :].astype(F32).astype(BF16)
                    )

    def prepare_slot(slot, carry):
        for part in range(2):
            prepare(slot, part)
            pl.when(2 * slot + part < AHEAD)(functools.partial(start_in, slot, part))
        for copy in own_copies(slot):
            copy.start()
        return carry

    for copy in small_loads:
        copy.wait()
    wait_load("images")
    for j in range(r.wide.shape[0]):
        r.wide[j] = r.raw[:, j * LANES : (j + 1) * LANES].astype(F32)
    wait_load("swin")
    if LOADS == 1:
        start_load("twin", "pwin", "cot")
    prepare(0, 0)
    pl.semaphore_wait(barrier, len(greeted))
    start_in(0, 0)
    if fused:
        r.flat[...] = jnp.zeros_like(r.flat)
        r.flat[0 : 2 * cl, 0:depth] = r.student_t[...]
        r.flat[2 * cl : 2 * cl + rl, 0:depth] = r.regress_t[...]
        r.filters[me, mine, 0:LANES] = r.flat[...].T[0:depth, :].astype(BF16)
        r.teach_flat[...] = jnp.zeros_like(r.teach_flat)
        r.teach_flat[0 : 2 * tl, :] = r.teacher_t[...].astype(F32)
        r.teach_cols[...] = r.teach_flat[...].T
        r.filters[me, mine, LANES:] = r.teach_cols[mine, :].astype(BF16)
        for copy in filter_z[:2] if n == 4 else filter_z:
            copy.start()
    for name in ("twin", "pwin", "cot"):
        wait_load(name)
    for j in range(r.cot_wide.shape[0]):
        r.cot_wide[j] = r.raw_cot[:, j * LANES : (j + 1) * LANES].astype(F32)
    prepare(0, 1)
    start_in(0, 1)
    for copy in own_copies(0):
        copy.start()
    if fused and n == 4:
        filter_z[1].wait_recv()
        filter_z[2].start()
    lax.fori_loop(1, slots, prepare_slot, 0)

    lane = lax.broadcasted_iota(jnp.int32, (16, pixels), 1)
    row_of, col_of = lane // IMG, lane % IMG
    for which, bad in enumerate((row_of == 0, row_of == IMG - 1, col_of == 0, col_of == IMG - 1)):
        r.edge[which] = jnp.where(bad, 0.0, 1.0).astype(BF16)
    spot = lax.broadcasted_iota(jnp.int32, (1, pixels), 1)
    home = (spot // (2 * IMG)) * (IMG // 2) + (spot % IMG) // 2
    r.up[...] = one_hot((cells, pixels), home, 0)
    r.sgrad[...] = jnp.zeros_like(r.sgrad)
    r.rgrad[...] = jnp.zeros_like(r.rgrad)

    if fused:
        picked = 2 * cl + rl + 2 * tl
        at = lax.broadcasted_iota(jnp.int32, (picked, 1), 0)
        teach = at - 2 * cl - rl
        lane_at = jnp.where(
            at < 2 * cl,
            2 * (at % cl) + at // cl,
            jnp.where(at < 2 * cl + rl, at, LANES + 2 * (teach % tl) + teach // tl),
        )
        r.gather_rows[...] = one_hot((picked, r.filters.shape[2]), lane_at, 1)
        for z in range(n):
            at = lax.broadcasted_iota(jnp.int32, (LANES, 1), 0)
            col_at = jnp.where(
                at < 2 * cl,
                (at % 2) * chans + z * cl + at // 2,
                jnp.where(at < 2 * cl + rl, 2 * chans + z * rl + at - 2 * cl, -1),
            )
            r.spread[z] = one_hot((LANES, r.spread.shape[2]), col_at, 1)

        for copy in (filter_z[0], filter_z[2]) if n == 4 else filter_z:
            copy.wait_recv()

        def filter_chip(step):
            to = lax.rem(chip + step, pairs)
            return remote(
                r.filters.at[:, mine],
                r.filters.at[:, mine],
                r.fx_send.at[step],
                r.fx_recv.at[step],
                at_row(2 * to + core),
            )

        def filter_core(step):
            rows = block(2 * lax.rem(chip + pairs - step, pairs) + core)
            return remote(
                r.filters.at[:, rows],
                r.filters.at[:, rows],
                r.fc_send.at[step],
                r.fc_recv.at[step],
                at_row(row + 1 - 2 * core),
            )

        for step in range(1, pairs):
            filter_chip(step).start()
        filter_core(0).start()
        for step in range(1, pairs):
            filter_chip(step).wait_recv()
            filter_core(step).start()
        for step in range(pairs):
            filter_core(step).wait_recv()

        for z in range(n):
            rows_of = dot_nt(r.gather_rows[...], r.filters[z]).astype(BF16)
            first = 0
            for dst, start, many in (
                (r.w_in, z * cl, cl),
                (r.w_in, chans + z * cl, cl),
                (r.w_reg, z * rl, rl),
                (r.w_in, 2 * chans + z * tl, tl),
                (r.w_in, 2 * chans + touts + z * tl, tl),
            ):
                dst[start : start + many, :] = rows_of[first : first + many, :]
                first += many
        for tap in range(9):
            rows = slice((8 - tap) * chans, (9 - tap) * chans)
            total = dot(r.filters[0, rows, 0:LANES], r.spread[0])
            for z in range(1, n):
                total += dot(r.filters[z, rows, 0:LANES], r.spread[z])
            total = total.astype(BF16)
            r.w_in_back[:, tap * 2 * chans : (tap + 1) * 2 * chans] = total[:, 0 : 2 * chans]
            r.w_reg_back[:, tap * regs : (tap + 1) * regs] = total[:, 2 * chans : 2 * chans + regs]

    def columns(load, rows, dst, stage):
        many = rows // (16 * STAGES)
        for g in range(many):
            first = pl.multiple_of((stage * many + g) * 16, 16)
            base = load(first)
            for ky in range(3):
                if ky == 1:
                    moved = base
                else:
                    moved = pltpu.roll(base, (pixels - IMG * (ky - 1)) % pixels, 1)
                    moved = moved * r.edge[0 if ky == 0 else 1]
                for kx in range(3):
                    if kx == 1:
                        tap = moved
                    else:
                        tap = pltpu.roll(moved, (pixels - (kx - 1)) % pixels, 1)
                        tap = tap * r.edge[2 if kx == 0 else 3]
                    dst[pl.ds((3 * ky + kx) * rows + first, 16), :] = tap

    def stages(*bodies):
        def one(stage, carry):
            for body in bodies:
                body(stage)
            return carry

        lax.fori_loop(0, STAGES, one, 0)

    def chunks(body):
        def one(stage):
            body(pl.ds(pl.multiple_of(stage * CHUNK, CHUNK), CHUNK))

        return one

    def add_grads(grads, left, right):
        many = grads.shape[0] // STAGES

        def one(stage):
            rows = pl.ds(pl.multiple_of(stage * many, 16), many)
            grads[rows, :] += dot_nt(left[rows, :], right[...])

        return one

    def corner_of(here):
        at = lax.broadcasted_iota(jnp.int32, (1, CHUNK), 1)
        return (2 * ((at // IMG) % 2) + at % 2).astype(F32)

    if fused:
        parts = ((r.rgrad, r.rc_send, r.rc_recv, r.rx_send, r.rx_recv),
                 (r.sgrad, r.sc_send, r.sc_recv, r.sx_send, r.sx_recv))

        def core_copy(which):
            return remote(
                parts[which][1],
                parts[which][2],
                r.core_send.at[which],
                r.core_recv.at[which],
                at_row(row + 1 - 2 * core),
            )

        def start_core(which):
            grads, out = parts[which][:2]
            for pair in range(pairs):
                out[pair] = grads[block(2 * pair + 1 - core), :].astype(BF16)
            core_copy(which).start()

        def chip_copy(which, step):
            return remote(
                parts[which][3].at[step],
                parts[which][4].at[step],
                r.chip_send.at[which, step],
                r.chip_recv.at[which, step],
                at_row(2 * lax.rem(chip + step, pairs) + core),
            )

        def chan_copy(step):
            return remote(
                r.zs_send.at[step],
                r.zs_recv.at[step],
                r.chan_send.at[step],
                r.chan_recv.at[step],
                at_chan(beside(step)),
            )

        def row_norm(step):
            return remote(
                r.part_rows.at[row],
                r.part_rows.at[row],
                r.rn_send.at[step],
                r.rn_recv.at[step],
                at_row(lax.rem(row + step, group)),
            )

        def chan_norm(step):
            return remote(
                r.part_chans.at[me],
                r.part_chans.at[me],
                r.cn_send.at[step],
                r.cn_recv.at[step],
                at_chan(beside(step)),
            )

    def step_chip(which):
        grads, _, came, out, _ = parts[which]
        cols = slice(2 * chans, 2 * chans + regs) if which == 0 else slice(0, 2 * chans)
        core_copy(which).wait_recv()
        for step in range(1, pairs):
            to = lax.rem(chip + step, pairs)
            out[step] = (grads[block(2 * to + core), :] + came[to].astype(F32)).astype(BF16)
            chip_copy(which, step).start()
        r.whole_grad[:, cols] = grads[block(row), :] + came[chip].astype(F32)

    def image(slot, carry):
        last = slot == slots - 1
        wait_in(slot, 0)
        start_later(slot, 0)
        for copy in own_copies(slot):
            copy.wait()

        def image_rows(first):
            return held[slot, first // cl, pl.ds(pl.multiple_of(first % cl, 16), 16), :]

        def picked(here):
            return held[slot, :, cl : 2 * cl, here].reshape(chans, CHUNK).astype(F32) > 0.5

        def head(here):
            pre = dot(r.w_in[0 : 2 * chans, :], r.x_cols[:, here])
            r.out_low[:, here] = jnp.where(picked(here), pre[chans:], pre[:chans]).astype(BF16)

        def teach(here):
            r.teach[:, here] = dot(r.w_in[2 * chans :, :], r.x_cols[:, here])

        def guess(here):
            r.guess[:, here] = dot(r.w_reg[...], r.o_cols[:, here])

        def pooling(here):
            cell_win = r.held_pool[slot, :, 0:cl, :].reshape(chans, cells)
            cell_cot = r.held_pool[slot, :, cl : 2 * cl, :].reshape(chans, cells)
            chosen = dot(cell_win, r.up[:, here]) == corner_of(here)
            spread = dot(cell_cot, r.up[:, here])
            r.pool_back[:, here] = jnp.where(chosen, spread, 0.0).astype(BF16)
            kept = jnp.where(chosen, r.out_low[:, here].astype(F32), 0.0).astype(BF16)
            part = dot_nt(kept, r.up[:, here])
            r.pool_part[slot] = (r.pool_part[slot].astype(F32) + part).astype(BF16)

        def hints(here):
            pick = held[slot, :, 2 * cl :, here].reshape(touts, CHUNK).astype(F32)
            target = jnp.where(pick > 0.5, r.teach[touts:, here], r.teach[:touts, here])
            weight = scale * r.mask[pl.ds(me * slots + slot, 1), here].astype(F32)
            r.hint[:, here] = (weight * (r.guess[:, here] - target)).astype(BF16)

        def back(here):
            total = dot(r.w_reg_back[...], r.h_cols[:, here]) + r.pool_back[:, here].astype(F32)
            pick = picked(here)
            r.pre_grad[0:chans, here] = jnp.where(pick, 0.0, total).astype(BF16)
            r.pre_grad[chans:, here] = jnp.where(pick, total, 0.0).astype(BF16)

        def image_back(here):
            r.low_part[slot, :, here] = dot(r.w_in_back[...], r.p_cols[:, here]).astype(BF16)

        def columns_of(src, dst):
            rows = src.shape[0]
            return lambda stage: columns(lambda first: src[pl.ds(first, 16), :], rows, dst, stage)

        spot_mask = r.mask[pl.ds(me * slots + slot, 1), :].astype(F32)
        count = jnp.sum(spot_mask, axis=1, keepdims=True)
        scale = HINT_WEIGHT * (pixels / count)
        r.pool_part[slot] = jnp.zeros((chans, cells), BF16)

        stages(lambda stage: columns(image_rows, chans, r.x_cols, stage))
        stages(chunks(head))
        stages(chunks(teach), columns_of(r.out_low, r.o_cols))
        stages(chunks(guess))
        wait_in(slot, 1)
        start_later(slot, 1)
        pl.when(last)(lambda: start_outs("early"))
        stages(chunks(hints))
        stages(add_grads(r.rgrad, r.o_cols, r.hint), columns_of(r.hint, r.h_cols))
        if fused:
            pl.when(last)(lambda: start_core(0))
        stages(chunks(pooling))
        stages(chunks(back))
        if fused and CHIP_AT == 1:
            pl.when(last)(lambda: step_chip(0))
        stages(add_grads(r.sgrad, r.x_cols, r.pre_grad), columns_of(r.pre_grad, r.p_cols))
        if fused:

            def reduce_more():
                start_core(1)
                if CHIP_AT == 0:
                    step_chip(0)

            pl.when(last)(reduce_more)
        stages(chunks(image_back))
        if not fused:

            def start_rest():
                start_outs("mid")
                start_outs("late")

            pl.when(last)(start_rest)
        for copy in own_out(slot):
            copy.start()
        return carry

    if fused:
        r.whole_grad[...] = jnp.zeros_like(r.whole_grad)
    lax.fori_loop(0, slots, image, 0)

    if fused:
        step_chip(1)
        for which, cols in ((0, slice(2 * chans, 2 * chans + regs)), (1, slice(0, 2 * chans))):
            came = parts[which][4]
            for step in range(1, pairs):
                chip_copy(which, step).wait_recv()
            total = r.whole_grad[:, cols]
            for step in range(1, pairs):
                total += came[step].astype(F32)
            r.whole_grad[:, cols] = total
        low_grad = r.whole_grad[...].astype(BF16)
        for step in partners:
            r.zs_send[step] = dot_nt(low_grad, r.spread[beside(step)]).astype(BF16)
            chan_copy(step).start()
        start_outs("mid")
        total = dot_nt(
            r.whole_grad[...], r.spread[me].astype(F32), precision=lax.Precision.HIGHEST
        )
        for slot in out_order["early"]:
            land(slot)
        for step in partners:
            chan_copy(step).wait_recv()
        for step in partners:
            total += r.zs_recv[step].astype(F32)
        r.tall[0:depth, :] = total
        total = r.tall[...].T[:, 0:depth]
        r.grad_sum[...] = total
        student, regress = r.student_t[...], r.regress_t[...]
        upd_s = lamb_update(student, total[0 : 2 * cl], r.mom_student[...], r.sq_student[...])[2]
        upd_r = lamb_update(
            regress, total[2 * cl : 2 * cl + rl], r.mom_regress[...], r.sq_regress[...]
        )[2]
        place = lax.broadcasted_iota(jnp.int32, (8, LANES), 1)
        tile = jnp.zeros((8, LANES), F32)
        for index, value in enumerate((student, upd_s, regress, upd_r)):
            square = jnp.sum(jnp.sum(value * value, axis=1, keepdims=True), axis=0, keepdims=True)
            tile = jnp.where(place == index, square, tile)
        r.part_chans[me] = tile
        for step in partners:
            chan_norm(step).start()
        start_outs("late")
        for slot in out_order["mid"]:
            land(slot)
        for step in partners:
            chan_norm(step).wait_recv()
        tile = r.part_chans[0]
        for index in range(1, n):
            tile += r.part_chans[index]
        r.part_rows[row] = tile
        for step in range(1, group):
            row_norm(step).start()
        for step in range(1, group):
            row_norm(step).wait_recv()
        tile = r.part_rows[0]
        for index in range(1, group):
            tile += r.part_rows[index]
        r.sums[...] = tile

    for slot in out_order["late"] if fused else range(slots):
        land(slot)
    for src, dst in ((r.wide, r.grad_out), (r.cot_wide, r.pool_out)):
        for j in range(src.shape[0]):
            dst[:, j * LANES : (j + 1) * LANES] = src[j].astype(BF16)

    def finish(slot, carry):
        for step in partners:
            for copy in (*in_copies(slot, step, 0), *in_copies(slot, step, 1), *out_copies(slot, step)):
                copy.wait_send()
        return carry

    lax.fori_loop(0, slots, finish, 0)
    if fused:
        for step in partners:
            filter_z[step - 1].wait_send()
            chan_copy(step).wait_send()
            chan_norm(step).wait_send()
        for step in range(1, group):
            row_norm(step).wait_send()
        for step in range(pairs):
            filter_core(step).wait_send()
        for step in range(1, pairs):
            filter_chip(step).wait_send()
        for which in range(2):
            core_copy(which).wait_send()
            for step in range(1, pairs):
                chip_copy(which, step).wait_send()


def lamb_update(weights, grads, moment, second):
    moment_new = BETA_ONE * moment + (1.0 - BETA_ONE) * grads
    second_new = BETA_TWO * second + (1.0 - BETA_TWO) * grads * grads
    moment_hat = moment_new / (1.0 - BETA_ONE**STEP)
    second_hat = second_new / (1.0 - BETA_TWO**STEP)
    update = moment_hat / (jnp.sqrt(second_hat) + EPSILON) + DECAY * weights
    return (moment_new, second_new, update)


def layer_pass(n, group, fused, arrays):
    cl, batch, pixels = arrays["images"].shape
    tl = arrays["twin"].shape[0]
    cells = arrays["pwin"].shape[2]
    slots = batch // n
    chans = n * cl
    if fused:
        rl, depth = arrays["regress_t"].shape
    else:
        rl = arrays["w_reg"].shape[0] // n
    regs, touts, pairs = n * rl, n * tl, group // 2
    size = dict(n=n, batch=batch, cl=cl, tl=tl, rl=rl, fused=fused, group=group)
    vmem = pl.BlockSpec(memory_space=pltpu.VMEM)
    in_hbm = ("images", "swin", "twin", "pwin", "cot")
    ins = {
        name: a.reshape(a.shape[0] * a.shape[1], a.shape[2]) if name in in_hbm else a
        for name, a in arrays.items()
    }
    outs = {
        "pool_out": jax.ShapeDtypeStruct((cl * batch, cells), BF16),
        "grad_out": jax.ShapeDtypeStruct((cl * batch, pixels), BF16),
    }
    small = tuple(name for name in ins if name not in in_hbm)
    size["small"] = small
    grads = {"sgrad": (9 * chans, 2 * chans), "rgrad": (9 * chans, regs)}
    dma = lambda *shape: pltpu.SemaphoreType.DMA(shape)
    scratch = {
        "raw": pltpu.VMEM((cl * batch, pixels), BF16),
        "raw_cot": pltpu.VMEM((cl * batch, cells), BF16),
        "wide": pltpu.VMEM((pixels // LANES, cl * batch, LANES), F32),
        "swin_wide": pltpu.VMEM((pixels // LANES, cl * batch, LANES), jnp.int32),
        "twin_wide": pltpu.VMEM((pixels // LANES, tl * batch, LANES), jnp.int32),
        "pwin_wide": pltpu.VMEM((cells // LANES, cl * batch, LANES), jnp.int32),
        "cot_wide": pltpu.VMEM((cells // LANES, cl * batch, LANES), F32),
        "load_sem": dma(2 + 2 * (pixels // LANES) + cells // LANES),
        "send": pltpu.VMEM((slots, n, 2 * cl + tl, pixels), BF16),
        "send_pool": pltpu.VMEM((slots, n, 2 * cl, cells), BF16),
        "held": pltpu.VMEM((slots, n, 2 * cl + tl, pixels), BF16),
        "held_pool": pltpu.VMEM((slots, n, 2 * cl, cells), BF16),
        "low_part": pltpu.VMEM((slots, chans, pixels), BF16),
        "pool_part": pltpu.VMEM((slots, chans, cells), BF16),
        "pool_land": pltpu.VMEM((batch, cl, cells), BF16),
        "grad_land": pltpu.VMEM((batch, cl, pixels), BF16),
        "edge": pltpu.VMEM((4, 16, pixels), BF16),
        "up": pltpu.VMEM((cells, pixels), BF16),
        "x_cols": pltpu.VMEM((9 * chans, pixels), BF16),
        "o_cols": pltpu.VMEM((9 * chans, pixels), BF16),
        "h_cols": pltpu.VMEM((9 * regs, pixels), BF16),
        "p_cols": pltpu.VMEM((9 * 2 * chans, pixels), BF16),
        "out_low": pltpu.VMEM((chans, pixels), BF16),
        "pool_back": pltpu.VMEM((chans, pixels), BF16),
        "hint": pltpu.VMEM((regs, pixels), BF16),
        "teach": pltpu.VMEM((2 * touts, pixels), F32),
        "guess": pltpu.VMEM((regs, pixels), F32),
        "pre_grad": pltpu.VMEM((2 * chans, pixels), BF16),
        "own_sem": dma(slots, 2),
        "own_out_sem": dma(slots, 2),
    }
    scratch["in_send"] = dma(slots, 2, n)
    scratch["in_recv"] = dma(slots, 2, n)
    for name in ("pool_in", "out", "pool_out"):
        scratch[name + "_send"] = dma(slots, n)
        scratch[name + "_recv"] = dma(slots, n)
    if fused:
        cols = 2 * chans + 2 * LANES
        tall = -(-depth // LANES) * LANES
        outs["grad_sum"] = jax.ShapeDtypeStruct((LANES, depth), F32)
        outs["sums"] = jax.ShapeDtypeStruct((8, LANES), F32)
        scratch.update({name: pltpu.VMEM(shape, F32) for name, shape in grads.items()})
        scratch.update(
            {
                "flat": pltpu.VMEM((LANES, tall), F32),
                "tall": pltpu.VMEM((tall, LANES), F32),
                "teach_flat": pltpu.VMEM((LANES, 9 * chans), F32),
                "teach_cols": pltpu.VMEM((9 * chans, LANES), F32),
                "filters": pltpu.VMEM((n, 9 * chans, 2 * LANES), BF16),
                "gather_rows": pltpu.VMEM((2 * cl + rl + 2 * tl, 2 * LANES), BF16),
                "spread": pltpu.VMEM((n, LANES, cols), BF16),
                "w_in": pltpu.VMEM((2 * chans + 2 * touts, 9 * chans), BF16),
                "w_reg": pltpu.VMEM((regs, 9 * chans), BF16),
                "w_reg_back": pltpu.VMEM((chans, 9 * regs), BF16),
                "w_in_back": pltpu.VMEM((chans, 9 * 2 * chans), BF16),
                "rc_send": pltpu.VMEM((pairs, depth, regs), BF16),
                "rc_recv": pltpu.VMEM((pairs, depth, regs), BF16),
                "rx_send": pltpu.VMEM((pairs, depth, regs), BF16),
                "rx_recv": pltpu.VMEM((pairs, depth, regs), BF16),
                "sc_send": pltpu.VMEM((pairs, depth, 2 * chans), BF16),
                "sc_recv": pltpu.VMEM((pairs, depth, 2 * chans), BF16),
                "sx_send": pltpu.VMEM((pairs, depth, 2 * chans), BF16),
                "sx_recv": pltpu.VMEM((pairs, depth, 2 * chans), BF16),
                "whole_grad": pltpu.VMEM((depth, cols), F32),
                "zs_send": pltpu.VMEM((n, depth, LANES), BF16),
                "zs_recv": pltpu.VMEM((n, depth, LANES), BF16),
                "part_rows": pltpu.VMEM((group, 8, LANES), F32),
                "part_chans": pltpu.VMEM((n, 8, LANES), F32),
                "core_send": dma(2),
                "core_recv": dma(2),
                "chip_send": dma(2, pairs),
                "chip_recv": dma(2, pairs),
            }
        )
        for name, many in (
            ("fz", n), ("fx", pairs), ("fc", pairs), ("chan", n), ("rn", group), ("cn", n)
        ):
            scratch[name + "_send"] = dma(many)
            scratch[name + "_recv"] = dma(many)
    else:
        outs.update({name: jax.ShapeDtypeStruct(shape, F32) for name, shape in grads.items()})
    flops = 2 * slots * pixels * 9 * chans * (3 * 2 * chans + 2 * touts + 3 * regs)
    scratch.update({name: pltpu.VMEM(ins[name].shape, ins[name].dtype) for name in small})
    scratch["small_sem"] = dma(len(small))
    in_names = tuple(name + "_hbm" if name in small else name for name in ins)
    names = in_names + tuple(outs) + tuple(scratch)
    return pl.pallas_call(
        functools.partial(layer_kernel, size, names),
        out_shape=list(outs.values()),
        in_specs=[pl.BlockSpec(memory_space=pl.ANY)] * len(ins),
        out_specs=[vmem] * len(outs),
        scratch_shapes=list(scratch.values()),
        compiler_params=pltpu.CompilerParams(
            collective_id=0, has_side_effects=True, vmem_limit_bytes=58 << 20
        ),
        cost_estimate=pl.CostEstimate(flops=flops, bytes_accessed=16 << 20, transcendentals=0),
        name="layer",
    )(*ins.values())


def final_kernel(*refs):
    pool_in, grad_in = refs[0:2]
    pooled, image_grad, new_s, new_r, trust = refs[12], refs[13], refs[14:19], refs[19:24], refs[24]
    held, middle, big_sem, small_sem = refs[25:35], refs[35:37], refs[37], refs[38]
    big, onward = [], []
    for index, path in enumerate(((pool_in, middle[0], pooled), (grad_in, middle[1], image_grad))):
        many = path[0].shape[0] // PIECES
        for piece in range(PIECES):
            at = pl.ds(piece * many, many)
            views = [ref.at[at] for ref in path]
            sems = [big_sem.at[index, piece, side] for side in range(2)]
            big.append(pltpu.make_async_copy(views[0], views[1], sems[0]))
            onward.append(pltpu.make_async_copy(views[1], views[2], sems[1]))
    small = [
        pltpu.make_async_copy(src, dst, small_sem.at[index])
        for index, (src, dst) in enumerate(zip(refs[2:12], held))
    ]
    for copy in big + small:
        copy.start()
    for copy, after in zip(big, onward):
        copy.wait()
        after.start()
    for copy in small:
        copy.wait()
    grad_sum, sums, student, regress, mom_s, sq_s, mom_r, sq_r, ema_s, ema_r = held
    norm = [jnp.sqrt(sums[0:1, k : k + 1]) for k in range(4)]
    souts, regs = student.shape[0], regress.shape[0]
    for weights, grads, moment, second, average, outs, top, bottom in (
        (student, grad_sum[0:souts, :], mom_s, sq_s, ema_s, new_s, norm[0], norm[1]),
        (regress, grad_sum[souts : souts + regs, :], mom_r, sq_r, ema_r, new_r, norm[2], norm[3]),
    ):
        moment_new, second_new, update = lamb_update(
            weights[...], grads, moment[...], second[...]
        )
        new = weights[...] - LEARN_RATE * (top / bottom) * update
        outs[0][...] = new
        outs[1][...] = moment_new
        outs[2][...] = second_new
        outs[3][...] = EMA_KEEP * average[...] + (1.0 - EMA_KEEP) * new
        outs[4][...] = new.astype(BF16)
    across = lax.broadcasted_iota(jnp.int32, (2, 2), 1)
    down = lax.broadcasted_iota(jnp.int32, (2, 2), 0)
    first = jnp.where(across == 0, norm[0], norm[1])
    trust[...] = jnp.where(down == 0, first, jnp.where(across == 0, norm[2], norm[3]))
    for copy in onward:
        copy.wait()


def final_pass(pooled, image_grad, grad_sum, sums, *small):
    student, regress = small[0:2]
    outs = [jax.ShapeDtypeStruct(a.shape, BF16) for a in (pooled, image_grad)]
    for a in (student, regress):
        outs += [jax.ShapeDtypeStruct(a.shape, F32)] * 4 + [jax.ShapeDtypeStruct(a.shape, BF16)]
    outs.append(jax.ShapeDtypeStruct((2, 2), F32))
    vmem, hbm = (pl.BlockSpec(memory_space=space) for space in (pltpu.VMEM, pl.ANY))
    kept = (grad_sum, sums, *small)
    results = pl.pallas_call(
        final_kernel,
        out_shape=outs,
        in_specs=[hbm] * (2 + len(kept)),
        out_specs=[hbm] * 2 + [vmem] * (len(outs) - 2),
        scratch_shapes=[pltpu.VMEM(a.shape, a.dtype) for a in (*kept, pooled, image_grad)]
        + [pltpu.SemaphoreType.DMA((2, PIECES, 2)), pltpu.SemaphoreType.DMA((len(kept),))],
        compiler_params=pltpu.CompilerParams(vmem_limit_bytes=58 << 20),
        name="final",
    )(pooled, image_grad, *kept)
    return (*results[0:2], *(a.T for a in results[2:12]), results[12])


def split_pieces(weights):
    rows, cols = weights.shape
    return weights.reshape(rows, cols // 2, 2).transpose(2, 1, 0).reshape(cols, rows)


def back_weights(weights, outs):
    channels = weights.shape[0] // 9
    taps = weights.reshape(9, channels, outs)[::-1]
    return taps.transpose(1, 0, 2).reshape(channels, 9 * outs)


def gathered_filters(student_master, regress_master, teacher_weight):
    student_full = lax.all_gather(student_master.astype(BF16), "dp", axis=0, tiled=True)
    student_full = lax.all_gather(student_full, "chan", axis=1, tiled=True)
    regress_full = lax.all_gather(regress_master.astype(BF16), "dp", axis=0, tiled=True)
    regress_full = lax.all_gather(regress_full, "chan", axis=1, tiled=True)
    teacher_full = lax.all_gather(teacher_weight, "chan", axis=1, tiled=True)
    student_rows = split_pieces(student_full)
    return {
        "w_in": jnp.concatenate([student_rows, split_pieces(teacher_full)], axis=0),
        "w_reg": regress_full.T,
        "w_reg_back": back_weights(regress_full, regress_full.shape[1]),
        "w_in_back": back_weights(student_rows.T, student_full.shape[1]),
    }


def scattered_grads(student_part, regress_part):
    souts = student_part.shape[1]
    student_part = student_part.reshape(-1, 2, souts // 2).transpose(0, 2, 1).reshape(-1, souts)
    student_grad = lax.psum_scatter(student_part, "dp", scatter_dimension=0, tiled=True)
    student_grad = lax.psum_scatter(student_grad, "chan", scatter_dimension=1, tiled=True)
    regress_grad = lax.psum_scatter(regress_part, "dp", scatter_dimension=0, tiled=True)
    regress_grad = lax.psum_scatter(regress_grad, "chan", scatter_dimension=1, tiled=True)
    return student_grad, regress_grad


def on_device(
    n,
    group,
    images,
    student_master,
    regress_master,
    teacher_weight,
    student_win,
    teacher_win,
    pool_win,
    hint_mask,
    cotangent,
    mom_student,
    sq_student,
    ema_student,
    mom_regress,
    sq_regress,
    ema_regress,
):
    image_like = lambda a: a.reshape(images.shape)
    pool_win_like = lambda a: a.reshape(pool_win.shape)
    depth = student_master.shape[0]
    fused = group % 2 == 0 and depth % 16 == 0
    arrays = dict(
        images=images,
        swin=student_win,
        twin=teacher_win,
        pwin=pool_win,
        cot=cotangent,
        mask=hint_mask,
    )
    if fused:
        small = (student_master, regress_master, mom_student, sq_student, mom_regress, sq_regress)
        small = [a.T for a in small]
        names = ("student_t", "regress_t", "mom_student", "sq_student", "mom_regress", "sq_regress")
        arrays.update(zip(names, small))
        parts = layer_pass(n, group, fused, dict(arrays, teacher_t=teacher_weight.T))
        results = final_pass(*parts, *small, ema_student.T, ema_regress.T)
        return (pool_win_like(results[0]), image_like(results[1]), *results[2:])
    arrays.update(gathered_filters(student_master, regress_master, teacher_weight))
    pooled, image_grad, student_part, regress_part = layer_pass(n, group, fused, arrays)
    student_grad, regress_grad = scattered_grads(student_part, regress_part)
    mom_s, sq_s, upd_s = lamb_update(student_master, student_grad, mom_student, sq_student)
    mom_r, sq_r, upd_r = lamb_update(regress_master, regress_grad, mom_regress, sq_regress)
    all_sums = lax.psum(
        jnp.stack([jnp.sum(v * v) for v in (student_master, upd_s, regress_master, upd_r)]),
        ("dp", "chan"),
    )
    norms = jnp.sqrt(all_sums)
    new_student = student_master - LEARN_RATE * (norms[0] / norms[1]) * upd_s
    new_regress = regress_master - LEARN_RATE * (norms[2] / norms[3]) * upd_r
    ema_s = EMA_KEEP * ema_student + (1.0 - EMA_KEEP) * new_student
    ema_r = EMA_KEEP * ema_regress + (1.0 - EMA_KEEP) * new_regress
    return (
        pool_win_like(pooled),
        image_like(image_grad),
        new_student,
        mom_s,
        sq_s,
        ema_s,
        new_student.astype(BF16),
        new_regress,
        mom_r,
        sq_r,
        ema_r,
        new_regress.astype(BF16),
        norms.reshape(2, 2),
    )


def solution(mesh):
    acts = P("chan", "dp", None)
    rows = P("dp", "chan")
    in_specs = (
        (acts, rows, rows, P(None, "chan"))
        + (acts, acts, acts, P("dp", None), acts)
        + (rows,) * 6
    )
    out_specs = (acts, acts) + (rows,) * 10 + (P(),)
    return jax.shard_map(
        functools.partial(on_device, mesh.shape["chan"], mesh.shape["dp"]),
        mesh=mesh,
        in_specs=in_specs,
        out_specs=out_specs,
        check_vma=False,
    )
```

```python
import functools
import types

import jax
import jax.numpy as jnp
from jax import lax
from jax.experimental import pallas as pl
from jax.experimental.pallas import tpu as pltpu
from jax.sharding import PartitionSpec as P

IMG = 32
STEP = 10
HINT_WEIGHT = 0.1
LEARN_RATE = 0.5
BETA_ONE = 0.9
BETA_TWO = 0.999
EPSILON = 1e-06
DECAY = 0.01
EMA_KEEP = 0.75

MESH = pl.DeviceIdType.MESH
F32 = jnp.float32
BF16 = jnp.bfloat16
STAGES = 1
CHUNK = IMG * IMG // STAGES
LANES = 128
AHEAD = 5
NEAR_LATE = 3
OUT_AT = 1
ORDER = (2, 1, 3)
EARLY = 2
LOADS = 1
CHIP_AT = 1


def dot(left, right):
    return jnp.dot(left, right, preferred_element_type=F32)


def dot_nt(left, right, precision=None):
    return lax.dot_general(
        left, right, (((1,), (1,)), ((), ())), precision=precision, preferred_element_type=F32
    )


def one_hot(shape, target, axis):
    at = lax.broadcasted_iota(jnp.int32, shape, axis)
    return jnp.where(at == target, 1.0, 0.0).astype(BF16)


def layer_kernel(size, names, *refs):
    r = types.SimpleNamespace(**dict(zip(names, refs)))
    small_loads = []
    for index, name in enumerate(size["small"]):
        small_loads.append(
            pltpu.make_async_copy(getattr(r, name + "_hbm"), getattr(r, name), r.small_sem.at[index])
        )
    n, batch, cl, tl, rl = size["n"], size["batch"], size["cl"], size["tl"], size["rl"]
    fused, group = size["fused"], size["group"]
    slots = batch // n
    chans, touts, regs = n * cl, n * tl, n * rl
    pixels = IMG * IMG
    cells = pixels // 4
    me = lax.axis_index("chan")
    row = lax.axis_index("dp")
    core, chip, pairs = row % 2, row // 2, group // 2
    held, send = r.held, r.send

    def beside(step):
        if n & (n - 1):
            return lax.rem(me + step, n)
        other, bit = me, 1
        while bit < n:
            if step & bit:
                other = other + bit - 2 * bit * ((me // bit) % 2)
            bit *= 2
        return other

    partners = ORDER if n == 4 else range(1, n)

    def at_chan(index):
        return {"chan": index}

    def at_row(index):
        return {"dp": index}

    def remote(src, dst, out_sem, in_sem, device):
        return pltpu.make_async_remote_copy(
            src, dst, out_sem, in_sem, device_id=device, device_id_type=MESH
        )

    greeted = [at_chan(beside(step)) for step in range(1, n)]
    if fused:
        greeted += [at_row(lax.rem(row + step, group)) for step in range(1, group)]

    sources = {
        "images": (r.images, r.raw, None),
        "swin": (r.swin, r.swin_wide, LANES),
        "twin": (r.twin, r.twin_wide, LANES),
        "pwin": (r.pwin, r.pwin_wide, LANES),
        "cot": (r.cot, r.raw_cot, None),
    }
    loads, count = {}, 0
    for name, (src, dst, lanes) in sources.items():
        loads[name] = []
        for j in range(dst.shape[0] if lanes else 1):
            pair = (src.at[:, pl.ds(j * LANES, LANES)], dst.at[j]) if lanes else (src, dst)
            loads[name].append(pltpu.make_async_copy(*pair, r.load_sem.at[count]))
            count += 1

    def start_load(*names):
        for name in names:
            for copy in loads[name]:
                copy.start()

    if LOADS == 0:
        start_load(*sources)
    else:
        start_load("images", "swin")

    for copy in small_loads:
        copy.start()

    def wait_load(name):
        for copy in loads[name]:
            copy.wait()

    barrier = pltpu.get_barrier_semaphore()
    for device in greeted:
        pl.semaphore_signal(barrier, inc=1, device_id=device, device_id_type=MESH)

    if fused:
        depth = r.student_t.shape[1]

        def block(index):
            return pl.ds(pl.multiple_of(index * depth, 16), depth)

        mine = block(row)
        filter_z = [
            remote(
                r.filters.at[me, mine],
                r.filters.at[me, mine],
                r.fz_send.at[step],
                r.fz_recv.at[step],
                at_chan(beside(step)),
            )
            for step in range(1, n)
        ]
        if n == 4:
            passed = beside(2)
            filter_z[2] = remote(
                r.filters.at[passed, mine],
                r.filters.at[passed, mine],
                r.fz_send.at[3],
                r.fz_recv.at[3],
                at_chan(beside(1)),
            )

    def in_copies(slot, step, part):
        to = beside(step)
        rows = pl.ds(0, 2 * cl) if part == 0 else pl.ds(2 * cl, tl)
        copies = [
            remote(
                send.at[slot, to, rows],
                held.at[slot, me, rows],
                r.in_send.at[slot, part, step],
                r.in_recv.at[slot, part, step],
                at_chan(to),
            )
        ]
        if part == 1:
            copies.append(
                remote(
                    r.send_pool.at[slot, to],
                    r.held_pool.at[slot, me],
                    r.pool_in_send.at[slot, step],
                    r.pool_in_recv.at[slot, step],
                    at_chan(to),
                )
            )
        return copies

    def start_in(slot, part):
        for step in partners:
            for copy in in_copies(slot, step, part):
                copy.start()

    def wait_in(slot, part):
        for step in partners:
            for copy in in_copies(slot, step, part):
                copy.wait_recv()

    def start_later(slot, part):
        later = slot + (part + AHEAD) // 2
        pl.when(later < slots)(lambda: start_in(later, (part + AHEAD) % 2))

    def own_copies(slot):
        return (
            pltpu.make_async_copy(send.at[slot, me], held.at[slot, me], r.own_sem.at[slot, 0]),
            pltpu.make_async_copy(
                r.send_pool.at[slot, me], r.held_pool.at[slot, me], r.own_sem.at[slot, 1]
            ),
        )

    def lanes_of(index):
        return pl.ds(pl.multiple_of(index * cl, cl), cl)

    def out_copies(slot, step):
        to = beside(step)
        return (
            remote(
                r.low_part.at[slot, lanes_of(to)],
                r.grad_land.at[me * slots + slot],
                r.out_send.at[slot, step],
                r.out_recv.at[slot, step],
                at_chan(to),
            ),
            remote(
                r.pool_part.at[slot, lanes_of(to)],
                r.pool_land.at[me * slots + slot],
                r.pool_out_send.at[slot, step],
                r.pool_out_recv.at[slot, step],
                at_chan(to),
            ),
        )

    def own_out(slot):
        here = me * slots + slot
        return (
            pltpu.make_async_copy(
                r.low_part.at[slot, lanes_of(me)], r.grad_land.at[here], r.own_out_sem.at[slot, 0]
            ),
            pltpu.make_async_copy(
                r.pool_part.at[slot, lanes_of(me)], r.pool_land.at[here], r.own_out_sem.at[slot, 1]
            ),
        )

    def start_out(slot, steps=partners):
        for step in steps:
            for copy in out_copies(slot, step):
                copy.start()

    def land(slot):
        for step in partners:
            for copy in out_copies(slot, step):
                copy.wait_recv()
        for copy in own_out(slot):
            copy.wait()
        for src, dst in ((r.grad_land, r.wide), (r.pool_land, r.cot_wide)):
            for z in range(n):
                for j in range(dst.shape[0]):
                    part = src[z * slots + slot, :, j * LANES : (j + 1) * LANES].astype(F32)
                    dst[j, pl.ds(z * slots + slot, cl, stride=batch), :] = part

    out_order = {"early": range(0, EARLY), "mid": range(EARLY, slots - 1), "late": range(slots - 1, slots)}

    def start_outs(when):
        for slot in out_order[when]:
            start_out(slot)

    def prepare(slot, part):
        if part == 0:
            pieces = ((r.wide, send, 0, cl), (r.swin_wide, send, cl, cl))
        else:
            pieces = (
                (r.twin_wide, send, 2 * cl, tl),
                (r.pwin_wide, r.send_pool, 0, cl),
                (r.cot_wide, r.send_pool, cl, cl),
            )
        for to in range(n):
            first_row = to * slots + slot
            for src, dst, first, rows in pieces:
                for j in range(src.shape[0]):
                    dst[slot, to, first : first + rows, j * LANES : (j + 1) * LANES] = (
                        src[j, pl.ds(first_row, rows, stride=batch), :].astype(F32).astype(BF16)
                    )

    def prepare_slot(slot, carry):
        for part in range(2):
            prepare(slot, part)
            pl.when(2 * slot + part < AHEAD)(functools.partial(start_in, slot, part))
        for copy in own_copies(slot):
            copy.start()
        return carry

    for copy in small_loads:
        copy.wait()
    wait_load("images")
    for j in range(r.wide.shape[0]):
        r.wide[j] = r.raw[:, j * LANES : (j + 1) * LANES].astype(F32)
    wait_load("swin")
    if LOADS == 1:
        start_load("twin", "pwin", "cot")
    prepare(0, 0)
    pl.semaphore_wait(barrier, len(greeted))
    start_in(0, 0)
    if fused:
        r.flat[...] = jnp.zeros_like(r.flat)
        r.flat[0 : 2 * cl, 0:depth] = r.student_t[...]
        r.flat[2 * cl : 2 * cl + rl, 0:depth] = r.regress_t[...]
        r.filters[me, mine, 0:LANES] = r.flat[...].T[0:depth, :].astype(BF16)
        r.teach_flat[...] = jnp.zeros_like(r.teach_flat)
        r.teach_flat[0 : 2 * tl, :] = r.teacher_t[...].astype(F32)
        r.teach_cols[...] = r.teach_flat[...].T
        r.filters[me, mine, LANES:] = r.teach_cols[mine, :].astype(BF16)
        for copy in filter_z[:2] if n == 4 else filter_z:
            copy.start()
    for name in ("twin", "pwin", "cot"):
        wait_load(name)
    for j in range(r.cot_wide.shape[0]):
        r.cot_wide[j] = r.raw_cot[:, j * LANES : (j + 1) * LANES].astype(F32)
    prepare(0, 1)
    start_in(0, 1)
    for copy in own_copies(0):
        copy.start()
    if fused and n == 4:
        filter_z[1].wait_recv()
        filter_z[2].start()
    lax.fori_loop(1, slots, prepare_slot, 0)

    lane = lax.broadcasted_iota(jnp.int32, (16, pixels), 1)
    row_of, col_of = lane // IMG, lane % IMG
    for which, bad in enumerate((row_of == 0, row_of == IMG - 1, col_of == 0, col_of == IMG - 1)):
        r.edge[which] = jnp.where(bad, 0.0, 1.0).astype(BF16)
    spot = lax.broadcasted_iota(jnp.int32, (1, pixels), 1)
    home = (spot // (2 * IMG)) * (IMG // 2) + (spot % IMG) // 2
    r.up[...] = one_hot((cells, pixels), home, 0)
    r.sgrad[...] = jnp.zeros_like(r.sgrad)
    r.rgrad[...] = jnp.zeros_like(r.rgrad)

    if fused:
        picked = 2 * cl + rl + 2 * tl
        at = lax.broadcasted_iota(jnp.int32, (picked, 1), 0)
        teach = at - 2 * cl - rl
        lane_at = jnp.where(
            at < 2 * cl,
            2 * (at % cl) + at // cl,
            jnp.where(at < 2 * cl + rl, at, LANES + 2 * (teach % tl) + teach // tl),
        )
        r.gather_rows[...] = one_hot((picked, r.filters.shape[2]), lane_at, 1)
        for z in range(n):
            at = lax.broadcasted_iota(jnp.int32, (LANES, 1), 0)
            col_at = jnp.where(
                at < 2 * cl,
                (at % 2) * chans + z * cl + at // 2,
                jnp.where(at < 2 * cl + rl, 2 * chans + z * rl + at - 2 * cl, -1),
            )
            r.spread[z] = one_hot((LANES, r.spread.shape[2]), col_at, 1)

        for copy in (filter_z[0], filter_z[2]) if n == 4 else filter_z:
            copy.wait_recv()

        def filter_chip(step):
            to = lax.rem(chip + step, pairs)
            return remote(
                r.filters.at[:, mine],
                r.filters.at[:, mine],
                r.fx_send.at[step],
                r.fx_recv.at[step],
                at_row(2 * to + core),
            )

        def filter_core(step):
            rows = block(2 * lax.rem(chip + pairs - step, pairs) + core)
            return remote(
                r.filters.at[:, rows],
                r.filters.at[:, rows],
                r.fc_send.at[step],
                r.fc_recv.at[step],
                at_row(row + 1 - 2 * core),
            )

        for step in range(1, pairs):
            filter_chip(step).start()
        filter_core(0).start()
        for step in range(1, pairs):
            filter_chip(step).wait_recv()
            filter_core(step).start()
        for step in range(pairs):
            filter_core(step).wait_recv()

        for z in range(n):
            rows_of = dot_nt(r.gather_rows[...], r.filters[z]).astype(BF16)
            first = 0
            for dst, start, many in (
                (r.w_in, z * cl, cl),
                (r.w_in, chans + z * cl, cl),
                (r.w_reg, z * rl, rl),
                (r.w_in, 2 * chans + z * tl, tl),
                (r.w_in, 2 * chans + touts + z * tl, tl),
            ):
                dst[start : start + many, :] = rows_of[first : first + many, :]
                first += many
        for tap in range(9):
            rows = slice((8 - tap) * chans, (9 - tap) * chans)
            total = dot(r.filters[0, rows, 0:LANES], r.spread[0])
            for z in range(1, n):
                total += dot(r.filters[z, rows, 0:LANES], r.spread[z])
            total = total.astype(BF16)
            r.w_in_back[:, tap * 2 * chans : (tap + 1) * 2 * chans] = total[:, 0 : 2 * chans]
            r.w_reg_back[:, tap * regs : (tap + 1) * regs] = total[:, 2 * chans : 2 * chans + regs]

    def columns(load, rows, dst, stage):
        many = rows // (16 * STAGES)
        for g in range(many):
            first = pl.multiple_of((stage * many + g) * 16, 16)
            base = load(first)
            for ky in range(3):
                if ky == 1:
                    moved = base
                else:
                    moved = pltpu.roll(base, (pixels - IMG * (ky - 1)) % pixels, 1)
                    moved = moved * r.edge[0 if ky == 0 else 1]
                for kx in range(3):
                    if kx == 1:
                        tap = moved
                    else:
                        tap = pltpu.roll(moved, (pixels - (kx - 1)) % pixels, 1)
                        tap = tap * r.edge[2 if kx == 0 else 3]
                    dst[pl.ds((3 * ky + kx) * rows + first, 16), :] = tap

    def stages(*bodies):
        def one(stage, carry):
            for body in bodies:
                body(stage)
            return carry

        lax.fori_loop(0, STAGES, one, 0)

    def chunks(body):
        def one(stage):
            body(pl.ds(pl.multiple_of(stage * CHUNK, CHUNK), CHUNK))

        return one

    def add_grads(grads, left, right):
        many = grads.shape[0] // STAGES

        def one(stage):
            rows = pl.ds(pl.multiple_of(stage * many, 16), many)
            grads[rows, :] += dot_nt(left[rows, :], right[...])

        return one

    def corner_of(here):
        at = lax.broadcasted_iota(jnp.int32, (1, CHUNK), 1)
        return (2 * ((at // IMG) % 2) + at % 2).astype(F32)

    if fused:
        parts = ((r.rgrad, r.rc_send, r.rc_recv, r.rx_send, r.rx_recv),
                 (r.sgrad, r.sc_send, r.sc_recv, r.sx_send, r.sx_recv))

        def core_copy(which):
            return remote(
                parts[which][1],
                parts[which][2],
                r.core_send.at[which],
                r.core_recv.at[which],
                at_row(row + 1 - 2 * core),
            )

        def start_core(which):
            grads, out = parts[which][:2]
            for pair in range(pairs):
                out[pair] = grads[block(2 * pair + 1 - core), :].astype(BF16)
            core_copy(which).start()

        def chip_copy(which, step):
            return remote(
                parts[which][3].at[step],
                parts[which][4].at[step],
                r.chip_send.at[which, step],
                r.chip_recv.at[which, step],
                at_row(2 * lax.rem(chip + step, pairs) + core),
            )

        def chan_copy(step):
            return remote(
                r.zs_send.at[step],
                r.zs_recv.at[step],
                r.chan_send.at[step],
                r.chan_recv.at[step],
                at_chan(beside(step)),
            )

        def row_norm(step):
            return remote(
                r.part_rows.at[row],
                r.part_rows.at[row],
                r.rn_send.at[step],
                r.rn_recv.at[step],
                at_row(lax.rem(row + step, group)),
            )

        def chan_norm(step):
            return remote(
                r.part_chans.at[me],
                r.part_chans.at[me],
                r.cn_send.at[step],
                r.cn_recv.at[step],
                at_chan(beside(step)),
            )

    def step_chip(which):
        grads, _, came, out, _ = parts[which]
        cols = slice(2 * chans, 2 * chans + regs) if which == 0 else slice(0, 2 * chans)
        core_copy(which).wait_recv()
        for step in range(1, pairs):
            to = lax.rem(chip + step, pairs)
            out[step] = (grads[block(2 * to + core), :] + came[to].astype(F32)).astype(BF16)
            chip_copy(which, step).start()
        r.whole_grad[:, cols] = grads[block(row), :] + came[chip].astype(F32)

    def image(slot, carry):
        last = slot == slots - 1
        wait_in(slot, 0)
        start_later(slot, 0)
        for copy in own_copies(slot):
            copy.wait()

        def image_rows(first):
            return held[slot, first // cl, pl.ds(pl.multiple_of(first % cl, 16), 16), :]

        def picked(here):
            return held[slot, :, cl : 2 * cl, here].reshape(chans, CHUNK).astype(F32) > 0.5

        def head(here):
            pre = dot(r.w_in[0 : 2 * chans, :], r.x_cols[:, here])
            r.out_low[:, here] = jnp.where(picked(here), pre[chans:], pre[:chans]).astype(BF16)

        def teach(here):
            r.teach[:, here] = dot(r.w_in[2 * chans :, :], r.x_cols[:, here])

        def guess(here):
            r.guess[:, here] = dot(r.w_reg[...], r.o_cols[:, here])

        def pooling(here):
            cell_win = r.held_pool[slot, :, 0:cl, :].reshape(chans, cells)
            cell_cot = r.held_pool[slot, :, cl : 2 * cl, :].reshape(chans, cells)
            chosen = dot(cell_win, r.up[:, here]) == corner_of(here)
            spread = dot(cell_cot, r.up[:, here])
            r.pool_back[:, here] = jnp.where(chosen, spread, 0.0).astype(BF16)
            kept = jnp.where(chosen, r.out_low[:, here].astype(F32), 0.0).astype(BF16)
            part = dot_nt(kept, r.up[:, here])
            r.pool_part[slot] = (r.pool_part[slot].astype(F32) + part).astype(BF16)

        def hints(here):
            pick = held[slot, :, 2 * cl :, here].reshape(touts, CHUNK).astype(F32)
            target = jnp.where(pick > 0.5, r.teach[touts:, here], r.teach[:touts, here])
            weight = scale * r.mask[pl.ds(me * slots + slot, 1), here].astype(F32)
            r.hint[:, here] = (weight * (r.guess[:, here] - target)).astype(BF16)

        def back(here):
            total = dot(r.w_reg_back[...], r.h_cols[:, here]) + r.pool_back[:, here].astype(F32)
            pick = picked(here)
            r.pre_grad[0:chans, here] = jnp.where(pick, 0.0, total).astype(BF16)
            r.pre_grad[chans:, here] = jnp.where(pick, total, 0.0).astype(BF16)

        def image_back(here):
            r.low_part[slot, :, here] = dot(r.w_in_back[...], r.p_cols[:, here]).astype(BF16)

        def columns_of(src, dst):
            rows = src.shape[0]
            return lambda stage: columns(lambda first: src[pl.ds(first, 16), :], rows, dst, stage)

        spot_mask = r.mask[pl.ds(me * slots + slot, 1), :].astype(F32)
        count = jnp.sum(spot_mask, axis=1, keepdims=True)
        scale = HINT_WEIGHT * (pixels / count)
        r.pool_part[slot] = jnp.zeros((chans, cells), BF16)

        stages(lambda stage: columns(image_rows, chans, r.x_cols, stage))
        stages(chunks(head))
        stages(chunks(teach), columns_of(r.out_low, r.o_cols))
        stages(chunks(guess))
        wait_in(slot, 1)
        start_later(slot, 1)
        if OUT_AT == 0 or not fused:
            pl.when(last)(lambda: start_outs("early"))
        stages(chunks(hints))
        stages(add_grads(r.rgrad, r.o_cols, r.hint), columns_of(r.hint, r.h_cols))
        if fused:
            pl.when(last)(lambda: start_core(0))
            if OUT_AT == 1:
                pl.when(last)(lambda: start_outs("early"))
        stages(chunks(pooling))
        stages(chunks(back))
        if fused and CHIP_AT == 1:
            pl.when(last)(lambda: step_chip(0))
        stages(add_grads(r.sgrad, r.x_cols, r.pre_grad), columns_of(r.pre_grad, r.p_cols))
        if fused:

            def reduce_more():
                start_core(1)
                if OUT_AT == 2:
                    start_outs("early")
                if CHIP_AT == 0:
                    step_chip(0)

            pl.when(last)(reduce_more)
        stages(chunks(image_back))
        if not fused:

            def start_rest():
                start_outs("mid")
                start_outs("late")

            pl.when(last)(start_rest)
        for copy in own_out(slot):
            copy.start()
        return carry

    if fused:
        r.whole_grad[...] = jnp.zeros_like(r.whole_grad)
    lax.fori_loop(0, slots, image, 0)

    if fused:
        step_chip(1)
        for which, cols in ((0, slice(2 * chans, 2 * chans + regs)), (1, slice(0, 2 * chans))):
            came = parts[which][4]
            for step in range(1, pairs):
                chip_copy(which, step).wait_recv()
            total = r.whole_grad[:, cols]
            for step in range(1, pairs):
                total += came[step].astype(F32)
            r.whole_grad[:, cols] = total
        low_grad = r.whole_grad[...].astype(BF16)
        for step in partners:
            r.zs_send[step] = dot_nt(low_grad, r.spread[beside(step)]).astype(BF16)
            chan_copy(step).start()
        start_outs("mid")
        far = [step for step in partners if step > NEAR_LATE]
        start_out(slots - 1, far)
        total = dot_nt(
            r.whole_grad[...], r.spread[me].astype(F32), precision=lax.Precision.HIGHEST
        )
        for slot in out_order["early"]:
            land(slot)
        for step in partners:
            chan_copy(step).wait_recv()
        for step in partners:
            total += r.zs_recv[step].astype(F32)
        r.tall[0:depth, :] = total
        total = r.tall[...].T[:, 0:depth]
        r.grad_sum[...] = total
        student, regress = r.student_t[...], r.regress_t[...]
        upd_s = lamb_update(student, total[0 : 2 * cl], r.mom_student[...], r.sq_student[...])[2]
        upd_r = lamb_update(
            regress, total[2 * cl : 2 * cl + rl], r.mom_regress[...], r.sq_regress[...]
        )[2]
        place = lax.broadcasted_iota(jnp.int32, (8, LANES), 1)
        tile = jnp.zeros((8, LANES), F32)
        for index, value in enumerate((student, upd_s, regress, upd_r)):
            square = jnp.sum(jnp.sum(value * value, axis=1, keepdims=True), axis=0, keepdims=True)
            tile = jnp.where(place == index, square, tile)
        r.part_chans[me] = tile
        for step in partners:
            chan_norm(step).start()
        start_out(slots - 1, [step for step in partners if step not in far])
        for slot in out_order["mid"]:
            land(slot)
        for step in partners:
            chan_norm(step).wait_recv()
        tile = r.part_chans[0]
        for index in range(1, n):
            tile += r.part_chans[index]
        r.part_rows[row] = tile
        for step in range(1, group):
            row_norm(step).start()
        for step in range(1, group):
            row_norm(step).wait_recv()
        tile = r.part_rows[0]
        for index in range(1, group):
            tile += r.part_rows[index]
        r.sums[...] = tile

    for slot in out_order["late"] if fused else range(slots):
        land(slot)
    for src, out in ((r.wide, r.grad_out), (r.cot_wide, r.pool_out)):
        for j in range(src.shape[0]):
            out[:, j * LANES : (j + 1) * LANES] = src[j].astype(BF16)

    def finish(slot, carry):
        for step in partners:
            for copy in (*in_copies(slot, step, 0), *in_copies(slot, step, 1), *out_copies(slot, step)):
                copy.wait_send()
        return carry

    lax.fori_loop(0, slots, finish, 0)
    if fused:
        for step in partners:
            filter_z[step - 1].wait_send()
            chan_copy(step).wait_send()
            chan_norm(step).wait_send()
        for step in range(1, group):
            row_norm(step).wait_send()
        for step in range(pairs):
            filter_core(step).wait_send()
        for step in range(1, pairs):
            filter_chip(step).wait_send()
        for which in range(2):
            core_copy(which).wait_send()
            for step in range(1, pairs):
                chip_copy(which, step).wait_send()


def lamb_update(weights, grads, moment, second):
    moment_new = BETA_ONE * moment + (1.0 - BETA_ONE) * grads
    second_new = BETA_TWO * second + (1.0 - BETA_TWO) * grads * grads
    moment_hat = moment_new / (1.0 - BETA_ONE**STEP)
    second_hat = second_new / (1.0 - BETA_TWO**STEP)
    update = moment_hat / (jnp.sqrt(second_hat) + EPSILON) + DECAY * weights
    return (moment_new, second_new, update)


def layer_pass(n, group, fused, arrays, handed=()):
    cl, batch, pixels = arrays["images"].shape
    tl = arrays["twin"].shape[0]
    cells = arrays["pwin"].shape[2]
    slots = batch // n
    chans = n * cl
    if fused:
        rl, depth = arrays["regress_t"].shape
    else:
        rl = arrays["w_reg"].shape[0] // n
    regs, touts, pairs = n * rl, n * tl, group // 2
    size = dict(n=n, batch=batch, cl=cl, tl=tl, rl=rl, fused=fused, group=group)
    vmem = pl.BlockSpec(memory_space=pltpu.VMEM)
    in_hbm = ("images", "swin", "twin", "pwin", "cot")
    ins = {
        name: a.reshape(a.shape[0] * a.shape[1], a.shape[2]) if name in in_hbm else a
        for name, a in arrays.items()
    }
    outs = {
        "pool_out": pltpu.VMEM((cl * batch, cells), BF16),
        "grad_out": pltpu.VMEM((cl * batch, pixels), BF16),
    }
    small = tuple(name for name in ins if name not in in_hbm)
    size["small"] = small
    grads = {"sgrad": (9 * chans, 2 * chans), "rgrad": (9 * chans, regs)}
    dma = lambda *shape: pltpu.SemaphoreType.DMA(shape)
    scratch = {
        "raw": pltpu.VMEM((cl * batch, pixels), BF16),
        "raw_cot": pltpu.VMEM((cl * batch, cells), BF16),
        "wide": pltpu.VMEM((pixels // LANES, cl * batch, LANES), F32),
        "swin_wide": pltpu.VMEM((pixels // LANES, cl * batch, LANES), jnp.int32),
        "twin_wide": pltpu.VMEM((pixels // LANES, tl * batch, LANES), jnp.int32),
        "pwin_wide": pltpu.VMEM((cells // LANES, cl * batch, LANES), jnp.int32),
        "cot_wide": pltpu.VMEM((cells // LANES, cl * batch, LANES), F32),
        "load_sem": dma(2 + 2 * (pixels // LANES) + cells // LANES),
        "send": pltpu.VMEM((slots, n, 2 * cl + tl, pixels), BF16),
        "send_pool": pltpu.VMEM((slots, n, 2 * cl, cells), BF16),
        "held": pltpu.VMEM((slots, n, 2 * cl + tl, pixels), BF16),
        "held_pool": pltpu.VMEM((slots, n, 2 * cl, cells), BF16),
        "low_part": pltpu.VMEM((slots, chans, pixels), BF16),
        "pool_part": pltpu.VMEM((slots, chans, cells), BF16),
        "pool_land": pltpu.VMEM((batch, cl, cells), BF16),
        "grad_land": pltpu.VMEM((batch, cl, pixels), BF16),
        "edge": pltpu.VMEM((4, 16, pixels), BF16),
        "up": pltpu.VMEM((cells, pixels), BF16),
        "x_cols": pltpu.VMEM((9 * chans, pixels), BF16),
        "o_cols": pltpu.VMEM((9 * chans, pixels), BF16),
        "h_cols": pltpu.VMEM((9 * regs, pixels), BF16),
        "p_cols": pltpu.VMEM((9 * 2 * chans, pixels), BF16),
        "out_low": pltpu.VMEM((chans, pixels), BF16),
        "pool_back": pltpu.VMEM((chans, pixels), BF16),
        "hint": pltpu.VMEM((regs, pixels), BF16),
        "teach": pltpu.VMEM((2 * touts, pixels), F32),
        "guess": pltpu.VMEM((regs, pixels), F32),
        "pre_grad": pltpu.VMEM((2 * chans, pixels), BF16),
        "own_sem": dma(slots, 2),
        "own_out_sem": dma(slots, 2),
    }
    scratch["in_send"] = dma(slots, 2, n)
    scratch["in_recv"] = dma(slots, 2, n)
    for name in ("pool_in", "out", "pool_out"):
        scratch[name + "_send"] = dma(slots, n)
        scratch[name + "_recv"] = dma(slots, n)
    if fused:
        cols = 2 * chans + 2 * LANES
        tall = -(-depth // LANES) * LANES
        outs["grad_sum"] = pltpu.VMEM((LANES, depth), F32)
        outs["sums"] = pltpu.VMEM((8, LANES), F32)
        outs.update({name: pltpu.VMEM(ins[name].shape, F32) for name in handed})
        scratch.update({name: pltpu.VMEM(shape, F32) for name, shape in grads.items()})
        scratch.update(
            {
                "flat": pltpu.VMEM((LANES, tall), F32),
                "tall": pltpu.VMEM((tall, LANES), F32),
                "teach_flat": pltpu.VMEM((LANES, 9 * chans), F32),
                "teach_cols": pltpu.VMEM((9 * chans, LANES), F32),
                "filters": pltpu.VMEM((n, 9 * chans, 2 * LANES), BF16),
                "gather_rows": pltpu.VMEM((2 * cl + rl + 2 * tl, 2 * LANES), BF16),
                "spread": pltpu.VMEM((n, LANES, cols), BF16),
                "w_in": pltpu.VMEM((2 * chans + 2 * touts, 9 * chans), BF16),
                "w_reg": pltpu.VMEM((regs, 9 * chans), BF16),
                "w_reg_back": pltpu.VMEM((chans, 9 * regs), BF16),
                "w_in_back": pltpu.VMEM((chans, 9 * 2 * chans), BF16),
                "rc_send": pltpu.VMEM((pairs, depth, regs), BF16),
                "rc_recv": pltpu.VMEM((pairs, depth, regs), BF16),
                "rx_send": pltpu.VMEM((pairs, depth, regs), BF16),
                "rx_recv": pltpu.VMEM((pairs, depth, regs), BF16),
                "sc_send": pltpu.VMEM((pairs, depth, 2 * chans), BF16),
                "sc_recv": pltpu.VMEM((pairs, depth, 2 * chans), BF16),
                "sx_send": pltpu.VMEM((pairs, depth, 2 * chans), BF16),
                "sx_recv": pltpu.VMEM((pairs, depth, 2 * chans), BF16),
                "whole_grad": pltpu.VMEM((depth, cols), F32),
                "zs_send": pltpu.VMEM((n, depth, LANES), BF16),
                "zs_recv": pltpu.VMEM((n, depth, LANES), BF16),
                "part_rows": pltpu.VMEM((group, 8, LANES), F32),
                "part_chans": pltpu.VMEM((n, 8, LANES), F32),
                "core_send": dma(2),
                "core_recv": dma(2),
                "chip_send": dma(2, pairs),
                "chip_recv": dma(2, pairs),
            }
        )
        for name, many in (
            ("fz", n), ("fx", pairs), ("fc", pairs), ("chan", n), ("rn", group), ("cn", n)
        ):
            scratch[name + "_send"] = dma(many)
            scratch[name + "_recv"] = dma(many)
    else:
        outs.update({name: jax.ShapeDtypeStruct(shape, F32) for name, shape in grads.items()})
    flops = 2 * slots * pixels * 9 * chans * (3 * 2 * chans + 2 * touts + 3 * regs)
    scratch.update(
        {name: pltpu.VMEM(ins[name].shape, ins[name].dtype) for name in small if name not in outs}
    )
    scratch["small_sem"] = dma(len(small))
    in_names = tuple(name + "_hbm" if name in small else name for name in ins)
    names = in_names + tuple(outs) + tuple(scratch)
    return pl.pallas_call(
        functools.partial(layer_kernel, size, names),
        out_shape=list(outs.values()),
        in_specs=[pl.BlockSpec(memory_space=pl.ANY)] * len(ins),
        out_specs=[vmem] * len(outs),
        scratch_shapes=list(scratch.values()),
        compiler_params=pltpu.CompilerParams(
            collective_id=0, has_side_effects=True, vmem_limit_bytes=58 << 20
        ),
        cost_estimate=pl.CostEstimate(flops=flops, bytes_accessed=16 << 20, transcendentals=0),
        name="layer",
    )(*ins.values())


def final_kernel(*refs):
    pool_in, grad_in = refs[0:2]
    pooled, image_grad, new_s, new_r, trust = refs[12], refs[13], refs[14:19], refs[19:24], refs[24]
    big_sem = refs[25]
    big = [
        pltpu.make_async_copy(src, dst, big_sem.at[index])
        for index, (src, dst) in enumerate(((grad_in, image_grad), (pool_in, pooled)))
    ]
    for copy in big:
        copy.start()
    grad_sum, sums, student, regress, mom_s, sq_s, mom_r, sq_r, ema_s, ema_r = refs[2:12]
    norm = [jnp.sqrt(sums[0:1, k : k + 1]) for k in range(4)]
    souts, regs = student.shape[0], regress.shape[0]
    for weights, grads, moment, second, average, outs, top, bottom in (
        (student, grad_sum[0:souts, :], mom_s, sq_s, ema_s, new_s, norm[0], norm[1]),
        (regress, grad_sum[souts : souts + regs, :], mom_r, sq_r, ema_r, new_r, norm[2], norm[3]),
    ):
        moment_new, second_new, update = lamb_update(
            weights[...], grads, moment[...], second[...]
        )
        new = weights[...] - LEARN_RATE * (top / bottom) * update
        outs[0][...] = new
        outs[1][...] = moment_new
        outs[2][...] = second_new
        outs[3][...] = EMA_KEEP * average[...] + (1.0 - EMA_KEEP) * new
        outs[4][...] = new.astype(BF16)
    across = lax.broadcasted_iota(jnp.int32, (2, 2), 1)
    down = lax.broadcasted_iota(jnp.int32, (2, 2), 0)
    first = jnp.where(across == 0, norm[0], norm[1])
    trust[...] = jnp.where(down == 0, first, jnp.where(across == 0, norm[2], norm[3]))
    for copy in big:
        copy.wait()


def final_pass(pooled, image_grad, grad_sum, sums, *small):
    student, regress = small[0:2]
    outs = [jax.ShapeDtypeStruct(a.shape, BF16) for a in (pooled, image_grad)]
    for a in (student, regress):
        outs += [jax.ShapeDtypeStruct(a.shape, F32)] * 4 + [jax.ShapeDtypeStruct(a.shape, BF16)]
    outs.append(jax.ShapeDtypeStruct((2, 2), F32))
    vmem, hbm = (pl.BlockSpec(memory_space=space) for space in (pltpu.VMEM, pl.ANY))
    kept = (grad_sum, sums, *small)
    results = pl.pallas_call(
        final_kernel,
        out_shape=outs,
        in_specs=[vmem] * (2 + len(kept)),
        out_specs=[hbm] * 2 + [vmem] * (len(outs) - 2),
        scratch_shapes=[pltpu.SemaphoreType.DMA((2,))],
        compiler_params=pltpu.CompilerParams(vmem_limit_bytes=16 << 20),
        name="final",
    )(*(pltpu.with_memory_space_constraint(a, pltpu.VMEM) for a in (pooled, image_grad, *kept)))
    return (*results[0:2], *(a.T for a in results[2:12]), results[12])


def split_pieces(weights):
    rows, cols = weights.shape
    return weights.reshape(rows, cols // 2, 2).transpose(2, 1, 0).reshape(cols, rows)


def back_weights(weights, outs):
    channels = weights.shape[0] // 9
    taps = weights.reshape(9, channels, outs)[::-1]
    return taps.transpose(1, 0, 2).reshape(channels, 9 * outs)


def gathered_filters(student_master, regress_master, teacher_weight):
    student_full = lax.all_gather(student_master.astype(BF16), "dp", axis=0, tiled=True)
    student_full = lax.all_gather(student_full, "chan", axis=1, tiled=True)
    regress_full = lax.all_gather(regress_master.astype(BF16), "dp", axis=0, tiled=True)
    regress_full = lax.all_gather(regress_full, "chan", axis=1, tiled=True)
    teacher_full = lax.all_gather(teacher_weight, "chan", axis=1, tiled=True)
    student_rows = split_pieces(student_full)
    return {
        "w_in": jnp.concatenate([student_rows, split_pieces(teacher_full)], axis=0),
        "w_reg": regress_full.T,
        "w_reg_back": back_weights(regress_full, regress_full.shape[1]),
        "w_in_back": back_weights(student_rows.T, student_full.shape[1]),
    }


def scattered_grads(student_part, regress_part):
    souts = student_part.shape[1]
    student_part = student_part.reshape(-1, 2, souts // 2).transpose(0, 2, 1).reshape(-1, souts)
    student_grad = lax.psum_scatter(student_part, "dp", scatter_dimension=0, tiled=True)
    student_grad = lax.psum_scatter(student_grad, "chan", scatter_dimension=1, tiled=True)
    regress_grad = lax.psum_scatter(regress_part, "dp", scatter_dimension=0, tiled=True)
    regress_grad = lax.psum_scatter(regress_grad, "chan", scatter_dimension=1, tiled=True)
    return student_grad, regress_grad


def on_device(
    n,
    group,
    images,
    student_master,
    regress_master,
    teacher_weight,
    student_win,
    teacher_win,
    pool_win,
    hint_mask,
    cotangent,
    mom_student,
    sq_student,
    ema_student,
    mom_regress,
    sq_regress,
    ema_regress,
):
    image_like = lambda a: a.reshape(images.shape)
    pool_win_like = lambda a: a.reshape(pool_win.shape)
    depth = student_master.shape[0]
    fused = group % 2 == 0 and depth % 16 == 0
    arrays = dict(
        images=images,
        swin=student_win,
        twin=teacher_win,
        pwin=pool_win,
        cot=cotangent,
        mask=hint_mask,
    )
    if fused:
        small = dict(
            student_t=student_master,
            regress_t=regress_master,
            mom_student=mom_student,
            sq_student=sq_student,
            mom_regress=mom_regress,
            sq_regress=sq_regress,
            ema_student=ema_student,
            ema_regress=ema_regress,
        )
        arrays.update({name: a.T for name, a in small.items()}, teacher_t=teacher_weight.T)
        results = final_pass(*layer_pass(n, group, fused, arrays, tuple(small)))
        return (pool_win_like(results[0]), image_like(results[1]), *results[2:])
    arrays.update(gathered_filters(student_master, regress_master, teacher_weight))
    pooled, image_grad, student_part, regress_part = layer_pass(n, group, fused, arrays)
    student_grad, regress_grad = scattered_grads(student_part, regress_part)
    mom_s, sq_s, upd_s = lamb_update(student_master, student_grad, mom_student, sq_student)
    mom_r, sq_r, upd_r = lamb_update(regress_master, regress_grad, mom_regress, sq_regress)
    all_sums = lax.psum(
        jnp.stack([jnp.sum(v * v) for v in (student_master, upd_s, regress_master, upd_r)]),
        ("dp", "chan"),
    )
    norms = jnp.sqrt(all_sums)
    new_student = student_master - LEARN_RATE * (norms[0] / norms[1]) * upd_s
    new_regress = regress_master - LEARN_RATE * (norms[2] / norms[3]) * upd_r
    ema_s = EMA_KEEP * ema_student + (1.0 - EMA_KEEP) * new_student
    ema_r = EMA_KEEP * ema_regress + (1.0 - EMA_KEEP) * new_regress
    return (
        pool_win_like(pooled),
        image_like(image_grad),
        new_student,
        mom_s,
        sq_s,
        ema_s,
        new_student.astype(BF16),
        new_regress,
        mom_r,
        sq_r,
        ema_r,
        new_regress.astype(BF16),
        norms.reshape(2, 2),
    )


def solution(mesh):
    acts = P("chan", "dp", None)
    rows = P("dp", "chan")
    in_specs = (
        (acts, rows, rows, P(None, "chan"))
        + (acts, acts, acts, P("dp", None), acts)
        + (rows,) * 6
    )
    out_specs = (acts, acts) + (rows,) * 10 + (P(),)
    return jax.shard_map(
        functools.partial(on_device, mesh.shape["chan"], mesh.shape["dp"]),
        mesh=mesh,
        in_specs=in_specs,
        out_specs=out_specs,
        check_vma=False,
    )
```

```python
import functools
import types

import jax
import jax.numpy as jnp
from jax import lax
from jax.experimental import pallas as pl
from jax.experimental.pallas import tpu as pltpu
from jax.sharding import PartitionSpec as P

IMG = 32
STEP = 10
HINT_WEIGHT = 0.1
LEARN_RATE = 0.5
BETA_ONE = 0.9
BETA_TWO = 0.999
EPSILON = 1e-06
DECAY = 0.01
EMA_KEEP = 0.75

MESH = pl.DeviceIdType.MESH
F32 = jnp.float32
BF16 = jnp.bfloat16
STAGES = 1
CHUNK = IMG * IMG // STAGES
LANES = 128
AHEAD = 5
ORDER = (2, 1, 3)
EARLY = 2


def dot(left, right):
    return jnp.dot(left, right, preferred_element_type=F32)


def dot_nt(left, right, precision=None):
    return lax.dot_general(
        left, right, (((1,), (1,)), ((), ())), precision=precision, preferred_element_type=F32
    )


def one_hot(shape, target, axis):
    at = lax.broadcasted_iota(jnp.int32, shape, axis)
    return jnp.where(at == target, 1.0, 0.0).astype(BF16)


def layer_kernel(size, names, *refs):
    r = types.SimpleNamespace(**dict(zip(names, refs)))
    small_loads = []
    for index, name in enumerate(size["small"]):
        small_loads.append(
            pltpu.make_async_copy(getattr(r, name + "_hbm"), getattr(r, name), r.small_sem.at[index])
        )
    n, batch, cl, tl, rl = size["n"], size["batch"], size["cl"], size["tl"], size["rl"]
    fused, group = size["fused"], size["group"]
    slots = batch // n
    chans, touts, regs = n * cl, n * tl, n * rl
    pixels = IMG * IMG
    cells = pixels // 4
    me = lax.axis_index("chan")
    row = lax.axis_index("dp")
    core, chip, pairs = row % 2, row // 2, group // 2
    held, send = r.held, r.send

    def beside(step):
        if n & (n - 1):
            return lax.rem(me + step, n)
        other, bit = me, 1
        while bit < n:
            if step & bit:
                other = other + bit - 2 * bit * ((me // bit) % 2)
            bit *= 2
        return other

    partners = ORDER if n == 4 else range(1, n)

    def at_chan(index):
        return {"chan": index}

    def at_row(index):
        return {"dp": index}

    def remote(src, dst, out_sem, in_sem, device):
        return pltpu.make_async_remote_copy(
            src, dst, out_sem, in_sem, device_id=device, device_id_type=MESH
        )

    greeted = [at_chan(beside(step)) for step in range(1, n)]
    if fused:
        greeted += [at_row(lax.rem(row + step, group)) for step in range(1, group)]

    sources = {
        "images": (r.images, r.raw, None),
        "swin": (r.swin, r.swin_wide, LANES),
        "twin": (r.twin, r.twin_wide, LANES),
        "pwin": (r.pwin, r.pwin_wide, LANES),
        "cot": (r.cot, r.raw_cot, None),
    }
    loads, count = {}, 0
    for name, (src, dst, lanes) in sources.items():
        loads[name] = []
        for j in range(dst.shape[0] if lanes else 1):
            pair = (src.at[:, pl.ds(j * LANES, LANES)], dst.at[j]) if lanes else (src, dst)
            loads[name].append(pltpu.make_async_copy(*pair, r.load_sem.at[count]))
            count += 1

    def start_load(*names):
        for name in names:
            for copy in loads[name]:
                copy.start()

    start_load("images", "swin")

    for copy in small_loads:
        copy.start()

    def wait_load(name):
        for copy in loads[name]:
            copy.wait()

    barrier = pltpu.get_barrier_semaphore()
    for device in greeted:
        pl.semaphore_signal(barrier, inc=1, device_id=device, device_id_type=MESH)

    if fused:
        depth = r.student_t.shape[1]

        def block(index):
            return pl.ds(pl.multiple_of(index * depth, 16), depth)

        mine = block(row)
        filter_z = [
            remote(
                r.filters.at[me, mine],
                r.filters.at[me, mine],
                r.fz_send.at[step],
                r.fz_recv.at[step],
                at_chan(beside(step)),
            )
            for step in range(1, n)
        ]
        if n == 4:
            passed = beside(2)
            filter_z[2] = remote(
                r.filters.at[passed, mine],
                r.filters.at[passed, mine],
                r.fz_send.at[3],
                r.fz_recv.at[3],
                at_chan(beside(1)),
            )

    def in_copies(slot, step, part):
        to = beside(step)
        rows = pl.ds(0, 2 * cl) if part == 0 else pl.ds(2 * cl, tl)
        copies = [
            remote(
                send.at[slot, to, rows],
                held.at[slot, me, rows],
                r.in_send.at[slot, part, step],
                r.in_recv.at[slot, part, step],
                at_chan(to),
            )
        ]
        if part == 1:
            copies.append(
                remote(
                    r.send_pool.at[slot, to],
                    r.held_pool.at[slot, me],
                    r.pool_in_send.at[slot, step],
                    r.pool_in_recv.at[slot, step],
                    at_chan(to),
                )
            )
        return copies

    def start_in(slot, part):
        for step in partners:
            for copy in in_copies(slot, step, part):
                copy.start()

    def wait_in(slot, part):
        for step in partners:
            for copy in in_copies(slot, step, part):
                copy.wait_recv()

    def start_later(slot, part):
        later = slot + (part + AHEAD) // 2
        pl.when(later < slots)(lambda: start_in(later, (part + AHEAD) % 2))

    def own_copies(slot):
        return (
            pltpu.make_async_copy(send.at[slot, me], held.at[slot, me], r.own_sem.at[slot, 0]),
            pltpu.make_async_copy(
                r.send_pool.at[slot, me], r.held_pool.at[slot, me], r.own_sem.at[slot, 1]
            ),
        )

    def lanes_of(index):
        return pl.ds(pl.multiple_of(index * cl, cl), cl)

    def out_copies(slot, step):
        to = beside(step)
        return (
            remote(
                r.low_part.at[slot, lanes_of(to)],
                r.grad_land.at[me * slots + slot],
                r.out_send.at[slot, step],
                r.out_recv.at[slot, step],
                at_chan(to),
            ),
            remote(
                r.pool_part.at[slot, lanes_of(to)],
                r.pool_land.at[me * slots + slot],
                r.pool_out_send.at[slot, step],
                r.pool_out_recv.at[slot, step],
                at_chan(to),
            ),
        )

    def own_out(slot):
        here = me * slots + slot
        return (
            pltpu.make_async_copy(
                r.low_part.at[slot, lanes_of(me)], r.grad_land.at[here], r.own_out_sem.at[slot, 0]
            ),
            pltpu.make_async_copy(
                r.pool_part.at[slot, lanes_of(me)], r.pool_land.at[here], r.own_out_sem.at[slot, 1]
            ),
        )

    def start_out(slot):
        for step in partners:
            for copy in out_copies(slot, step):
                copy.start()

    def land(slot):
        for step in partners:
            for copy in out_copies(slot, step):
                copy.wait_recv()
        for copy in own_out(slot):
            copy.wait()
        for src, dst in ((r.grad_land, r.wide), (r.pool_land, r.cot_wide)):
            for z in range(n):
                for j in range(dst.shape[0]):
                    part = src[z * slots + slot, :, j * LANES : (j + 1) * LANES].astype(F32)
                    dst[j, pl.ds(z * slots + slot, cl, stride=batch), :] = part

    out_order = {"early": range(0, EARLY), "mid": range(EARLY, slots - 1), "late": range(slots - 1, slots)}

    def start_outs(when):
        for slot in out_order[when]:
            start_out(slot)

    def prepare(slot, part):
        if part == 0:
            pieces = ((r.wide, send, 0, cl), (r.swin_wide, send, cl, cl))
        else:
            pieces = (
                (r.twin_wide, send, 2 * cl, tl),
                (r.pwin_wide, r.send_pool, 0, cl),
                (r.cot_wide, r.send_pool, cl, cl),
            )
        for to in range(n):
            first_row = to * slots + slot
            for src, dst, first, rows in pieces:
                for j in range(src.shape[0]):
                    dst[slot, to, first : first + rows, j * LANES : (j + 1) * LANES] = (
                        src[j, pl.ds(first_row, rows, stride=batch), :].astype(F32).astype(BF16)
                    )

    def prepare_slot(slot, carry):
        for part in range(2):
            prepare(slot, part)
            pl.when(2 * slot + part < AHEAD)(functools.partial(start_in, slot, part))
        for copy in own_copies(slot):
            copy.start()
        return carry

    for copy in small_loads:
        copy.wait()
    wait_load("images")
    for j in range(r.wide.shape[0]):
        r.wide[j] = r.raw[:, j * LANES : (j + 1) * LANES].astype(F32)
    wait_load("swin")
    start_load("twin", "pwin", "cot")
    prepare(0, 0)
    pl.semaphore_wait(barrier, len(greeted))
    start_in(0, 0)
    if fused:
        r.flat[...] = jnp.zeros_like(r.flat)
        r.flat[0 : 2 * cl, 0:depth] = r.student_t[...]
        r.flat[2 * cl : 2 * cl + rl, 0:depth] = r.regress_t[...]
        r.filters[me, mine, 0:LANES] = r.flat[...].T[0:depth, :].astype(BF16)
        r.teach_flat[...] = jnp.zeros_like(r.teach_flat)
        r.teach_flat[0 : 2 * tl, :] = r.teacher_t[...].astype(F32)
        r.teach_cols[...] = r.teach_flat[...].T
        r.filters[me, mine, LANES:] = r.teach_cols[mine, :].astype(BF16)
        for copy in filter_z[:2] if n == 4 else filter_z:
            copy.start()
    for name in ("twin", "pwin", "cot"):
        wait_load(name)
    for j in range(r.cot_wide.shape[0]):
        r.cot_wide[j] = r.raw_cot[:, j * LANES : (j + 1) * LANES].astype(F32)
    prepare(0, 1)
    start_in(0, 1)
    for copy in own_copies(0):
        copy.start()
    if fused and n == 4:
        filter_z[1].wait_recv()
        filter_z[2].start()
    lax.fori_loop(1, slots, prepare_slot, 0)

    lane = lax.broadcasted_iota(jnp.int32, (16, pixels), 1)
    row_of, col_of = lane // IMG, lane % IMG
    for which, bad in enumerate((row_of == 0, row_of == IMG - 1, col_of == 0, col_of == IMG - 1)):
        r.edge[which] = jnp.where(bad, 0.0, 1.0).astype(BF16)
    spot = lax.broadcasted_iota(jnp.int32, (1, pixels), 1)
    home = (spot // (2 * IMG)) * (IMG // 2) + (spot % IMG) // 2
    r.up[...] = one_hot((cells, pixels), home, 0)
    r.sgrad[...] = jnp.zeros_like(r.sgrad)
    r.rgrad[...] = jnp.zeros_like(r.rgrad)

    if fused:
        picked = 2 * cl + rl + 2 * tl
        at = lax.broadcasted_iota(jnp.int32, (picked, 1), 0)
        teach = at - 2 * cl - rl
        lane_at = jnp.where(
            at < 2 * cl,
            2 * (at % cl) + at // cl,
            jnp.where(at < 2 * cl + rl, at, LANES + 2 * (teach % tl) + teach // tl),
        )
        r.gather_rows[...] = one_hot((picked, r.filters.shape[2]), lane_at, 1)
        for z in range(n):
            at = lax.broadcasted_iota(jnp.int32, (LANES, 1), 0)
            col_at = jnp.where(
                at < 2 * cl,
                (at % 2) * chans + z * cl + at // 2,
                jnp.where(at < 2 * cl + rl, 2 * chans + z * rl + at - 2 * cl, -1),
            )
            r.spread[z] = one_hot((LANES, r.spread.shape[2]), col_at, 1)

        for copy in (filter_z[0], filter_z[2]) if n == 4 else filter_z:
            copy.wait_recv()

        def filter_chip(step):
            to = lax.rem(chip + step, pairs)
            return remote(
                r.filters.at[:, mine],
                r.filters.at[:, mine],
                r.fx_send.at[step],
                r.fx_recv.at[step],
                at_row(2 * to + core),
            )

        def filter_core(step):
            rows = block(2 * lax.rem(chip + pairs - step, pairs) + core)
            return remote(
                r.filters.at[:, rows],
                r.filters.at[:, rows],
                r.fc_send.at[step],
                r.fc_recv.at[step],
                at_row(row + 1 - 2 * core),
            )

        for step in range(1, pairs):
            filter_chip(step).start()
        filter_core(0).start()
        for step in range(1, pairs):
            filter_chip(step).wait_recv()
            filter_core(step).start()
        for step in range(pairs):
            filter_core(step).wait_recv()

        for z in range(n):
            rows_of = dot_nt(r.gather_rows[...], r.filters[z]).astype(BF16)
            first = 0
            for dst, start, many in (
                (r.w_in, z * cl, cl),
                (r.w_in, chans + z * cl, cl),
                (r.w_reg, z * rl, rl),
                (r.w_in, 2 * chans + z * tl, tl),
                (r.w_in, 2 * chans + touts + z * tl, tl),
            ):
                dst[start : start + many, :] = rows_of[first : first + many, :]
                first += many
        for tap in range(9):
            rows = slice((8 - tap) * chans, (9 - tap) * chans)
            total = dot(r.filters[0, rows, 0:LANES], r.spread[0])
            for z in range(1, n):
                total += dot(r.filters[z, rows, 0:LANES], r.spread[z])
            total = total.astype(BF16)
            r.w_in_back[:, tap * 2 * chans : (tap + 1) * 2 * chans] = total[:, 0 : 2 * chans]
            r.w_reg_back[:, tap * regs : (tap + 1) * regs] = total[:, 2 * chans : 2 * chans + regs]

    def columns(load, rows, dst, stage):
        many = rows // (16 * STAGES)
        for g in range(many):
            first = pl.multiple_of((stage * many + g) * 16, 16)
            base = load(first)
            for ky in range(3):
                if ky == 1:
                    moved = base
                else:
                    moved = pltpu.roll(base, (pixels - IMG * (ky - 1)) % pixels, 1)
                    moved = moved * r.edge[0 if ky == 0 else 1]
                for kx in range(3):
                    if kx == 1:
                        tap = moved
                    else:
                        tap = pltpu.roll(moved, (pixels - (kx - 1)) % pixels, 1)
                        tap = tap * r.edge[2 if kx == 0 else 3]
                    dst[pl.ds((3 * ky + kx) * rows + first, 16), :] = tap

    def stages(*bodies):
        def one(stage, carry):
            for body in bodies:
                body(stage)
            return carry

        lax.fori_loop(0, STAGES, one, 0)

    def chunks(body):
        def one(stage):
            body(pl.ds(pl.multiple_of(stage * CHUNK, CHUNK), CHUNK))

        return one

    def add_grads(grads, left, right):
        many = grads.shape[0] // STAGES

        def one(stage):
            rows = pl.ds(pl.multiple_of(stage * many, 16), many)
            grads[rows, :] += dot_nt(left[rows, :], right[...])

        return one

    def corner_of(here):
        at = lax.broadcasted_iota(jnp.int32, (1, CHUNK), 1)
        return (2 * ((at // IMG) % 2) + at % 2).astype(F32)

    if fused:
        parts = ((r.rgrad, r.rc_send, r.rc_recv, r.rx_send, r.rx_recv),
                 (r.sgrad, r.sc_send, r.sc_recv, r.sx_send, r.sx_recv))

        def core_copy(which):
            return remote(
                parts[which][1],
                parts[which][2],
                r.core_send.at[which],
                r.core_recv.at[which],
                at_row(row + 1 - 2 * core),
            )

        def start_core(which):
            grads, out = parts[which][:2]
            for pair in range(pairs):
                out[pair] = grads[block(2 * pair + 1 - core), :].astype(BF16)
            core_copy(which).start()

        def chip_copy(which, step):
            return remote(
                parts[which][3].at[step],
                parts[which][4].at[step],
                r.chip_send.at[which, step],
                r.chip_recv.at[which, step],
                at_row(2 * lax.rem(chip + step, pairs) + core),
            )

        def chan_copy(step):
            return remote(
                r.zs_send.at[step],
                r.zs_recv.at[step],
                r.chan_send.at[step],
                r.chan_recv.at[step],
                at_chan(beside(step)),
            )

        def row_norm(step):
            return remote(
                r.part_rows.at[row],
                r.part_rows.at[row],
                r.rn_send.at[step],
                r.rn_recv.at[step],
                at_row(lax.rem(row + step, group)),
            )

        def chan_norm(step):
            return remote(
                r.part_chans.at[me],
                r.part_chans.at[me],
                r.cn_send.at[step],
                r.cn_recv.at[step],
                at_chan(beside(step)),
            )

    def step_chip(which):
        grads, _, came, out, _ = parts[which]
        cols = slice(2 * chans, 2 * chans + regs) if which == 0 else slice(0, 2 * chans)
        core_copy(which).wait_recv()
        for step in range(1, pairs):
            to = lax.rem(chip + step, pairs)
            out[step] = (grads[block(2 * to + core), :] + came[to].astype(F32)).astype(BF16)
            chip_copy(which, step).start()
        r.whole_grad[:, cols] = grads[block(row), :] + came[chip].astype(F32)

    def image(slot, carry):
        last = slot == slots - 1
        wait_in(slot, 0)
        start_later(slot, 0)
        for copy in own_copies(slot):
            copy.wait()

        def image_rows(first):
            return held[slot, first // cl, pl.ds(pl.multiple_of(first % cl, 16), 16), :]

        def picked(here):
            return held[slot, :, cl : 2 * cl, here].reshape(chans, CHUNK).astype(F32) > 0.5

        def head(here):
            pre = dot(r.w_in[0 : 2 * chans, :], r.x_cols[:, here])
            r.out_low[:, here] = jnp.where(picked(here), pre[chans:], pre[:chans]).astype(BF16)

        def teach(here):
            r.teach[:, here] = dot(r.w_in[2 * chans :, :], r.x_cols[:, here])

        def guess(here):
            r.guess[:, here] = dot(r.w_reg[...], r.o_cols[:, here])

        def pooling(here):
            cell_win = r.held_pool[slot, :, 0:cl, :].reshape(chans, cells)
            cell_cot = r.held_pool[slot, :, cl : 2 * cl, :].reshape(chans, cells)
            chosen = dot(cell_win, r.up[:, here]) == corner_of(here)
            spread = dot(cell_cot, r.up[:, here])
            r.pool_back[:, here] = jnp.where(chosen, spread, 0.0).astype(BF16)
            kept = jnp.where(chosen, r.out_low[:, here].astype(F32), 0.0).astype(BF16)
            part = dot_nt(kept, r.up[:, here])
            r.pool_part[slot] = (r.pool_part[slot].astype(F32) + part).astype(BF16)

        def hints(here):
            pick = held[slot, :, 2 * cl :, here].reshape(touts, CHUNK).astype(F32)
            target = jnp.where(pick > 0.5, r.teach[touts:, here], r.teach[:touts, here])
            weight = scale * r.mask[pl.ds(me * slots + slot, 1), here].astype(F32)
            r.hint[:, here] = (weight * (r.guess[:, here] - target)).astype(BF16)

        def back(here):
            total = dot(r.w_reg_back[...], r.h_cols[:, here]) + r.pool_back[:, here].astype(F32)
            pick = picked(here)
            r.pre_grad[0:chans, here] = jnp.where(pick, 0.0, total).astype(BF16)
            r.pre_grad[chans:, here] = jnp.where(pick, total, 0.0).astype(BF16)

        def image_back(here):
            r.low_part[slot, :, here] = dot(r.w_in_back[...], r.p_cols[:, here]).astype(BF16)

        def columns_of(src, dst):
            rows = src.shape[0]
            return lambda stage: columns(lambda first: src[pl.ds(first, 16), :], rows, dst, stage)

        spot_mask = r.mask[pl.ds(me * slots + slot, 1), :].astype(F32)
        count = jnp.sum(spot_mask, axis=1, keepdims=True)
        scale = HINT_WEIGHT * (pixels / count)
        r.pool_part[slot] = jnp.zeros((chans, cells), BF16)

        stages(lambda stage: columns(image_rows, chans, r.x_cols, stage))
        stages(chunks(head))
        stages(chunks(teach), columns_of(r.out_low, r.o_cols))
        stages(chunks(guess))
        wait_in(slot, 1)
        start_later(slot, 1)
        pl.when(last)(lambda: start_outs("early"))
        stages(chunks(hints))
        stages(add_grads(r.rgrad, r.o_cols, r.hint), columns_of(r.hint, r.h_cols))
        if fused:
            pl.when(last)(lambda: start_core(0))
        stages(chunks(pooling))
        stages(chunks(back))
        if fused:
            pl.when(last)(lambda: step_chip(0))
        stages(add_grads(r.sgrad, r.x_cols, r.pre_grad), columns_of(r.pre_grad, r.p_cols))
        if fused:
            pl.when(last)(lambda: start_core(1))
        stages(chunks(image_back))
        if not fused:

            def start_rest():
                start_outs("mid")
                start_outs("late")

            pl.when(last)(start_rest)
        for copy in own_out(slot):
            copy.start()
        return carry

    if fused:
        r.whole_grad[...] = jnp.zeros_like(r.whole_grad)
    lax.fori_loop(0, slots, image, 0)

    if fused:
        step_chip(1)
        for which, cols in ((0, slice(2 * chans, 2 * chans + regs)), (1, slice(0, 2 * chans))):
            came = parts[which][4]
            for step in range(1, pairs):
                chip_copy(which, step).wait_recv()
            total = r.whole_grad[:, cols]
            for step in range(1, pairs):
                total += came[step].astype(F32)
            r.whole_grad[:, cols] = total
        low_grad = r.whole_grad[...].astype(BF16)
        for step in partners:
            r.zs_send[step] = dot_nt(low_grad, r.spread[beside(step)]).astype(BF16)
            chan_copy(step).start()
        start_outs("mid")
        total = dot_nt(
            r.whole_grad[...], r.spread[me].astype(F32), precision=lax.Precision.HIGHEST
        )
        for slot in out_order["early"]:
            land(slot)
        for step in partners:
            chan_copy(step).wait_recv()
        for step in partners:
            total += r.zs_recv[step].astype(F32)
        r.tall[0:depth, :] = total
        total = r.tall[...].T[:, 0:depth]
        r.grad_sum[...] = total
        student, regress = r.student_t[...], r.regress_t[...]
        upd_s = lamb_update(student, total[0 : 2 * cl], r.mom_student[...], r.sq_student[...])[2]
        upd_r = lamb_update(
            regress, total[2 * cl : 2 * cl + rl], r.mom_regress[...], r.sq_regress[...]
        )[2]
        place = lax.broadcasted_iota(jnp.int32, (8, LANES), 1)
        tile = jnp.zeros((8, LANES), F32)
        for index, value in enumerate((student, upd_s, regress, upd_r)):
            square = jnp.sum(jnp.sum(value * value, axis=1, keepdims=True), axis=0, keepdims=True)
            tile = jnp.where(place == index, square, tile)
        r.part_chans[me] = tile
        for step in partners:
            chan_norm(step).start()
        start_outs("late")
        for slot in out_order["mid"]:
            land(slot)
        for step in partners:
            chan_norm(step).wait_recv()
        tile = r.part_chans[0]
        for index in range(1, n):
            tile += r.part_chans[index]
        r.part_rows[row] = tile
        for step in range(1, group):
            row_norm(step).start()
        for step in range(1, group):
            row_norm(step).wait_recv()
        tile = r.part_rows[0]
        for index in range(1, group):
            tile += r.part_rows[index]
        r.sums[...] = tile

    for slot in out_order["late"] if fused else range(slots):
        land(slot)
    for src, out in ((r.wide, r.grad_out), (r.cot_wide, r.pool_out)):
        for j in range(src.shape[0]):
            out[:, j * LANES : (j + 1) * LANES] = src[j].astype(BF16)

    def finish(slot, carry):
        for step in partners:
            for copy in (*in_copies(slot, step, 0), *in_copies(slot, step, 1), *out_copies(slot, step)):
                copy.wait_send()
        return carry

    lax.fori_loop(0, slots, finish, 0)
    if fused:
        for step in partners:
            filter_z[step - 1].wait_send()
            chan_copy(step).wait_send()
            chan_norm(step).wait_send()
        for step in range(1, group):
            row_norm(step).wait_send()
        for step in range(pairs):
            filter_core(step).wait_send()
        for step in range(1, pairs):
            filter_chip(step).wait_send()
        for which in range(2):
            core_copy(which).wait_send()
            for step in range(1, pairs):
                chip_copy(which, step).wait_send()


def lamb_update(weights, grads, moment, second):
    moment_new = BETA_ONE * moment + (1.0 - BETA_ONE) * grads
    second_new = BETA_TWO * second + (1.0 - BETA_TWO) * grads * grads
    moment_hat = moment_new / (1.0 - BETA_ONE**STEP)
    second_hat = second_new / (1.0 - BETA_TWO**STEP)
    update = moment_hat / (jnp.sqrt(second_hat) + EPSILON) + DECAY * weights
    return (moment_new, second_new, update)


def layer_pass(n, group, fused, arrays, handed=()):
    cl, batch, pixels = arrays["images"].shape
    tl = arrays["twin"].shape[0]
    cells = arrays["pwin"].shape[2]
    slots = batch // n
    chans = n * cl
    if fused:
        rl, depth = arrays["regress_t"].shape
    else:
        rl = arrays["w_reg"].shape[0] // n
    regs, touts, pairs = n * rl, n * tl, group // 2
    size = dict(n=n, batch=batch, cl=cl, tl=tl, rl=rl, fused=fused, group=group)
    vmem = pl.BlockSpec(memory_space=pltpu.VMEM)
    in_hbm = ("images", "swin", "twin", "pwin", "cot")
    ins = {
        name: a.reshape(a.shape[0] * a.shape[1], a.shape[2]) if name in in_hbm else a
        for name, a in arrays.items()
    }
    outs = {
        "pool_out": pltpu.VMEM((cl * batch, cells), BF16),
        "grad_out": pltpu.VMEM((cl * batch, pixels), BF16),
    }
    small = tuple(name for name in ins if name not in in_hbm)
    size["small"] = small
    grads = {"sgrad": (9 * chans, 2 * chans), "rgrad": (9 * chans, regs)}
    dma = lambda *shape: pltpu.SemaphoreType.DMA(shape)
    scratch = {
        "raw": pltpu.VMEM((cl * batch, pixels), BF16),
        "raw_cot": pltpu.VMEM((cl * batch, cells), BF16),
        "wide": pltpu.VMEM((pixels // LANES, cl * batch, LANES), F32),
        "swin_wide": pltpu.VMEM((pixels // LANES, cl * batch, LANES), jnp.int32),
        "twin_wide": pltpu.VMEM((pixels // LANES, tl * batch, LANES), jnp.int32),
        "pwin_wide": pltpu.VMEM((cells // LANES, cl * batch, LANES), jnp.int32),
        "cot_wide": pltpu.VMEM((cells // LANES, cl * batch, LANES), F32),
        "load_sem": dma(2 + 2 * (pixels // LANES) + cells // LANES),
        "send": pltpu.VMEM((slots, n, 2 * cl + tl, pixels), BF16),
        "send_pool": pltpu.VMEM((slots, n, 2 * cl, cells), BF16),
        "held": pltpu.VMEM((slots, n, 2 * cl + tl, pixels), BF16),
        "held_pool": pltpu.VMEM((slots, n, 2 * cl, cells), BF16),
        "low_part": pltpu.VMEM((slots, chans, pixels), BF16),
        "pool_part": pltpu.VMEM((slots, chans, cells), BF16),
        "pool_land": pltpu.VMEM((batch, cl, cells), BF16),
        "grad_land": pltpu.VMEM((batch, cl, pixels), BF16),
        "edge": pltpu.VMEM((4, 16, pixels), BF16),
        "up": pltpu.VMEM((cells, pixels), BF16),
        "x_cols": pltpu.VMEM((9 * chans, pixels), BF16),
        "o_cols": pltpu.VMEM((9 * chans, pixels), BF16),
        "h_cols": pltpu.VMEM((9 * regs, pixels), BF16),
        "p_cols": pltpu.VMEM((9 * 2 * chans, pixels), BF16),
        "out_low": pltpu.VMEM((chans, pixels), BF16),
        "pool_back": pltpu.VMEM((chans, pixels), BF16),
        "hint": pltpu.VMEM((regs, pixels), BF16),
        "teach": pltpu.VMEM((2 * touts, pixels), F32),
        "guess": pltpu.VMEM((regs, pixels), F32),
        "pre_grad": pltpu.VMEM((2 * chans, pixels), BF16),
        "own_sem": dma(slots, 2),
        "own_out_sem": dma(slots, 2),
    }
    scratch["in_send"] = dma(slots, 2, n)
    scratch["in_recv"] = dma(slots, 2, n)
    for name in ("pool_in", "out", "pool_out"):
        scratch[name + "_send"] = dma(slots, n)
        scratch[name + "_recv"] = dma(slots, n)
    if fused:
        cols = 2 * chans + 2 * LANES
        tall = -(-depth // LANES) * LANES
        outs["grad_sum"] = pltpu.VMEM((LANES, depth), F32)
        outs["sums"] = pltpu.VMEM((8, LANES), F32)
        outs.update({name: pltpu.VMEM(ins[name].shape, F32) for name in handed})
        scratch.update({name: pltpu.VMEM(shape, F32) for name, shape in grads.items()})
        scratch.update(
            {
                "flat": pltpu.VMEM((LANES, tall), F32),
                "tall": pltpu.VMEM((tall, LANES), F32),
                "teach_flat": pltpu.VMEM((LANES, 9 * chans), F32),
                "teach_cols": pltpu.VMEM((9 * chans, LANES), F32),
                "filters": pltpu.VMEM((n, 9 * chans, 2 * LANES), BF16),
                "gather_rows": pltpu.VMEM((2 * cl + rl + 2 * tl, 2 * LANES), BF16),
                "spread": pltpu.VMEM((n, LANES, cols), BF16),
                "w_in": pltpu.VMEM((2 * chans + 2 * touts, 9 * chans), BF16),
                "w_reg": pltpu.VMEM((regs, 9 * chans), BF16),
                "w_reg_back": pltpu.VMEM((chans, 9 * regs), BF16),
                "w_in_back": pltpu.VMEM((chans, 9 * 2 * chans), BF16),
                "rc_send": pltpu.VMEM((pairs, depth, regs), BF16),
                "rc_recv": pltpu.VMEM((pairs, depth, regs), BF16),
                "rx_send": pltpu.VMEM((pairs, depth, regs), BF16),
                "rx_recv": pltpu.VMEM((pairs, depth, regs), BF16),
                "sc_send": pltpu.VMEM((pairs, depth, 2 * chans), BF16),
                "sc_recv": pltpu.VMEM((pairs, depth, 2 * chans), BF16),
                "sx_send": pltpu.VMEM((pairs, depth, 2 * chans), BF16),
                "sx_recv": pltpu.VMEM((pairs, depth, 2 * chans), BF16),
                "whole_grad": pltpu.VMEM((depth, cols), F32),
                "zs_send": pltpu.VMEM((n, depth, LANES), BF16),
                "zs_recv": pltpu.VMEM((n, depth, LANES), BF16),
                "part_rows": pltpu.VMEM((group, 8, LANES), F32),
                "part_chans": pltpu.VMEM((n, 8, LANES), F32),
                "core_send": dma(2),
                "core_recv": dma(2),
                "chip_send": dma(2, pairs),
                "chip_recv": dma(2, pairs),
            }
        )
        for name, many in (
            ("fz", n), ("fx", pairs), ("fc", pairs), ("chan", n), ("rn", group), ("cn", n)
        ):
            scratch[name + "_send"] = dma(many)
            scratch[name + "_recv"] = dma(many)
    else:
        outs.update({name: jax.ShapeDtypeStruct(shape, F32) for name, shape in grads.items()})
    flops = 2 * slots * pixels * 9 * chans * (3 * 2 * chans + 2 * touts + 3 * regs)
    scratch.update(
        {name: pltpu.VMEM(ins[name].shape, ins[name].dtype) for name in small if name not in outs}
    )
    scratch["small_sem"] = dma(len(small))
    in_names = tuple(name + "_hbm" if name in small else name for name in ins)
    names = in_names + tuple(outs) + tuple(scratch)
    return pl.pallas_call(
        functools.partial(layer_kernel, size, names),
        out_shape=list(outs.values()),
        in_specs=[pl.BlockSpec(memory_space=pl.ANY)] * len(ins),
        out_specs=[vmem] * len(outs),
        scratch_shapes=list(scratch.values()),
        compiler_params=pltpu.CompilerParams(
            collective_id=0, has_side_effects=True, vmem_limit_bytes=58 << 20
        ),
        cost_estimate=pl.CostEstimate(flops=flops, bytes_accessed=16 << 20, transcendentals=0),
        name="layer",
    )(*ins.values())


def final_kernel(*refs):
    pool_in, grad_in = refs[0:2]
    pooled, image_grad, new_s, new_r, trust = refs[12], refs[13], refs[14:19], refs[19:24], refs[24]
    big_sem = refs[25]
    big = [
        pltpu.make_async_copy(src, dst, big_sem.at[index])
        for index, (src, dst) in enumerate(((grad_in, image_grad), (pool_in, pooled)))
    ]
    for copy in big:
        copy.start()
    grad_sum, sums, student, regress, mom_s, sq_s, mom_r, sq_r, ema_s, ema_r = refs[2:12]
    norm = [jnp.sqrt(sums[0:1, k : k + 1]) for k in range(4)]
    souts, regs = student.shape[0], regress.shape[0]
    for weights, grads, moment, second, average, outs, top, bottom in (
        (student, grad_sum[0:souts, :], mom_s, sq_s, ema_s, new_s, norm[0], norm[1]),
        (regress, grad_sum[souts : souts + regs, :], mom_r, sq_r, ema_r, new_r, norm[2], norm[3]),
    ):
        moment_new, second_new, update = lamb_update(
            weights[...], grads, moment[...], second[...]
        )
        new = weights[...] - LEARN_RATE * (top / bottom) * update
        outs[0][...] = new
        outs[1][...] = moment_new
        outs[2][...] = second_new
        outs[3][...] = EMA_KEEP * average[...] + (1.0 - EMA_KEEP) * new
        outs[4][...] = new.astype(BF16)
    across = lax.broadcasted_iota(jnp.int32, (2, 2), 1)
    down = lax.broadcasted_iota(jnp.int32, (2, 2), 0)
    first = jnp.where(across == 0, norm[0], norm[1])
    trust[...] = jnp.where(down == 0, first, jnp.where(across == 0, norm[2], norm[3]))
    for copy in big:
        copy.wait()


def final_pass(pooled, image_grad, grad_sum, sums, *small):
    student, regress = small[0:2]
    outs = [jax.ShapeDtypeStruct(a.shape, BF16) for a in (pooled, image_grad)]
    for a in (student, regress):
        outs += [jax.ShapeDtypeStruct(a.shape, F32)] * 4 + [jax.ShapeDtypeStruct(a.shape, BF16)]
    outs.append(jax.ShapeDtypeStruct((2, 2), F32))
    vmem, hbm = (pl.BlockSpec(memory_space=space) for space in (pltpu.VMEM, pl.ANY))
    kept = (grad_sum, sums, *small)
    results = pl.pallas_call(
        final_kernel,
        out_shape=outs,
        in_specs=[vmem] * (2 + len(kept)),
        out_specs=[hbm] * 2 + [vmem] * (len(outs) - 2),
        scratch_shapes=[pltpu.SemaphoreType.DMA((2,))],
        compiler_params=pltpu.CompilerParams(vmem_limit_bytes=16 << 20),
        name="final",
    )(*(pltpu.with_memory_space_constraint(a, pltpu.VMEM) for a in (pooled, image_grad, *kept)))
    return (*results[0:2], *(a.T for a in results[2:12]), results[12])


def split_pieces(weights):
    rows, cols = weights.shape
    return weights.reshape(rows, cols // 2, 2).transpose(2, 1, 0).reshape(cols, rows)


def back_weights(weights, outs):
    channels = weights.shape[0] // 9
    taps = weights.reshape(9, channels, outs)[::-1]
    return taps.transpose(1, 0, 2).reshape(channels, 9 * outs)


def gathered_filters(student_master, regress_master, teacher_weight):
    student_full = lax.all_gather(student_master.astype(BF16), "dp", axis=0, tiled=True)
    student_full = lax.all_gather(student_full, "chan", axis=1, tiled=True)
    regress_full = lax.all_gather(regress_master.astype(BF16), "dp", axis=0, tiled=True)
    regress_full = lax.all_gather(regress_full, "chan", axis=1, tiled=True)
    teacher_full = lax.all_gather(teacher_weight, "chan", axis=1, tiled=True)
    student_rows = split_pieces(student_full)
    return {
        "w_in": jnp.concatenate([student_rows, split_pieces(teacher_full)], axis=0),
        "w_reg": regress_full.T,
        "w_reg_back": back_weights(regress_full, regress_full.shape[1]),
        "w_in_back": back_weights(student_rows.T, student_full.shape[1]),
    }


def scattered_grads(student_part, regress_part):
    souts = student_part.shape[1]
    student_part = student_part.reshape(-1, 2, souts // 2).transpose(0, 2, 1).reshape(-1, souts)
    student_grad = lax.psum_scatter(student_part, "dp", scatter_dimension=0, tiled=True)
    student_grad = lax.psum_scatter(student_grad, "chan", scatter_dimension=1, tiled=True)
    regress_grad = lax.psum_scatter(regress_part, "dp", scatter_dimension=0, tiled=True)
    regress_grad = lax.psum_scatter(regress_grad, "chan", scatter_dimension=1, tiled=True)
    return student_grad, regress_grad


def on_device(
    n,
    group,
    images,
    student_master,
    regress_master,
    teacher_weight,
    student_win,
    teacher_win,
    pool_win,
    hint_mask,
    cotangent,
    mom_student,
    sq_student,
    ema_student,
    mom_regress,
    sq_regress,
    ema_regress,
):
    image_like = lambda a: a.reshape(images.shape)
    pool_like = lambda a: a.reshape(pool_win.shape)
    depth = student_master.shape[0]
    fused = group % 2 == 0 and depth % 16 == 0
    arrays = dict(
        images=images,
        swin=student_win,
        twin=teacher_win,
        pwin=pool_win,
        cot=cotangent,
        mask=hint_mask,
    )
    if fused:
        small = dict(
            student_t=student_master,
            regress_t=regress_master,
            mom_student=mom_student,
            sq_student=sq_student,
            mom_regress=mom_regress,
            sq_regress=sq_regress,
            ema_student=ema_student,
            ema_regress=ema_regress,
        )
        arrays.update({name: a.T for name, a in small.items()}, teacher_t=teacher_weight.T)
        results = final_pass(*layer_pass(n, group, fused, arrays, tuple(small)))
        return (pool_like(results[0]), image_like(results[1]), *results[2:])
    arrays.update(gathered_filters(student_master, regress_master, teacher_weight))
    pooled, image_grad, student_part, regress_part = layer_pass(n, group, fused, arrays)
    student_grad, regress_grad = scattered_grads(student_part, regress_part)
    mom_s, sq_s, upd_s = lamb_update(student_master, student_grad, mom_student, sq_student)
    mom_r, sq_r, upd_r = lamb_update(regress_master, regress_grad, mom_regress, sq_regress)
    all_sums = lax.psum(
        jnp.stack([jnp.sum(v * v) for v in (student_master, upd_s, regress_master, upd_r)]),
        ("dp", "chan"),
    )
    norms = jnp.sqrt(all_sums)
    new_student = student_master - LEARN_RATE * (norms[0] / norms[1]) * upd_s
    new_regress = regress_master - LEARN_RATE * (norms[2] / norms[3]) * upd_r
    ema_s = EMA_KEEP * ema_student + (1.0 - EMA_KEEP) * new_student
    ema_r = EMA_KEEP * ema_regress + (1.0 - EMA_KEEP) * new_regress
    return (
        pool_like(pooled),
        image_like(image_grad),
        new_student,
        mom_s,
        sq_s,
        ema_s,
        new_student.astype(BF16),
        new_regress,
        mom_r,
        sq_r,
        ema_r,
        new_regress.astype(BF16),
        norms.reshape(2, 2),
    )


def solution(mesh):
    acts = P("chan", "dp", None)
    rows = P("dp", "chan")
    in_specs = (
        (acts, rows, rows, P(None, "chan"))
        + (acts, acts, acts, P("dp", None), acts)
        + (rows,) * 6
    )
    out_specs = (acts, acts) + (rows,) * 10 + (P(),)
    return jax.shard_map(
        functools.partial(on_device, mesh.shape["chan"], mesh.shape["dp"]),
        mesh=mesh,
        in_specs=in_specs,
        out_specs=out_specs,
        check_vma=False,
    )
```
